128 devices in a mesh: row: 8 (over y, core), col: 16 (over z, x).
Axes of the slice: x: 4, y: 4, z: 4, core: 2. Of those that a mesh axis runs over, the one named last changes fastest.
Arguments:
- noise_latents: bfloat16 [8192, 2048], P('row', 'col'), may hold values from -40 to 40
- data_latents: bfloat16 [32768, 2048], P('col', 'row'), may hold values from -6 to 6
- noise_sizes: int32 [8], replicated, may hold values from 1 to 2048, 8192 in all
- data_sizes: int32 [8], replicated, may hold values from 1 to 8192, 32768 in all
Outputs:
- velocity: float32 [8192, 2048], P('row', 'col')
- noise_potential: float32 [8192], P('row')
- data_potential: float32 [32768], P('col')
The draws below stay inside these ranges and needn't reach their ends.
Inputs may be any that keep to these rules, and one draw needn't show every extreme that they name: `noise_sizes`: clusters take consecutive runs of noise samples in order of the cluster number; every cluster is non-empty and the largest holds exactly 2048. `data_sizes`: clusters take consecutive runs of data samples in order of the cluster number; every cluster is non-empty and the largest holds exactly 8192.
All inputs are finite; a program needn't handle non-finite values.
Results may differ from the reference program's by a relative error of at most 0.007.
Values may be sent and summed in bfloat16 or wider, within the bound.
No kernel may reach another device: no remote copies, remote signals or barrier semaphores. Data moves between devices by JAX's collectives and lax.ppermute only.
A program may use at most 128 MiB of HBM per device.

```python
import math
import jax
import jax.numpy as jnp
import numpy as np
from jax import lax

W = 2048
COLS_DEV = 2048
CLUSTERS = 8
ITERS = 3
NN = 8192
ND = 32768
N_COL = 16


def draw_noise_latents(key, part):
    key = jax.random.fold_in(key, 11)
    gauss_key = jax.random.fold_in(key, 0)
    gaussian = jax.random.normal(gauss_key, (NN, W), jnp.float32)
    return jnp.clip(gaussian, -6.0, 6.0).astype(jnp.bfloat16)


def block_scale(own_key, extent, cuts, low, high):
    def one(dim, parts):
        steps = jax.random.uniform(jax.random.fold_in(jax.random.fold_in(own_key, 6), dim), (parts,), jnp.float32, low / len(cuts), high / len(cuts))
        return jnp.repeat(jnp.exp(steps), extent[dim] // parts).reshape((-1,) + (1,) * (len(extent) - dim - 1))

    level = one(*cuts[0])
    for cut in cuts[1:]:
        level = level * one(*cut)
    return level


def length_profile(count, total, limit, slope):
    portions = [(1 << 20) // math.isqrt(grade ** slope) + 1 for grade in range(2, count + 1)]
    surplus, given = total - limit - (count - 1), [1] * (count - 1)
    while surplus > 0:
        free = [i for i in range(count - 1) if given[i] < limit]
        pool, left = sum([portions[i] for i in free]), surplus
        for i in free:
            addition = min(limit - given[i], max(1, left * portions[i] // pool), surplus)
            given[i] = given[i] + addition
            surplus = surplus - addition
    return np.array([limit] + given)


def ragged(stream_key, count, total, limit, skew):
    if count == 2:
        one = jax.random.randint(stream_key, (), max(1, total - limit), min(limit, total - 1) + 1)
        return jnp.stack([one, total - one])
    sizes = jnp.asarray(length_profile(count, total, limit, skew), jnp.int32)
    twos = (count - 1) // 2
    giver, sink = sizes[1:1 + 2 * twos:2], sizes[2:2 + 2 * twos:2]
    margin = jnp.minimum(giver - 1, limit - sink)
    passed = jax.random.randint(jax.random.fold_in(stream_key, 1), (twos,), 0, 1 << 20) % (margin + 1)
    sizes = sizes.at[1:1 + 2 * twos:2].set(giver - passed).at[2:2 + 2 * twos:2].set(sink + passed)
    return sizes[jax.random.permutation(jax.random.fold_in(stream_key, 2), count)]


def bell_draw(own_key, shape, spread, bound, cuts=(), kind=jnp.bfloat16):
    drawn = jax.random.normal(own_key, shape, jnp.float32) * spread
    if len(cuts) > 0:
        drawn = block_scale(own_key, shape, cuts, -0.22, 0.18) * drawn
    return jnp.clip(drawn, min=-bound, max=bound).astype(kind)


def setup_inputs(seed: int = 0) -> dict:
    seeds = jax.random.split(jax.random.key(seed), 5)
    noise_latents = draw_noise_latents(jax.random.fold_in(seeds[4], 71), 0)
    data_latents = bell_draw(seeds[1], (ND, W), 1.0, 6.0, ((0, 16), (1, 8)))
    noise_sizes = ragged(seeds[2], CLUSTERS, NN, NN // 4, 2).astype(jnp.int32)
    data_sizes = ragged(seeds[3], CLUSTERS, ND, ND // 4, 2).astype(jnp.int32)
    return {"noise_latents": noise_latents, "data_latents": data_latents, "noise_sizes": noise_sizes, "data_sizes": data_sizes}


epsilon = 0.05
masked_value = -1e30


def cluster_of(positions, cluster_sizes):
    boundaries = jnp.cumsum(cluster_sizes).astype(jnp.int32)[:-1]
    return jnp.sum((positions[:, None] >= boundaries[None, :]).astype(jnp.int32), axis=1)


def masked_lse(scores, same_cluster, reduce_axis):
    masked = jnp.where(same_cluster, scores, masked_value)
    largest = jnp.max(masked, axis=reduce_axis, keepdims=True)
    totals = jnp.sum(jnp.where(same_cluster, jnp.exp(masked - largest), 0.0), axis=reduce_axis, keepdims=True)
    return jnp.squeeze(largest + jnp.log(totals), reduce_axis)


def reference(noise_latents, data_latents, noise_sizes, data_sizes):
    full_width = noise_latents.shape[1]
    row_block = math.gcd(NN, 512)
    noise_sq = jnp.sum(jnp.square(noise_latents.astype(jnp.float32)), axis=1)
    data_sq = jnp.sum(jnp.square(data_latents.astype(jnp.float32)), axis=1)
    blocks = noise_latents.reshape(NN // row_block, row_block, full_width)
    data_turned = data_latents.T

    def inner_block(block_rows):
        return jnp.dot(block_rows, data_turned, preferred_element_type=jnp.float32)

    inner = lax.map(inner_block, blocks).reshape(NN, ND)
    cost = (noise_sq[:, None] + data_sq[None, :] - 2.0 * inner) / full_width
    noise_cluster = cluster_of(jnp.arange(NN, dtype=jnp.int32), noise_sizes)
    data_cluster = cluster_of(jnp.arange(ND, dtype=jnp.int32), data_sizes)
    same_cluster = noise_cluster[:, None] == data_cluster[None, :]
    data_potential = jnp.zeros((ND,), jnp.float32)
    noise_potential = jnp.zeros((NN,), jnp.float32)
    for iteration in range(ITERS):
        noise_potential = -epsilon * masked_lse((data_potential[None, :] - cost) / epsilon, same_cluster, 1)
        data_potential = -epsilon * masked_lse((noise_potential[:, None] - cost) / epsilon, same_cluster, 0)
    scores = (data_potential[None, :] - cost) / epsilon
    row_lse = masked_lse(scores, same_cluster, 1)
    weights = jnp.where(same_cluster, jnp.exp(jnp.where(same_cluster, scores, masked_value) - row_lse[:, None]), 0.0)
    weights = weights.astype(jnp.bfloat16).reshape(NN // row_block, row_block, N_COL, COLS_DEV)
    data_blocks = data_latents.astype(jnp.float32).reshape(N_COL, COLS_DEV, full_width)

    def target_block(weight_rows):
        partials = jnp.einsum("rbk,bkw->rbw", weight_rows.astype(jnp.float32), data_blocks, precision=lax.Precision.HIGHEST)
        rounded = lax.optimization_barrier(partials.astype(jnp.bfloat16)).astype(jnp.float32)
        return jnp.sum(rounded, axis=1)

    target = lax.map(target_block, weights).reshape(NN, full_width)
    velocity = target - noise_latents.astype(jnp.float32)
    return (velocity, noise_potential, data_potential)
```

```python
import functools

import jax
import jax.numpy as jnp
from jax import lax
from jax.experimental import pallas as pl
from jax.experimental.pallas import tpu as pltpu
from jax.sharding import PartitionSpec as P

EPS = 0.05
LOG2E = 1.4426950408889634
LN2 = 0.6931471805599453
MASKED = -1e30
CLUSTERS = 8
F32 = jnp.float32
BF16 = jnp.bfloat16
MIB = 1 << 20

ROWS = 1024
COLS = 2048
WIDTH = 2048
COL_BLOCK = 256
ROW_BLOCK = 256
N_ROW = 8
N_COL = 16
KAPPA = LOG2E / (WIDTH * EPS)


def vmem(shape, index_map=None):
    if index_map is None:
        return pl.BlockSpec(shape, lambda *_: (0,) * len(shape))
    return pl.BlockSpec(shape, index_map)


def params(mib):
    return pltpu.CompilerParams(vmem_limit_bytes=mib * MIB, dimension_semantics=("arbitrary",))


def lane_totals(pieces):
    return [piece.T for piece in pieces]


def to_column(rows):
    n = rows.shape[0]
    return [jnp.broadcast_to(rows[a : a + 1, :], (128, 128)).T for a in range(n)]


def to_lanes(rows):
    return jnp.concatenate([rows[a : a + 1, :] for a in range(rows.shape[0])], axis=1)


def from_lanes(row):
    return jnp.concatenate([row[:, 128 * a : 128 * (a + 1)] for a in range(row.shape[1] // 128)], axis=0)


def score_kernel(info_ref, noise_ref, data_ref, score_ref, lse_ref, noise_sq_ref, data_sq_ref, big, total):
    step = pl.program_id(0)

    @pl.when(step == 0)
    def _():
        big[...] = jnp.full(big.shape, MASKED, F32)
        total[...] = jnp.zeros(total.shape, F32)
        for a in range(ROWS // 128):
            squares = jnp.zeros((128, 128), F32)
            for k in range(N_COL):
                piece = noise_ref[k, 128 * a : 128 * (a + 1), :].astype(F32)
                squares += piece * piece
            noise_sq_ref[a : a + 1, :] = jnp.sum(squares.T, axis=0, keepdims=True)

    data = jnp.concatenate([data_ref[k] for k in range(N_ROW)], axis=1)
    data_sq = []
    for a in range(COL_BLOCK // 128):
        squares = jnp.zeros((128, 128), F32)
        for k in range(WIDTH // 128):
            piece = data[128 * a : 128 * (a + 1), 128 * k : 128 * (k + 1)].astype(F32)
            squares += piece * piece
        data_sq.append(jnp.sum(squares.T, axis=0, keepdims=True))
        data_sq_ref[0, a : a + 1, :] = data_sq[a]

    j = info_ref[17] + step * COL_BLOCK + lax.broadcasted_iota(jnp.int32, (1, COL_BLOCK), 1)
    low = jnp.zeros((1, COL_BLOCK), jnp.int32)
    high = jnp.zeros((1, COL_BLOCK), jnp.int32)
    noise_at = jnp.int32(0)
    data_at = jnp.int32(0)
    for c in range(CLUSTERS):
        noise_end = noise_at + info_ref[c]
        data_end = data_at + info_ref[8 + c]
        if c == CLUSTERS - 1:
            inside = j >= data_at
        else:
            inside = (j >= data_at) & (j < data_end)
        low = jnp.where(inside, noise_at, low)
        high = jnp.where(inside, noise_end, high)
        noise_at, data_at = noise_end, data_end
    low = low - info_ref[16]
    high = high - info_ref[16]

    half = 256
    for r in range(ROWS // half):
        noise = jnp.concatenate([noise_ref[k, half * r : half * (r + 1), :] for k in range(N_COL)], axis=1)
        inner = lax.dot_general(noise, data, (((1,), (1,)), ((), ())), preferred_element_type=F32)
        i = half * r + lax.broadcasted_iota(jnp.int32, (half, COL_BLOCK), 0)
        score = jnp.where((i >= low) & (i < high), inner * (2.0 * KAPPA), MASKED)
        score_ref[half * r : half * (r + 1), :] = score
        lo = score[:, :128] - KAPPA * data_sq[0]
        hi = score[:, 128:] - KAPPA * data_sq[1]
        at = slice(half * r, half * (r + 1))
        old = big[at, :]
        new = jnp.maximum(old, jnp.maximum(lo, hi))
        total[at, :] = total[at, :] * jnp.exp2(old - new) + (jnp.exp2(lo - new) + jnp.exp2(hi - new))
        big[at, :] = new

    @pl.when(step == pl.num_programs(0) - 1)
    def _():
        rows = []
        for a in range(ROWS // 128):
            at = slice(128 * a, 128 * (a + 1))
            m = big[at, :].T
            s = total[at, :].T
            largest = jnp.max(m, axis=0, keepdims=True)
            summed = jnp.sum(s * jnp.exp2(m - largest), axis=0, keepdims=True)
            rows.append(largest + jnp.log2(summed))
        lse_ref[...] = jnp.broadcast_to(jnp.concatenate(rows, axis=0)[None], lse_ref.shape)


def scores(info, noise, data):
    return pl.pallas_call(
        score_kernel,
        grid=(COLS // COL_BLOCK,),
        in_specs=[
            pl.BlockSpec(memory_space=pltpu.SMEM),
            vmem((N_COL, ROWS, 128)),
            vmem((N_ROW, COL_BLOCK, 256), lambda j: (0, j, 0)),
        ],
        out_specs=[
            vmem((ROWS, COL_BLOCK), lambda j: (0, j)),
            vmem((N_COL, 8, 128)),
            vmem((8, 128)),
            vmem((1, 2, 128), lambda j: (j, 0, 0)),
        ],
        out_shape=[
            jax.ShapeDtypeStruct((ROWS, COLS), F32),
            jax.ShapeDtypeStruct((N_COL, 8, 128), F32),
            jax.ShapeDtypeStruct((8, 128), F32),
            jax.ShapeDtypeStruct((COLS // COL_BLOCK, 2, 128), F32),
        ],
        scratch_shapes=[pltpu.VMEM((ROWS, 128), F32), pltpu.VMEM((ROWS, 128), F32)],
        compiler_params=params(40),
        cost_estimate=pl.CostEstimate(flops=2 * ROWS * COLS * WIDTH, bytes_accessed=20 * MIB, transcendentals=3 << 20),
        name="scores",
    )(info, noise, data)


def merge_lse(parts_ref):
    parts = parts_ref[...]
    largest = jnp.max(parts, axis=0)
    return -(largest + jnp.log2(jnp.sum(jnp.exp2(parts - largest[None]), axis=0)))


def merge_scale(parts_ref):
    return 1.0 / jnp.sum(parts_ref[...], axis=0)


GROUP = 8


def first_columns_kernel(parts_ref, score_ref, lse_ref, noise_ref, column, big, total):
    step = pl.program_id(0)

    @pl.when(step == 0)
    def _():
        potential = merge_lse(parts_ref)
        noise_ref[...] = potential
        for a, piece in enumerate(to_column(potential)):
            column[128 * a : 128 * (a + 1), :] = piece
        big[...] = jnp.full(big.shape, MASKED, F32)
        total[...] = jnp.zeros(total.shape, F32)

    base = step * ROW_BLOCK
    tiles = COLS // 128

    def largest(g, carry):
        shift = column[pl.ds(pl.multiple_of(base + g * GROUP, GROUP), GROUP), :]
        at = pl.ds(pl.multiple_of(g * GROUP, GROUP), GROUP)
        return tuple(jnp.maximum(carry[t], score_ref[at, 128 * t : 128 * (t + 1)] + shift) for t in range(tiles))

    old = tuple(big[:, 128 * t : 128 * (t + 1)] for t in range(tiles))
    new = lax.fori_loop(0, ROW_BLOCK // GROUP, largest, old, unroll=2)

    def add(g, carry):
        shift = column[pl.ds(pl.multiple_of(base + g * GROUP, GROUP), GROUP), :]
        at = pl.ds(pl.multiple_of(g * GROUP, GROUP), GROUP)
        return tuple(
            carry[t] + jnp.exp2(score_ref[at, 128 * t : 128 * (t + 1)] + (shift - new[t])) for t in range(tiles)
        )

    start = tuple(total[:, 128 * t : 128 * (t + 1)] * jnp.exp2(old[t] - new[t]) for t in range(tiles))
    summed = lax.fori_loop(0, ROW_BLOCK // GROUP, add, start, unroll=2)
    for t in range(tiles):
        big[:, 128 * t : 128 * (t + 1)] = new[t]
        total[:, 128 * t : 128 * (t + 1)] = summed[t]

    @pl.when(step == pl.num_programs(0) - 1)
    def _():
        m = jnp.max(big[...], axis=0, keepdims=True)
        s = jnp.sum(total[...] * jnp.exp2(big[...] - m), axis=0, keepdims=True)
        lse_ref[...] = jnp.broadcast_to(from_lanes(m + jnp.log2(s))[None], lse_ref.shape)


def pass_call(kernel, inputs, in_specs, outs, out_specs, scratch, name, transcendentals=0):
    return pl.pallas_call(
        kernel,
        grid=(ROWS // ROW_BLOCK,),
        in_specs=in_specs,
        out_specs=out_specs,
        out_shape=outs,
        scratch_shapes=scratch,
        compiler_params=params(24),
        cost_estimate=pl.CostEstimate(flops=4 * ROWS * COLS, bytes_accessed=8 * MIB, transcendentals=transcendentals),
        name=name,
    )(*inputs)


FROM_COL = vmem((N_COL, 8, 128))
FROM_ROW = vmem((N_ROW, 16, 128))
NOISE = vmem((8, 128))
DATA = vmem((16, 128))
BLOCK = vmem((ROW_BLOCK, COLS), lambda i: (i, 0))
FROM_COL_SHAPE = jax.ShapeDtypeStruct((N_COL, 8, 128), F32)
FROM_ROW_SHAPE = jax.ShapeDtypeStruct((N_ROW, 16, 128), F32)
NOISE_SHAPE = jax.ShapeDtypeStruct((8, 128), F32)
DATA_SHAPE = jax.ShapeDtypeStruct((16, 128), F32)
BLOCK_SHAPE = jax.ShapeDtypeStruct((ROWS, COLS), F32)


def first_columns(parts, score):
    return pass_call(
        first_columns_kernel,
        (parts, score),
        [FROM_COL, BLOCK],
        [FROM_ROW_SHAPE, NOISE_SHAPE],
        [FROM_ROW, NOISE],
        [pltpu.VMEM((ROWS, 128), F32), pltpu.VMEM((8, COLS), F32), pltpu.VMEM((8, COLS), F32)],
        "first_columns",
        ROWS * COLS,
    )


def write_row_sums(sums, out_ref, rows, step):
    per = ROW_BLOCK // 128
    for a in range(per):
        piece = sums[128 * a : 128 * (a + 1), :].T
        rows[pl.ds(step * per + a, 1), :] = jnp.sum(piece, axis=0, keepdims=True)

    @pl.when(step == pl.num_programs(0) - 1)
    def _():
        out_ref[...] = jnp.broadcast_to(rows[...][None], out_ref.shape)


def kernel_matrix_kernel(parts_ref, noise_ref, score_ref, k_ref, sums_ref, data_ref, column, lanes, sums, rows):
    step = pl.program_id(0)

    @pl.when(step == 0)
    def _():
        potential = merge_lse(parts_ref)
        data_ref[...] = potential
        lanes[...] = jnp.broadcast_to(to_lanes(potential), lanes.shape)
        for a, piece in enumerate(to_column(noise_ref[...])):
            column[128 * a : 128 * (a + 1), :] = piece

    base = step * ROW_BLOCK
    tiles = COLS // 128
    shifts = [lanes[:, 128 * t : 128 * (t + 1)] for t in range(tiles)]

    def body(g, _):
        shift = column[pl.ds(pl.multiple_of(base + g * GROUP, GROUP), GROUP), :]
        at = pl.ds(pl.multiple_of(g * GROUP, GROUP), GROUP)
        summed = jnp.zeros((GROUP, 128), F32)
        for t in range(tiles):
            here = slice(128 * t, 128 * (t + 1))
            value = jnp.exp2(score_ref[at, here] + shift + shifts[t])
            k_ref[at, here] = value
            summed += value
        sums[at, :] = summed
        return 0

    lax.fori_loop(0, ROW_BLOCK // GROUP, body, 0, unroll=2)
    write_row_sums(sums, sums_ref, rows, step)


def kernel_matrix(parts, noise_potential, score):
    return pass_call(
        kernel_matrix_kernel,
        (parts, noise_potential, score),
        [FROM_ROW, NOISE, BLOCK],
        [BLOCK_SHAPE, FROM_COL_SHAPE, DATA_SHAPE],
        [BLOCK, FROM_COL, DATA],
        [
            pltpu.VMEM((ROWS, 128), F32),
            pltpu.VMEM((GROUP, COLS), F32),
            pltpu.VMEM((ROW_BLOCK, 128), F32),
            pltpu.VMEM((8, 128), F32),
        ],
        "kernel_matrix",
        ROWS * COLS,
    )


def column_sums_kernel(parts_ref, k_ref, sums_ref, scale_ref, column, total):
    step = pl.program_id(0)

    @pl.when(step == 0)
    def _():
        scale = merge_scale(parts_ref)
        scale_ref[...] = scale
        for a, piece in enumerate(to_column(scale)):
            column[128 * a : 128 * (a + 1), :] = piece
        total[...] = jnp.zeros(total.shape, F32)

    base = step * ROW_BLOCK
    tiles = COLS // 128

    def add(g, carry):
        scale = column[pl.ds(pl.multiple_of(base + g * GROUP, GROUP), GROUP), :]
        at = pl.ds(pl.multiple_of(g * GROUP, GROUP), GROUP)
        return tuple(carry[t] + k_ref[at, 128 * t : 128 * (t + 1)] * scale for t in range(tiles))

    start = tuple(total[:, 128 * t : 128 * (t + 1)] for t in range(tiles))
    summed = lax.fori_loop(0, ROW_BLOCK // GROUP, add, start, unroll=4)
    for t in range(tiles):
        total[:, 128 * t : 128 * (t + 1)] = summed[t]

    @pl.when(step == pl.num_programs(0) - 1)
    def _():
        s = jnp.sum(total[...], axis=0, keepdims=True)
        sums_ref[...] = jnp.broadcast_to(from_lanes(s)[None], sums_ref.shape)


def column_sums(parts, k):
    return pass_call(
        column_sums_kernel,
        (parts, k),
        [FROM_COL, BLOCK],
        [FROM_ROW_SHAPE, NOISE_SHAPE],
        [FROM_ROW, NOISE],
        [pltpu.VMEM((ROWS, 128), F32), pltpu.VMEM((GROUP, COLS), F32)],
        "column_sums",
    )


def row_sums_kernel(parts_ref, k_ref, sums_ref, lanes, sums, rows):
    step = pl.program_id(0)

    @pl.when(step == 0)
    def _():
        lanes[...] = jnp.broadcast_to(to_lanes(merge_scale(parts_ref)), lanes.shape)

    tiles = COLS // 128
    scales = [lanes[:, 128 * t : 128 * (t + 1)] for t in range(tiles)]

    def body(g, _):
        at = pl.ds(pl.multiple_of(g * GROUP, GROUP), GROUP)
        summed = [k_ref[at, 128 * t : 128 * (t + 1)] * scales[t] for t in range(4)]
        for t in range(4, tiles):
            summed[t % 4] += k_ref[at, 128 * t : 128 * (t + 1)] * scales[t]
        sums[at, :] = (summed[0] + summed[1]) + (summed[2] + summed[3])
        return 0

    lax.fori_loop(0, ROW_BLOCK // GROUP, body, 0, unroll=4)
    write_row_sums(sums, sums_ref, rows, step)


def row_sums(parts, k):
    return pass_call(
        row_sums_kernel,
        (parts, k),
        [FROM_ROW, BLOCK],
        [FROM_COL_SHAPE],
        [FROM_COL],
        [pltpu.VMEM((GROUP, COLS), F32), pltpu.VMEM((ROW_BLOCK, 128), F32), pltpu.VMEM((8, 128), F32)],
        "row_sums",
    )[0]


def coupling_kernel(parts_ref, scale_ref, k_ref, p_ref, sums_ref, data_scale_ref, column, lanes, sums, rows):
    step = pl.program_id(0)

    @pl.when(step == 0)
    def _():
        scale = merge_scale(parts_ref)
        data_scale_ref[...] = scale
        lanes[...] = jnp.broadcast_to(to_lanes(scale), lanes.shape)
        for a, piece in enumerate(to_column(scale_ref[...])):
            column[128 * a : 128 * (a + 1), :] = piece

    base = step * ROW_BLOCK
    tiles = COLS // 128

    def body(g, _):
        at = pl.ds(pl.multiple_of(g * 16, 16), 16)
        scale = column[pl.ds(pl.multiple_of(base + g * 16, 16), 16), :]
        summed = jnp.zeros((16, 128), F32)
        for t in range(tiles):
            here = slice(128 * t, 128 * (t + 1))
            value = k_ref[at, here] * (scale * lanes[:, here])
            p_ref[at, here] = value.astype(BF16)
            summed += value
        sums[at, :] = summed
        return 0

    lax.fori_loop(0, ROW_BLOCK // 16, body, 0, unroll=2)
    write_row_sums(sums, sums_ref, rows, step)


def coupling(parts, noise_scale, k):
    return pass_call(
        coupling_kernel,
        (parts, noise_scale, k),
        [FROM_ROW, NOISE, BLOCK],
        [jax.ShapeDtypeStruct((ROWS, COLS), BF16), FROM_COL_SHAPE, DATA_SHAPE],
        [BLOCK, FROM_COL, DATA],
        [
            pltpu.VMEM((ROWS, 128), F32),
            pltpu.VMEM((16, COLS), F32),
            pltpu.VMEM((ROW_BLOCK, 128), F32),
            pltpu.VMEM((8, 128), F32),
        ],
        "coupling",
    )


def target_kernel(p_ref, data_ref, out_ref):
    for r in range(ROWS // 256):
        at = slice(256 * r, 256 * (r + 1))
        summed = jnp.dot(p_ref[at, :], data_ref[0], preferred_element_type=F32)
        out_ref[0, at, :] = summed[:, :128].astype(BF16)
        out_ref[1, at, :] = summed[:, 128:].astype(BF16)


def targets(p, data):
    return pl.pallas_call(
        target_kernel,
        grid=(N_ROW,),
        in_specs=[vmem((ROWS, COLS)), vmem((1, COLS, 256), lambda k: (k, 0, 0))],
        out_specs=vmem((2, ROWS, 128), lambda k: (k, 0, 0)),
        out_shape=jax.ShapeDtypeStruct((N_COL, ROWS, 128), BF16),
        compiler_params=params(32),
        cost_estimate=pl.CostEstimate(flops=2 * ROWS * COLS * WIDTH, bytes_accessed=16 * MIB, transcendentals=0),
        name="targets",
    )(p, data)


def finish_kernel(parts_ref, sums_ref, noise_ref, out_ref):
    inverse = merge_scale(sums_ref)
    for a, piece in enumerate(to_column(inverse)):
        at = slice(128 * a, 128 * (a + 1))
        summed = parts_ref[0, at, :].astype(F32)
        for k in range(1, N_COL):
            summed += parts_ref[k, at, :].astype(F32)
        out_ref[at, :] = summed * piece - noise_ref[at, :].astype(F32)


def finish(parts, sums, noise):
    return pl.pallas_call(
        finish_kernel,
        out_shape=jax.ShapeDtypeStruct((ROWS, 128), F32),
        compiler_params=pltpu.CompilerParams(vmem_limit_bytes=24 * MIB),
        name="finish",
    )(parts, sums, noise)


def swap(x, axis):
    return lax.all_to_all(x, axis, 0, 0, tiled=True)


def per_device(noise_latents, data_latents, noise_sizes, data_sizes):
    places = jnp.stack([lax.axis_index("row") * ROWS, lax.axis_index("col") * COLS]).astype(jnp.int32)
    info = jnp.concatenate([noise_sizes, data_sizes, places])
    data = lax.all_gather(data_latents, "row")
    noise = lax.all_gather(noise_latents, "col")
    score, lse, noise_sq, data_sq = scores(info, noise, data)
    lse, noise_first = first_columns(swap(lse, "col"), score)
    k, sums, data_first = kernel_matrix(swap(lse, "row"), noise_first, score)
    sums, _ = column_sums(swap(sums, "col"), k)
    sums = row_sums(swap(sums, "row"), k)
    sums, noise_scale = column_sums(swap(sums, "col"), k)
    p, sums, data_scale = coupling(swap(sums, "row"), noise_scale, k)
    sums = swap(sums, "col")
    parts = swap(targets(p, data), "col")
    velocity = finish(parts, sums, noise_latents)
    noise_potential = (EPS * LN2) * (noise_first + jnp.log2(noise_scale)) + noise_sq / WIDTH
    data_potential = (EPS * LN2) * (data_first + jnp.log2(data_scale)) + data_sq.reshape(16, 128) / WIDTH
    return velocity, noise_potential.reshape(ROWS), data_potential.reshape(COLS)


def solution(mesh):
    placed = (P("row", "col"), P("col", "row"), P(), P())
    return jax.shard_map(
        per_device,
        mesh=mesh,
        in_specs=placed,
        out_specs=(P("row", "col"), P("row"), P("col")),
        check_vma=False,
    )
```

```python
import functools

import jax
import jax.numpy as jnp
from jax import lax
from jax.experimental import pallas as pl
from jax.experimental.pallas import tpu as pltpu
from jax.sharding import PartitionSpec as P

EPS = 0.05
LOG2E = 1.4426950408889634
LN2 = 0.6931471805599453
MASKED = -1e30
CLUSTERS = 8
F32 = jnp.float32
BF16 = jnp.bfloat16
MIB = 1 << 20

ROWS = 1024
COLS = 2048
WIDTH = 2048
COL_BLOCK = 256
ROW_BLOCK = 256
HALF = 512
N_ROW = 8
N_COL = 16
KAPPA = LOG2E / (WIDTH * EPS)


def vmem(shape, index_map=None):
    if index_map is None:
        return pl.BlockSpec(shape, lambda *_: (0,) * len(shape))
    return pl.BlockSpec(shape, index_map)


def params(mib):
    return pltpu.CompilerParams(vmem_limit_bytes=mib * MIB, dimension_semantics=("arbitrary",))


def lane_totals(pieces):
    return [piece.T for piece in pieces]


def to_column(rows):
    n = rows.shape[0]
    return [jnp.broadcast_to(rows[a : a + 1, :], (128, 128)).T for a in range(n)]


def to_lanes(rows):
    return jnp.concatenate([rows[a : a + 1, :] for a in range(rows.shape[0])], axis=1)


def from_lanes(row):
    return jnp.concatenate([row[:, 128 * a : 128 * (a + 1)] for a in range(row.shape[1] // 128)], axis=0)


def arrange_kernel(info_ref, *refs):
    out_ref, noise_sq_ref = refs[10:]
    z, x = info_ref[18], info_ref[19]
    sums = []
    for half in range(2):
        own, before, after, second_a, second_b = refs[5 * half : 5 * half + 5]
        at = slice(HALF * half, HALF * (half + 1))
        squares = jnp.zeros((HALF, 128), F32)
        for far, source in ((0, own), (1, before), (3, after), (2, None)):
            for near in range(4):
                if source is not None:
                    piece = source[near]
                else:
                    piece = second_a[near] if near < 2 else second_b[near - 2]
                if half == 0:
                    index = lax.rem(z + 4 - far, 4) * 4 + lax.rem(x + 4 - near, 4)
                else:
                    index = lax.rem(z + 4 - near, 4) * 4 + lax.rem(x + 4 - far, 4)
                out_ref[at, pl.ds(pl.multiple_of(index * 128, 128), 128)] = piece
                squares += piece.astype(F32) * piece.astype(F32)
        for a in range(HALF // 128):
            sums.append(jnp.sum(squares[128 * a : 128 * (a + 1), :].T, axis=0, keepdims=True))
    noise_sq_ref[...] = jnp.concatenate(sums, axis=0)


def arrange(info, pieces):
    return pl.pallas_call(
        arrange_kernel,
        in_specs=[pl.BlockSpec(memory_space=pltpu.SMEM)] + [pl.BlockSpec(memory_space=pltpu.VMEM)] * 10,
        out_shape=[jax.ShapeDtypeStruct((ROWS, WIDTH), BF16), NOISE_SHAPE],
        compiler_params=pltpu.CompilerParams(vmem_limit_bytes=24 * MIB),
        cost_estimate=pl.CostEstimate(flops=4 << 20, bytes_accessed=8 * MIB, transcendentals=0),
        name="arrange",
    )(info, *pieces)


def over_x(v, d):
    return lax.ppermute(v, "col", [(4 * z + x, 4 * z + (x + d) % 4) for z in range(4) for x in range(4)])


def over_z(v, d):
    return lax.ppermute(v, "col", [(4 * z + x, 4 * ((z + d) % 4) + x) for z in range(4) for x in range(4)])


def gather_noise(noise):
    gathered = []
    for half, (first, second) in enumerate(((over_x, over_z), (over_z, over_x))):
        own = noise[HALF * half : HALF * (half + 1)]
        own = jnp.stack([own] + [first(own, d) for d in (1, 2, 3)])
        gathered.append((own, second(own, 1), second(own, 3), second))
    pieces = []
    for own, before, after, second in gathered:
        pieces += [own, before, after, second(before[:2], 1), second(after[2:], 3)]
    return pieces


def score_kernel(info_ref, noise_ref, data_ref, score_ref, lse_ref, data_sq_ref, big, total):
    step = pl.program_id(0)

    @pl.when(step == 0)
    def _():
        big[...] = jnp.full(big.shape, MASKED, F32)
        total[...] = jnp.zeros(total.shape, F32)

    data = jnp.concatenate([data_ref[k] for k in range(N_ROW)], axis=1)
    data_sq = []
    for a in range(COL_BLOCK // 128):
        squares = jnp.zeros((128, 128), F32)
        for k in range(WIDTH // 128):
            piece = data[128 * a : 128 * (a + 1), 128 * k : 128 * (k + 1)].astype(F32)
            squares += piece * piece
        data_sq.append(jnp.sum(squares.T, axis=0, keepdims=True))
        data_sq_ref[0, a : a + 1, :] = data_sq[a]

    j = info_ref[17] + step * COL_BLOCK + lax.broadcasted_iota(jnp.int32, (1, COL_BLOCK), 1)
    low = jnp.zeros((1, COL_BLOCK), jnp.int32)
    high = jnp.zeros((1, COL_BLOCK), jnp.int32)
    noise_at = jnp.int32(0)
    data_at = jnp.int32(0)
    for c in range(CLUSTERS):
        noise_end = noise_at + info_ref[c]
        data_end = data_at + info_ref[8 + c]
        if c == CLUSTERS - 1:
            inside = j >= data_at
        else:
            inside = (j >= data_at) & (j < data_end)
        low = jnp.where(inside, noise_at, low)
        high = jnp.where(inside, noise_end, high)
        noise_at, data_at = noise_end, data_end
    low = low - info_ref[16]
    high = high - info_ref[16]

    half = 256
    for r in range(ROWS // half):
        inner = lax.dot_general(noise_ref[half * r : half * (r + 1), :], data, (((1,), (1,)), ((), ())), preferred_element_type=F32)
        i = half * r + lax.broadcasted_iota(jnp.int32, (half, COL_BLOCK), 0)
        score = jnp.where((i >= low) & (i < high), inner * (2.0 * KAPPA), MASKED)
        score_ref[half * r : half * (r + 1), :] = score
        lo = score[:, :128] - KAPPA * data_sq[0]
        hi = score[:, 128:] - KAPPA * data_sq[1]
        at = slice(half * r, half * (r + 1))
        old = big[at, :]
        new = jnp.maximum(old, jnp.maximum(lo, hi))
        total[at, :] = total[at, :] * jnp.exp2(old - new) + (jnp.exp2(lo - new) + jnp.exp2(hi - new))
        big[at, :] = new

    @pl.when(step == pl.num_programs(0) - 1)
    def _():
        rows = []
        for a in range(ROWS // 128):
            at = slice(128 * a, 128 * (a + 1))
            m = big[at, :].T
            s = total[at, :].T
            largest = jnp.max(m, axis=0, keepdims=True)
            summed = jnp.sum(s * jnp.exp2(m - largest), axis=0, keepdims=True)
            rows.append(largest + jnp.log2(summed))
        lse_ref[...] = jnp.broadcast_to(jnp.concatenate(rows, axis=0)[None], lse_ref.shape)


def scores(info, noise, data):
    return pl.pallas_call(
        score_kernel,
        grid=(COLS // COL_BLOCK,),
        in_specs=[
            pl.BlockSpec(memory_space=pltpu.SMEM),
            vmem((ROWS, WIDTH)),
            vmem((N_ROW, COL_BLOCK, 256), lambda j: (0, j, 0)),
        ],
        out_specs=[
            vmem((ROWS, COL_BLOCK), lambda j: (0, j)),
            vmem((N_COL, 8, 128)),
            vmem((1, 2, 128), lambda j: (j, 0, 0)),
        ],
        out_shape=[
            jax.ShapeDtypeStruct((ROWS, COLS), F32),
            jax.ShapeDtypeStruct((N_COL, 8, 128), F32),
            jax.ShapeDtypeStruct((COLS // COL_BLOCK, 2, 128), F32),
        ],
        scratch_shapes=[pltpu.VMEM((ROWS, 128), F32), pltpu.VMEM((ROWS, 128), F32)],
        compiler_params=params(40),
        cost_estimate=pl.CostEstimate(flops=2 * ROWS * COLS * WIDTH, bytes_accessed=20 * MIB, transcendentals=3 << 20),
        name="scores",
    )(info, noise, data)


def merge_lse(parts_ref):
    parts = parts_ref[...]
    largest = jnp.max(parts, axis=0)
    return -(largest + jnp.log2(jnp.sum(jnp.exp2(parts - largest[None]), axis=0)))


def merge_scale(parts_ref):
    return 1.0 / jnp.sum(parts_ref[...], axis=0)


GROUP = 8


def first_columns_kernel(parts_ref, score_ref, lse_ref, noise_ref, column, big, total):
    step = pl.program_id(0)

    @pl.when(step == 0)
    def _():
        potential = merge_lse(parts_ref)
        noise_ref[...] = potential
        for a, piece in enumerate(to_column(potential)):
            column[128 * a : 128 * (a + 1), :] = piece
        big[...] = jnp.full(big.shape, MASKED, F32)
        total[...] = jnp.zeros(total.shape, F32)

    base = step * ROW_BLOCK
    tiles = COLS // 128

    def largest(g, carry):
        shift = column[pl.ds(pl.multiple_of(base + g * GROUP, GROUP), GROUP), :]
        at = pl.ds(pl.multiple_of(g * GROUP, GROUP), GROUP)
        return tuple(jnp.maximum(carry[t], score_ref[at, 128 * t : 128 * (t + 1)] + shift) for t in range(tiles))

    old = tuple(big[:, 128 * t : 128 * (t + 1)] for t in range(tiles))
    new = lax.fori_loop(0, ROW_BLOCK // GROUP, largest, old, unroll=2)

    def add(g, carry):
        shift = column[pl.ds(pl.multiple_of(base + g * GROUP, GROUP), GROUP), :]
        at = pl.ds(pl.multiple_of(g * GROUP, GROUP), GROUP)
        return tuple(
            carry[t] + jnp.exp2(score_ref[at, 128 * t : 128 * (t + 1)] + (shift - new[t])) for t in range(tiles)
        )

    start = tuple(total[:, 128 * t : 128 * (t + 1)] * jnp.exp2(old[t] - new[t]) for t in range(tiles))
    summed = lax.fori_loop(0, ROW_BLOCK // GROUP, add, start, unroll=2)
    for t in range(tiles):
        big[:, 128 * t : 128 * (t + 1)] = new[t]
        total[:, 128 * t : 128 * (t + 1)] = summed[t]

    @pl.when(step == pl.num_programs(0) - 1)
    def _():
        m = jnp.max(big[...], axis=0, keepdims=True)
        s = jnp.sum(total[...] * jnp.exp2(big[...] - m), axis=0, keepdims=True)
        lse_ref[...] = jnp.broadcast_to(from_lanes(m + jnp.log2(s))[None], lse_ref.shape)


def pass_call(kernel, inputs, in_specs, outs, out_specs, scratch, name, transcendentals=0):
    return pl.pallas_call(
        kernel,
        grid=(ROWS // ROW_BLOCK,),
        in_specs=in_specs,
        out_specs=out_specs,
        out_shape=outs,
        scratch_shapes=scratch,
        compiler_params=params(24),
        cost_estimate=pl.CostEstimate(flops=4 * ROWS * COLS, bytes_accessed=8 * MIB, transcendentals=transcendentals),
        name=name,
    )(*inputs)


FROM_COL = vmem((N_COL, 8, 128))
FROM_ROW = vmem((N_ROW, 16, 128))
NOISE = vmem((8, 128))
DATA = vmem((16, 128))
BLOCK = vmem((ROW_BLOCK, COLS), lambda i: (i, 0))
FROM_COL_SHAPE = jax.ShapeDtypeStruct((N_COL, 8, 128), F32)
FROM_ROW_SHAPE = jax.ShapeDtypeStruct((N_ROW, 16, 128), F32)
NOISE_SHAPE = jax.ShapeDtypeStruct((8, 128), F32)
DATA_SHAPE = jax.ShapeDtypeStruct((16, 128), F32)
BLOCK_SHAPE = jax.ShapeDtypeStruct((ROWS, COLS), F32)


def first_columns(parts, score):
    return pass_call(
        first_columns_kernel,
        (parts, score),
        [FROM_COL, BLOCK],
        [FROM_ROW_SHAPE, NOISE_SHAPE],
        [FROM_ROW, NOISE],
        [pltpu.VMEM((ROWS, 128), F32), pltpu.VMEM((8, COLS), F32), pltpu.VMEM((8, COLS), F32)],
        "first_columns",
        ROWS * COLS,
    )


def write_row_sums(sums, out_ref, rows, step):
    per = ROW_BLOCK // 128
    for a in range(per):
        piece = sums[128 * a : 128 * (a + 1), :].T
        rows[pl.ds(step * per + a, 1), :] = jnp.sum(piece, axis=0, keepdims=True)

    @pl.when(step == pl.num_programs(0) - 1)
    def _():
        out_ref[...] = jnp.broadcast_to(rows[...][None], out_ref.shape)


def kernel_matrix_kernel(parts_ref, noise_ref, score_ref, k_ref, sums_ref, data_ref, column, lanes, sums, rows):
    step = pl.program_id(0)

    @pl.when(step == 0)
    def _():
        potential = merge_lse(parts_ref)
        data_ref[...] = potential
        lanes[...] = jnp.broadcast_to(to_lanes(potential), lanes.shape)
        for a, piece in enumerate(to_column(noise_ref[...])):
            column[128 * a : 128 * (a + 1), :] = piece

    base = step * ROW_BLOCK
    tiles = COLS // 128
    shifts = [lanes[:, 128 * t : 128 * (t + 1)] for t in range(tiles)]

    def body(g, _):
        shift = column[pl.ds(pl.multiple_of(base + g * GROUP, GROUP), GROUP), :]
        at = pl.ds(pl.multiple_of(g * GROUP, GROUP), GROUP)
        summed = jnp.zeros((GROUP, 128), F32)
        for t in range(tiles):
            here = slice(128 * t, 128 * (t + 1))
            value = jnp.exp2(score_ref[at, here] + shift + shifts[t])
            k_ref[at, here] = value
            summed += value
        sums[at, :] = summed
        return 0

    lax.fori_loop(0, ROW_BLOCK // GROUP, body, 0, unroll=2)
    write_row_sums(sums, sums_ref, rows, step)


def kernel_matrix(parts, noise_potential, score):
    return pass_call(
        kernel_matrix_kernel,
        (parts, noise_potential, score),
        [FROM_ROW, NOISE, BLOCK],
        [BLOCK_SHAPE, FROM_COL_SHAPE, DATA_SHAPE],
        [BLOCK, FROM_COL, DATA],
        [
            pltpu.VMEM((ROWS, 128), F32),
            pltpu.VMEM((GROUP, COLS), F32),
            pltpu.VMEM((ROW_BLOCK, 128), F32),
            pltpu.VMEM((8, 128), F32),
        ],
        "kernel_matrix",
        ROWS * COLS,
    )


def column_sums_kernel(parts_ref, k_ref, sums_ref, scale_ref, column, total):
    step = pl.program_id(0)

    @pl.when(step == 0)
    def _():
        scale = merge_scale(parts_ref)
        scale_ref[...] = scale
        for a, piece in enumerate(to_column(scale)):
            column[128 * a : 128 * (a + 1), :] = piece
        total[...] = jnp.zeros(total.shape, F32)

    base = step * ROW_BLOCK
    tiles = COLS // 128

    def add(g, carry):
        scale = column[pl.ds(pl.multiple_of(base + g * GROUP, GROUP), GROUP), :]
        at = pl.ds(pl.multiple_of(g * GROUP, GROUP), GROUP)
        return tuple(carry[t] + k_ref[at, 128 * t : 128 * (t + 1)] * scale for t in range(tiles))

    start = tuple(total[:, 128 * t : 128 * (t + 1)] for t in range(tiles))
    summed = lax.fori_loop(0, ROW_BLOCK // GROUP, add, start, unroll=4)
    for t in range(tiles):
        total[:, 128 * t : 128 * (t + 1)] = summed[t]

    @pl.when(step == pl.num_programs(0) - 1)
    def _():
        s = jnp.sum(total[...], axis=0, keepdims=True)
        sums_ref[...] = jnp.broadcast_to(from_lanes(s)[None], sums_ref.shape)


def column_sums(parts, k):
    return pass_call(
        column_sums_kernel,
        (parts, k),
        [FROM_COL, BLOCK],
        [FROM_ROW_SHAPE, NOISE_SHAPE],
        [FROM_ROW, NOISE],
        [pltpu.VMEM((ROWS, 128), F32), pltpu.VMEM((GROUP, COLS), F32)],
        "column_sums",
    )


def row_sums_kernel(parts_ref, k_ref, sums_ref, lanes, sums, rows):
    step = pl.program_id(0)

    @pl.when(step == 0)
    def _():
        lanes[...] = jnp.broadcast_to(to_lanes(merge_scale(parts_ref)), lanes.shape)

    tiles = COLS // 128
    scales = [lanes[:, 128 * t : 128 * (t + 1)] for t in range(tiles)]

    def body(g, _):
        at = pl.ds(pl.multiple_of(g * GROUP, GROUP), GROUP)
        summed = [k_ref[at, 128 * t : 128 * (t + 1)] * scales[t] for t in range(4)]
        for t in range(4, tiles):
            summed[t % 4] += k_ref[at, 128 * t : 128 * (t + 1)] * scales[t]
        sums[at, :] = (summed[0] + summed[1]) + (summed[2] + summed[3])
        return 0

    lax.fori_loop(0, ROW_BLOCK // GROUP, body, 0, unroll=4)
    write_row_sums(sums, sums_ref, rows, step)


def row_sums(parts, k):
    return pass_call(
        row_sums_kernel,
        (parts, k),
        [FROM_ROW, BLOCK],
        [FROM_COL_SHAPE],
        [FROM_COL],
        [pltpu.VMEM((GROUP, COLS), F32), pltpu.VMEM((ROW_BLOCK, 128), F32), pltpu.VMEM((8, 128), F32)],
        "row_sums",
    )[0]


def coupling_kernel(
    parts_ref, scale_ref, noise_first, noise_sq, data_first, data_sq, k_ref,
    pa_ref, pb_ref, sums_ref, noise_ref, data_ref, column, lanes, sums,
):
    step = pl.program_id(0)

    @pl.when(step == 0)
    def _():
        scale = merge_scale(parts_ref)
        lanes[...] = jnp.broadcast_to(to_lanes(scale), lanes.shape)
        for a, piece in enumerate(to_column(scale_ref[...])):
            column[128 * a : 128 * (a + 1), :] = piece
        noise_ref[...] = (EPS * LN2) * (noise_first[...] + jnp.log2(scale_ref[...])) + noise_sq[...] * (1.0 / WIDTH)
        potential = (EPS * LN2) * (data_first[...] + jnp.log2(scale))
        for k in range(8):
            data_ref[2 * k : 2 * k + 2, :] = potential[2 * k : 2 * k + 2, :] + data_sq[k] * (1.0 / WIDTH)

    base = step * ROW_BLOCK
    tiles = COLS // 128

    def block(p_ref):
        def body(g, _):
            at = pl.ds(pl.multiple_of(g * 16, 16), 16)
            scale = column[pl.ds(pl.multiple_of(base + g * 16, 16), 16), :]
            summed = jnp.zeros((16, 128), F32)
            for t in range(tiles):
                here = slice(128 * t, 128 * (t + 1))
                value = k_ref[at, here] * (scale * lanes[:, here])
                p_ref[at, here] = value.astype(BF16)
                summed += value
            sums[at, :] = summed
            return 0

        lax.fori_loop(0, ROW_BLOCK // 16, body, 0, unroll=2)

    @pl.when(step < 2)
    def _():
        block(pa_ref)

    @pl.when(step >= 2)
    def _():
        block(pb_ref)

    per = ROW_BLOCK // 128
    for a in range(per):
        piece = sums[128 * a : 128 * (a + 1), :].T
        sums_ref[pl.ds(step * per + a, 1), :] = jnp.sum(piece, axis=0, keepdims=True)


def coupling(parts, noise_scale, noise_first, noise_sq, data_first, data_sq, k):
    half = jax.ShapeDtypeStruct((HALF, COLS), BF16)
    return pass_call(
        coupling_kernel,
        (parts, noise_scale, noise_first, noise_sq, data_first, data_sq, k),
        [FROM_ROW, NOISE, NOISE, NOISE, DATA, vmem((8, 2, 128)), BLOCK],
        [half, half, NOISE_SHAPE, NOISE_SHAPE, DATA_SHAPE],
        [
            vmem((ROW_BLOCK, COLS), lambda i: (jnp.minimum(i, 1), 0)),
            vmem((ROW_BLOCK, COLS), lambda i: (jnp.maximum(i - 2, 0), 0)),
            NOISE,
            NOISE,
            DATA,
        ],
        [
            pltpu.VMEM((ROWS, 128), F32),
            pltpu.VMEM((16, COLS), F32),
            pltpu.VMEM((ROW_BLOCK, 128), F32),
        ],
        "coupling",
    )


EXTRA = 16


def split(value):
    high = value.astype(BF16)
    return high, (value - high.astype(F32)).astype(BF16)


def target_kernel(side, d, info_ref, p_ref, sums_ref, *refs):
    data_refs, out_ref = refs[:-1], refs[-1]
    if side == 0:
        lanes = pl.ds(pl.multiple_of(lax.rem(info_ref[19] + d, 2) * 128, 128), 128)
        data = jnp.concatenate([ref[0, :, lanes] for ref in data_refs], axis=1)
    else:
        data = data_refs[0][0]
    summed = jnp.dot(p_ref[...], data, preferred_element_type=F32).astype(BF16)
    high, low = split(sums_ref[4 * side : 4 * side + 4, :])
    tail = jnp.concatenate([high, low, high, low], axis=0)
    for b in range(2):
        out_ref[b, :HALF, :] = summed[:, 128 * b : 128 * (b + 1)]
        out_ref[b, HALF:, :] = tail


def message(side, d, info, p, sums, data):
    if side == 0:
        chunks = [
            vmem((1, COLS, 256), lambda g, f, b=b: (4 * g + 2 * b + lax.rem(f[19] + d, 4) // 2, 0, 0)) for b in (0, 1)
        ]
    else:
        chunks = [vmem((1, COLS, 256), lambda g, f: (2 * lax.rem(f[18] + d, 4) + g, 0, 0))]
    return pl.pallas_call(
        functools.partial(target_kernel, side, d),
        grid_spec=pltpu.PrefetchScalarGridSpec(
            num_scalar_prefetch=1,
            grid=(2,),
            in_specs=[vmem((HALF, COLS)), NOISE] + chunks,
            out_specs=vmem((2, HALF + EXTRA, 128), lambda g, f: (g, 0, 0)),
        ),
        out_shape=jax.ShapeDtypeStruct((4, HALF + EXTRA, 128), BF16),
        compiler_params=params(24),
        cost_estimate=pl.CostEstimate(flops=ROWS * COLS * WIDTH // 4, bytes_accessed=4 * MIB, transcendentals=0),
        name="targets",
    )(info, p, sums, *[data] * len(chunks))


def row_sums_of(ref, index=None):
    high, low = (ref[HALF + 4 * i : HALF + 4 * i + 4, :] if index is None else ref[index, HALF + 4 * i : HALF + 4 * i + 4, :] for i in (0, 1))
    return high.astype(F32) + low.astype(F32)


def combine_kernel(side, info_ref, own, r1, r2, r3, keep_ref, s1, s2, s3):
    place = info_ref[18 + side]
    sums = (row_sums_of(own, 0) + row_sums_of(r1, 0)) + (row_sums_of(r2, 0) + row_sums_of(r3, 0))
    high, low = split(sums)
    tail = jnp.concatenate([high, low, high, low], axis=0)

    def summed(index):
        at = slice(0, HALF)
        return (own[index, at, :].astype(F32) + r1[index, at, :].astype(F32)) + (
            r2[index, at, :].astype(F32) + r3[index, at, :].astype(F32)
        )

    for d, out_ref in ((1, s1), (2, s2), (3, s3)):
        out_ref[:HALF, :] = summed(lax.rem(place + d, 4)).astype(BF16)
        out_ref[HALF:, :] = tail
    keep_ref[:HALF, :] = summed(place)
    keep_ref[HALF:, :] = jnp.concatenate([sums, jnp.zeros((EXTRA - 4, 128), F32)], axis=0)


def combine(side, info, parts):
    return pl.pallas_call(
        functools.partial(combine_kernel, side),
        in_specs=[pl.BlockSpec(memory_space=pltpu.SMEM)] + [pl.BlockSpec(memory_space=pltpu.VMEM)] * 4,
        out_shape=[jax.ShapeDtypeStruct((HALF + EXTRA, 128), F32)] + [jax.ShapeDtypeStruct((HALF + EXTRA, 128), BF16)] * 3,
        compiler_params=pltpu.CompilerParams(vmem_limit_bytes=16 * MIB),
        cost_estimate=pl.CostEstimate(flops=1 << 20, bytes_accessed=3 * MIB, transcendentals=0),
        name="combine",
    )(info, *parts)


def finish_kernel(noise_ref, *refs):
    out_ref = refs[-1]
    for half in range(2):
        own, *others = refs[4 * half : 4 * half + 4]
        sums = own[HALF : HALF + 4, :]
        for other in others:
            sums += row_sums_of(other)
        for a, inverse in enumerate(to_column(1.0 / sums)):
            here = slice(128 * a, 128 * (a + 1))
            at = slice(HALF * half + 128 * a, HALF * half + 128 * (a + 1))
            summed = own[here, :]
            for other in others:
                summed += other[here, :].astype(F32)
            out_ref[at, :] = summed * inverse - noise_ref[at, :].astype(F32)


def finish(noise, parts):
    return pl.pallas_call(
        finish_kernel,
        out_shape=jax.ShapeDtypeStruct((ROWS, 128), F32),
        compiler_params=pltpu.CompilerParams(vmem_limit_bytes=16 * MIB),
        name="finish",
    )(noise, *parts)


def swap(x, axis):
    return lax.all_to_all(x, axis, 0, 0, tiled=True)


def per_device(noise_latents, data_latents, noise_sizes, data_sizes):
    row, col = lax.axis_index("row"), lax.axis_index("col")
    places = jnp.stack([row * ROWS, col * COLS, col // 4, col % 4]).astype(jnp.int32)
    info = jnp.concatenate([noise_sizes, data_sizes, places])
    data = lax.all_gather(data_latents, "row")
    noise, noise_sq = arrange(info, gather_noise(noise_latents))
    score, lse, data_sq = scores(info, noise, data)
    lse, noise_first = first_columns(swap(lse, "col"), score)
    k, sums, data_first = kernel_matrix(swap(lse, "row"), noise_first, score)
    sums, _ = column_sums(swap(sums, "col"), k)
    sums = row_sums(swap(sums, "row"), k)
    sums, noise_scale = column_sums(swap(sums, "col"), k)
    *p, sums, noise_potential, data_potential = coupling(
        swap(sums, "row"), noise_scale, noise_first, noise_sq, data_first, data_sq, k
    )
    way = (over_x, over_z)
    parts = [[None] * 4, [None] * 4]
    for d in (2, 1, 3, 0):
        for side in (0, 1):
            made = message(side, d, info, p[side], sums, data)
            parts[side][d] = way[side](made, d) if d else made
    ends = []
    for side in (0, 1):
        keep, *others = combine(side, info, parts[side])
        ends += [keep] + [way[1 - side](v, d) for d, v in zip((1, 2, 3), others)]
    velocity = finish(noise_latents, ends)
    return velocity, noise_potential.reshape(ROWS), data_potential.reshape(COLS)


def solution(mesh):
    placed = (P("row", "col"), P("col", "row"), P(), P())
    return jax.shard_map(
        per_device,
        mesh=mesh,
        in_specs=placed,
        out_specs=(P("row", "col"), P("row"), P("col")),
        check_vma=False,
    )
```

```python
import functools

import jax
import jax.numpy as jnp
from jax import lax
from jax.experimental import pallas as pl
from jax.experimental.pallas import tpu as pltpu
from jax.sharding import PartitionSpec as P

EPS = 0.05
LOG2E = 1.4426950408889634
LN2 = 0.6931471805599453
MASKED = -1e30
CLUSTERS = 8
F32 = jnp.float32
BF16 = jnp.bfloat16
MIB = 1 << 20

ROWS = 1024
COLS = 2048
WIDTH = 2048
COL_BLOCK = 256
ROW_BLOCK = 256
HALF = 512
N_ROW = 8
N_COL = 16
KAPPA = LOG2E / (WIDTH * EPS)


def vmem(shape, index_map=None):
    if index_map is None:
        return pl.BlockSpec(shape, lambda *_: (0,) * len(shape))
    return pl.BlockSpec(shape, index_map)


def params(mib):
    return pltpu.CompilerParams(vmem_limit_bytes=mib * MIB, dimension_semantics=("arbitrary",))


def lane_totals(pieces):
    return [piece.T for piece in pieces]


def to_column(rows):
    n = rows.shape[0]
    return [jnp.broadcast_to(rows[a : a + 1, :], (128, 128)).T for a in range(n)]


def to_lanes(rows):
    return jnp.concatenate([rows[a : a + 1, :] for a in range(rows.shape[0])], axis=1)


def from_lanes(row):
    return jnp.concatenate([row[:, 128 * a : 128 * (a + 1)] for a in range(row.shape[1] // 128)], axis=0)


def arrange_kernel(info_ref, *refs):
    out_ref, noise_sq_ref = refs[10:]
    z, x = info_ref[18], info_ref[19]
    sums = []
    for half in range(2):
        own, before, after, second_a, second_b = refs[5 * half : 5 * half + 5]
        at = slice(HALF * half, HALF * (half + 1))
        squares = jnp.zeros((HALF, 128), F32)
        for far, source in ((0, own), (1, before), (3, after), (2, None)):
            for near in range(4):
                if source is not None:
                    piece = source[near]
                else:
                    piece = second_a[near] if near < 2 else second_b[near - 2]
                if half == 0:
                    index = lax.rem(z + 4 - far, 4) * 4 + lax.rem(x + 4 - near, 4)
                else:
                    index = lax.rem(z + 4 - near, 4) * 4 + lax.rem(x + 4 - far, 4)
                out_ref[at, pl.ds(pl.multiple_of(index * 128, 128), 128)] = piece
                squares += piece.astype(F32) * piece.astype(F32)
        for a in range(HALF // 128):
            sums.append(jnp.sum(squares[128 * a : 128 * (a + 1), :].T, axis=0, keepdims=True))
    noise_sq_ref[...] = jnp.concatenate(sums, axis=0)


def arrange(info, pieces):
    return pl.pallas_call(
        arrange_kernel,
        in_specs=[pl.BlockSpec(memory_space=pltpu.SMEM)] + [pl.BlockSpec(memory_space=pltpu.VMEM)] * 10,
        out_shape=[jax.ShapeDtypeStruct((ROWS, WIDTH), BF16), NOISE_SHAPE],
        compiler_params=pltpu.CompilerParams(vmem_limit_bytes=24 * MIB),
        cost_estimate=pl.CostEstimate(flops=4 << 20, bytes_accessed=8 * MIB, transcendentals=0),
        name="arrange",
    )(info, *pieces)


def over_x(v, d):
    return lax.ppermute(v, "col", [(4 * z + x, 4 * z + (x + d) % 4) for z in range(4) for x in range(4)])


def over_z(v, d):
    return lax.ppermute(v, "col", [(4 * z + x, 4 * ((z + d) % 4) + x) for z in range(4) for x in range(4)])


def gather_noise(noise):
    gathered = []
    for half, (first, second) in enumerate(((over_x, over_z), (over_z, over_x))):
        own = noise[HALF * half : HALF * (half + 1)]
        own = jnp.stack([own] + [first(own, d) for d in (1, 2, 3)])
        gathered.append((own, second(own, 1), second(own, 3), second))
    pieces = []
    for own, before, after, second in gathered:
        pieces += [own, before, after, second(before[:2], 1), second(after[2:], 3)]
    return pieces


def score_kernel(info_ref, noise_ref, data_ref, score_ref, lse_ref, data_sq_ref, big, total):
    step = pl.program_id(0)

    @pl.when(step == 0)
    def _():
        big[...] = jnp.full(big.shape, MASKED, F32)
        total[...] = jnp.zeros(total.shape, F32)

    data = jnp.concatenate([data_ref[k] for k in range(N_ROW)], axis=1)
    data_sq = []
    for a in range(COL_BLOCK // 128):
        squares = jnp.zeros((128, 128), F32)
        for k in range(WIDTH // 128):
            piece = data[128 * a : 128 * (a + 1), 128 * k : 128 * (k + 1)].astype(F32)
            squares += piece * piece
        data_sq.append(jnp.sum(squares.T, axis=0, keepdims=True))
        data_sq_ref[0, a : a + 1, :] = data_sq[a]

    j = info_ref[17] + step * COL_BLOCK + lax.broadcasted_iota(jnp.int32, (1, COL_BLOCK), 1)
    low = jnp.zeros((1, COL_BLOCK), jnp.int32)
    high = jnp.zeros((1, COL_BLOCK), jnp.int32)
    noise_at = jnp.int32(0)
    data_at = jnp.int32(0)
    for c in range(CLUSTERS):
        noise_end = noise_at + info_ref[c]
        data_end = data_at + info_ref[8 + c]
        if c == CLUSTERS - 1:
            inside = j >= data_at
        else:
            inside = (j >= data_at) & (j < data_end)
        low = jnp.where(inside, noise_at, low)
        high = jnp.where(inside, noise_end, high)
        noise_at, data_at = noise_end, data_end
    low = low - info_ref[16]
    high = high - info_ref[16]

    half = 256
    for r in range(ROWS // half):
        inner = lax.dot_general(noise_ref[half * r : half * (r + 1), :], data, (((1,), (1,)), ((), ())), preferred_element_type=F32)
        i = half * r + lax.broadcasted_iota(jnp.int32, (half, COL_BLOCK), 0)
        score = jnp.where((i >= low) & (i < high), inner * (2.0 * KAPPA), MASKED)
        score_ref[half * r : half * (r + 1), :] = score
        lo = score[:, :128] - KAPPA * data_sq[0]
        hi = score[:, 128:] - KAPPA * data_sq[1]
        at = slice(half * r, half * (r + 1))
        old = big[at, :]
        new = jnp.maximum(old, jnp.maximum(lo, hi))
        total[at, :] = total[at, :] * jnp.exp2(old - new) + (jnp.exp2(lo - new) + jnp.exp2(hi - new))
        big[at, :] = new

    @pl.when(step == pl.num_programs(0) - 1)
    def _():
        rows = []
        for a in range(ROWS // 128):
            at = slice(128 * a, 128 * (a + 1))
            m = big[at, :].T
            s = total[at, :].T
            largest = jnp.max(m, axis=0, keepdims=True)
            summed = jnp.sum(s * jnp.exp2(m - largest), axis=0, keepdims=True)
            rows.append(largest + jnp.log2(summed))
        lse_ref[...] = jnp.broadcast_to(jnp.concatenate(rows, axis=0)[None], lse_ref.shape)


def scores(info, noise, data):
    return pl.pallas_call(
        score_kernel,
        grid=(COLS // COL_BLOCK,),
        in_specs=[
            pl.BlockSpec(memory_space=pltpu.SMEM),
            vmem((ROWS, WIDTH)),
            vmem((N_ROW, COL_BLOCK, 256), lambda j: (0, j, 0)),
        ],
        out_specs=[
            vmem((ROWS, COL_BLOCK), lambda j: (0, j)),
            vmem((N_COL, 8, 128)),
            vmem((1, 2, 128), lambda j: (j, 0, 0)),
        ],
        out_shape=[
            jax.ShapeDtypeStruct((ROWS, COLS), F32),
            jax.ShapeDtypeStruct((N_COL, 8, 128), F32),
            jax.ShapeDtypeStruct((COLS // COL_BLOCK, 2, 128), F32),
        ],
        scratch_shapes=[pltpu.VMEM((ROWS, 128), F32), pltpu.VMEM((ROWS, 128), F32)],
        compiler_params=params(40),
        cost_estimate=pl.CostEstimate(flops=2 * ROWS * COLS * WIDTH, bytes_accessed=20 * MIB, transcendentals=3 << 20),
        name="scores",
    )(info, noise, data)


def merge_lse(parts_ref):
    parts = parts_ref[...]
    largest = jnp.max(parts, axis=0)
    return -(largest + jnp.log2(jnp.sum(jnp.exp2(parts - largest[None]), axis=0)))


def merge_scale(parts_ref):
    return 1.0 / jnp.sum(parts_ref[...], axis=0)


GROUP = 8


def first_columns_kernel(parts_ref, score_ref, lse_ref, noise_ref, column, big, total):
    step = pl.program_id(0)

    @pl.when(step == 0)
    def _():
        potential = merge_lse(parts_ref)
        noise_ref[...] = potential
        for a, piece in enumerate(to_column(potential)):
            column[128 * a : 128 * (a + 1), :] = piece
        big[...] = jnp.full(big.shape, MASKED, F32)
        total[...] = jnp.zeros(total.shape, F32)

    base = step * ROW_BLOCK
    tiles = COLS // 128

    def largest(g, carry):
        shift = column[pl.ds(pl.multiple_of(base + g * GROUP, GROUP), GROUP), :]
        at = pl.ds(pl.multiple_of(g * GROUP, GROUP), GROUP)
        return tuple(jnp.maximum(carry[t], score_ref[at, 128 * t : 128 * (t + 1)] + shift) for t in range(tiles))

    old = tuple(big[:, 128 * t : 128 * (t + 1)] for t in range(tiles))
    new = lax.fori_loop(0, ROW_BLOCK // GROUP, largest, old, unroll=2)

    def add(g, carry):
        shift = column[pl.ds(pl.multiple_of(base + g * GROUP, GROUP), GROUP), :]
        at = pl.ds(pl.multiple_of(g * GROUP, GROUP), GROUP)
        return tuple(
            carry[t] + jnp.exp2(score_ref[at, 128 * t : 128 * (t + 1)] + (shift - new[t])) for t in range(tiles)
        )

    start = tuple(total[:, 128 * t : 128 * (t + 1)] * jnp.exp2(old[t] - new[t]) for t in range(tiles))
    summed = lax.fori_loop(0, ROW_BLOCK // GROUP, add, start, unroll=2)
    for t in range(tiles):
        big[:, 128 * t : 128 * (t + 1)] = new[t]
        total[:, 128 * t : 128 * (t + 1)] = summed[t]

    @pl.when(step == pl.num_programs(0) - 1)
    def _():
        m = jnp.max(big[...], axis=0, keepdims=True)
        s = jnp.sum(total[...] * jnp.exp2(big[...] - m), axis=0, keepdims=True)
        lse_ref[...] = jnp.broadcast_to(from_lanes(m + jnp.log2(s))[None], lse_ref.shape)


def pass_call(kernel, inputs, in_specs, outs, out_specs, scratch, name, transcendentals=0):
    return pl.pallas_call(
        kernel,
        grid=(ROWS // ROW_BLOCK,),
        in_specs=in_specs,
        out_specs=out_specs,
        out_shape=outs,
        scratch_shapes=scratch,
        compiler_params=params(24),
        cost_estimate=pl.CostEstimate(flops=4 * ROWS * COLS, bytes_accessed=8 * MIB, transcendentals=transcendentals),
        name=name,
    )(*inputs)


FROM_COL = vmem((N_COL, 8, 128))
FROM_ROW = vmem((N_ROW, 16, 128))
NOISE = vmem((8, 128))
DATA = vmem((16, 128))
BLOCK = vmem((ROW_BLOCK, COLS), lambda i: (i, 0))
FROM_COL_SHAPE = jax.ShapeDtypeStruct((N_COL, 8, 128), F32)
FROM_ROW_SHAPE = jax.ShapeDtypeStruct((N_ROW, 16, 128), F32)
NOISE_SHAPE = jax.ShapeDtypeStruct((8, 128), F32)
DATA_SHAPE = jax.ShapeDtypeStruct((16, 128), F32)
BLOCK_SHAPE = jax.ShapeDtypeStruct((ROWS, COLS), F32)


def first_columns(parts, score):
    return pass_call(
        first_columns_kernel,
        (parts, score),
        [FROM_COL, BLOCK],
        [FROM_ROW_SHAPE, NOISE_SHAPE],
        [FROM_ROW, NOISE],
        [pltpu.VMEM((ROWS, 128), F32), pltpu.VMEM((8, COLS), F32), pltpu.VMEM((8, COLS), F32)],
        "first_columns",
        ROWS * COLS,
    )


def write_row_sums(sums, out_ref, rows, step):
    per = ROW_BLOCK // 128
    for a in range(per):
        piece = sums[128 * a : 128 * (a + 1), :].T
        rows[pl.ds(step * per + a, 1), :] = jnp.sum(piece, axis=0, keepdims=True)

    @pl.when(step == pl.num_programs(0) - 1)
    def _():
        out_ref[...] = jnp.broadcast_to(rows[...][None], out_ref.shape)


def kernel_matrix_kernel(parts_ref, noise_ref, score_ref, k_ref, sums_ref, data_ref, column, lanes, sums, rows):
    step = pl.program_id(0)

    @pl.when(step == 0)
    def _():
        potential = merge_lse(parts_ref)
        data_ref[...] = potential
        lanes[...] = jnp.broadcast_to(to_lanes(potential), lanes.shape)
        for a, piece in enumerate(to_column(noise_ref[...])):
            column[128 * a : 128 * (a + 1), :] = piece

    base = step * ROW_BLOCK
    tiles = COLS // 128
    shifts = [lanes[:, 128 * t : 128 * (t + 1)] for t in range(tiles)]

    def body(g, _):
        shift = column[pl.ds(pl.multiple_of(base + g * GROUP, GROUP), GROUP), :]
        at = pl.ds(pl.multiple_of(g * GROUP, GROUP), GROUP)
        summed = jnp.zeros((GROUP, 128), F32)
        for t in range(tiles):
            here = slice(128 * t, 128 * (t + 1))
            value = jnp.exp2(score_ref[at, here] + shift + shifts[t])
            k_ref[at, here] = value
            summed += value
        sums[at, :] = summed
        return 0

    lax.fori_loop(0, ROW_BLOCK // GROUP, body, 0, unroll=2)
    write_row_sums(sums, sums_ref, rows, step)


def kernel_matrix(parts, noise_potential, score):
    return pass_call(
        kernel_matrix_kernel,
        (parts, noise_potential, score),
        [FROM_ROW, NOISE, BLOCK],
        [BLOCK_SHAPE, FROM_COL_SHAPE, DATA_SHAPE],
        [BLOCK, FROM_COL, DATA],
        [
            pltpu.VMEM((ROWS, 128), F32),
            pltpu.VMEM((GROUP, COLS), F32),
            pltpu.VMEM((ROW_BLOCK, 128), F32),
            pltpu.VMEM((8, 128), F32),
        ],
        "kernel_matrix",
        ROWS * COLS,
    )


def column_sums_kernel(parts_ref, k_ref, sums_ref, scale_ref, column, total):
    step = pl.program_id(0)

    @pl.when(step == 0)
    def _():
        scale = merge_scale(parts_ref)
        scale_ref[...] = scale
        for a, piece in enumerate(to_column(scale)):
            column[128 * a : 128 * (a + 1), :] = piece
        total[...] = jnp.zeros(total.shape, F32)

    base = step * ROW_BLOCK
    tiles = COLS // 128

    def add(g, carry):
        scale = column[pl.ds(pl.multiple_of(base + g * GROUP, GROUP), GROUP), :]
        at = pl.ds(pl.multiple_of(g * GROUP, GROUP), GROUP)
        return tuple(carry[t] + k_ref[at, 128 * t : 128 * (t + 1)] * scale for t in range(tiles))

    start = tuple(total[:, 128 * t : 128 * (t + 1)] for t in range(tiles))
    summed = lax.fori_loop(0, ROW_BLOCK // GROUP, add, start, unroll=4)
    for t in range(tiles):
        total[:, 128 * t : 128 * (t + 1)] = summed[t]

    @pl.when(step == pl.num_programs(0) - 1)
    def _():
        s = jnp.sum(total[...], axis=0, keepdims=True)
        sums_ref[...] = jnp.broadcast_to(from_lanes(s)[None], sums_ref.shape)


def column_sums(parts, k):
    return pass_call(
        column_sums_kernel,
        (parts, k),
        [FROM_COL, BLOCK],
        [FROM_ROW_SHAPE, NOISE_SHAPE],
        [FROM_ROW, NOISE],
        [pltpu.VMEM((ROWS, 128), F32), pltpu.VMEM((GROUP, COLS), F32)],
        "column_sums",
    )


def row_sums_kernel(parts_ref, k_ref, sums_ref, lanes, sums, rows):
    step = pl.program_id(0)

    @pl.when(step == 0)
    def _():
        lanes[...] = jnp.broadcast_to(to_lanes(merge_scale(parts_ref)), lanes.shape)

    tiles = COLS // 128
    scales = [lanes[:, 128 * t : 128 * (t + 1)] for t in range(tiles)]

    def body(g, _):
        at = pl.ds(pl.multiple_of(g * GROUP, GROUP), GROUP)
        summed = [k_ref[at, 128 * t : 128 * (t + 1)] * scales[t] for t in range(4)]
        for t in range(4, tiles):
            summed[t % 4] += k_ref[at, 128 * t : 128 * (t + 1)] * scales[t]
        sums[at, :] = (summed[0] + summed[1]) + (summed[2] + summed[3])
        return 0

    lax.fori_loop(0, ROW_BLOCK // GROUP, body, 0, unroll=4)
    write_row_sums(sums, sums_ref, rows, step)


def row_sums(parts, k):
    return pass_call(
        row_sums_kernel,
        (parts, k),
        [FROM_ROW, BLOCK],
        [FROM_COL_SHAPE],
        [FROM_COL],
        [pltpu.VMEM((GROUP, COLS), F32), pltpu.VMEM((ROW_BLOCK, 128), F32), pltpu.VMEM((8, 128), F32)],
        "row_sums",
    )[0]


def coupling_kernel(
    parts_ref, scale_ref, noise_first, noise_sq, data_first, data_sq, k_ref,
    pa_ref, pb_ref, sums_ref, noise_ref, data_ref, column, lanes, sums,
):
    step = pl.program_id(0)

    @pl.when(step == 0)
    def _():
        scale = merge_scale(parts_ref)
        lanes[...] = jnp.broadcast_to(to_lanes(scale), lanes.shape)
        for a, piece in enumerate(to_column(scale_ref[...])):
            column[128 * a : 128 * (a + 1), :] = piece
        noise_ref[...] = (EPS * LN2) * (noise_first[...] + jnp.log2(scale_ref[...])) + noise_sq[...] * (1.0 / WIDTH)
        potential = (EPS * LN2) * (data_first[...] + jnp.log2(scale))
        for k in range(8):
            data_ref[2 * k : 2 * k + 2, :] = potential[2 * k : 2 * k + 2, :] + data_sq[k] * (1.0 / WIDTH)

    base = step * ROW_BLOCK
    tiles = COLS // 128

    def block(p_ref):
        def body(g, _):
            at = pl.ds(pl.multiple_of(g * 16, 16), 16)
            scale = column[pl.ds(pl.multiple_of(base + g * 16, 16), 16), :]
            summed = jnp.zeros((16, 128), F32)
            for t in range(tiles):
                here = slice(128 * t, 128 * (t + 1))
                value = k_ref[at, here] * (scale * lanes[:, here])
                p_ref[at, here] = value.astype(BF16)
                summed += value
            sums[at, :] = summed
            return 0

        lax.fori_loop(0, ROW_BLOCK // 16, body, 0, unroll=2)

    @pl.when(step < 2)
    def _():
        block(pa_ref)

    @pl.when(step >= 2)
    def _():
        block(pb_ref)

    per = ROW_BLOCK // 128
    for a in range(per):
        piece = sums[128 * a : 128 * (a + 1), :].T
        sums_ref[pl.ds(step * per + a, 1), :] = jnp.sum(piece, axis=0, keepdims=True)


def coupling(parts, noise_scale, noise_first, noise_sq, data_first, data_sq, k):
    half = jax.ShapeDtypeStruct((HALF, COLS), BF16)
    return pass_call(
        coupling_kernel,
        (parts, noise_scale, noise_first, noise_sq, data_first, data_sq, k),
        [FROM_ROW, NOISE, NOISE, NOISE, DATA, vmem((8, 2, 128)), BLOCK],
        [half, half, NOISE_SHAPE, NOISE_SHAPE, DATA_SHAPE],
        [
            vmem((ROW_BLOCK, COLS), lambda i: (jnp.minimum(i, 1), 0)),
            vmem((ROW_BLOCK, COLS), lambda i: (jnp.maximum(i - 2, 0), 0)),
            NOISE,
            NOISE,
            DATA,
        ],
        [
            pltpu.VMEM((ROWS, 128), F32),
            pltpu.VMEM((16, COLS), F32),
            pltpu.VMEM((ROW_BLOCK, 128), F32),
        ],
        "coupling",
    )


EXTRA = 16


def split(value):
    high = value.astype(BF16)
    return high, (value - high.astype(F32)).astype(BF16)


def row_sum_rows(sums):
    high, low = split(sums)
    return jnp.concatenate([high, low, high, low], axis=0)


def target_kernel(side, ways, info_ref, p_ref, sums_ref, *refs):
    chunks = 2 - side
    data_refs, out_refs = refs[:chunks], refs[chunks:]
    step = pl.program_id(0)
    if side == 0:
        way = ways[0] if len(ways) == 1 else jnp.where(step < 2, ways[0], ways[1])
        lanes = pl.ds(pl.multiple_of(lax.rem(info_ref[19] + way, 2) * 128, 128), 128)
        data = jnp.concatenate([ref[0, :, lanes] for ref in data_refs], axis=1)
    else:
        data = data_refs[0][0]
    summed = jnp.dot(p_ref[...], data, preferred_element_type=F32).astype(BF16)
    tail = row_sum_rows(sums_ref[4 * side : 4 * side + 4, :])
    if ways == (2,):
        for half, out_ref in enumerate(out_refs):
            for b in range(2):
                out_ref[b, : HALF // 2, :] = summed[HALF // 2 * half : HALF // 2 * (half + 1), 128 * b : 128 * (b + 1)]
                out_ref[b, HALF // 2 :, :] = tail
    else:
        for n, out_ref in enumerate(out_refs):

            @pl.when(step // 2 == n)
            def _(out_ref=out_ref):
                for b in range(2):
                    out_ref[b, :HALF, :] = summed[:, 128 * b : 128 * (b + 1)]
                    out_ref[b, HALF:, :] = tail


def messages(side, ways, info, p, sums, data):
    def place(g, f):
        way = ways[0] if len(ways) == 1 else jnp.where(g < 2, ways[0], ways[1])
        return lax.rem(f[19 - side] + way, 4)

    if side == 0:
        chunks = [
            vmem((1, COLS, 256), lambda g, f, b=b: (4 * lax.rem(g, 2) + 2 * b + place(g, f) // 2, 0, 0)) for b in (0, 1)
        ]
    else:
        chunks = [vmem((1, COLS, 256), lambda g, f: (2 * place(g, f) + lax.rem(g, 2), 0, 0))]
    if ways == (2,):
        outs = [vmem((2, HALF // 2 + EXTRA, 128), lambda g, f: (g, 0, 0))] * 2
        shapes = [jax.ShapeDtypeStruct((4, HALF // 2 + EXTRA, 128), BF16)] * 2
    else:
        outs = [
            vmem((2, HALF + EXTRA, 128), lambda g, f, n=n: (jnp.clip(g - 2 * n, 0, 1), 0, 0)) for n in range(len(ways))
        ]
        shapes = [jax.ShapeDtypeStruct((4, HALF + EXTRA, 128), BF16)] * len(ways)
    return pl.pallas_call(
        functools.partial(target_kernel, side, ways),
        grid_spec=pltpu.PrefetchScalarGridSpec(
            num_scalar_prefetch=1,
            grid=(2 * len(ways),),
            in_specs=[vmem((HALF, COLS)), NOISE] + chunks,
            out_specs=outs,
        ),
        out_shape=shapes,
        compiler_params=params(24),
        cost_estimate=pl.CostEstimate(
            flops=ROWS * COLS * WIDTH // 4 * len(ways), bytes_accessed=4 * MIB, transcendentals=0
        ),
        name="targets",
    )(info, p, sums, *[data] * len(chunks))


def forward_kernel(next_ref, last_ref, from_left, from_right, out_next, out_last):
    half = HALF // 2
    low, high, rest = slice(0, half), slice(half, HALF), slice(HALF, HALF + EXTRA)
    for b in range(4):
        out_next[b, low, :] = (next_ref[b, low, :].astype(F32) + from_left[b, low, :].astype(F32)).astype(BF16)
        out_next[b, high, :] = next_ref[b, high, :]
        out_last[b, low, :] = last_ref[b, low, :]
        out_last[b, high, :] = (last_ref[b, high, :].astype(F32) + from_right[b, low, :].astype(F32)).astype(BF16)
        out_next[b, rest, :] = row_sum_rows(row_sums_of(next_ref, 0, HALF) + row_sums_of(from_left, 0, half))
        out_last[b, rest, :] = last_ref[b, rest, :]


def forward(following, preceding, from_left, from_right):
    return pl.pallas_call(
        forward_kernel,
        out_shape=[jax.ShapeDtypeStruct((4, HALF + EXTRA, 128), BF16)] * 2,
        compiler_params=pltpu.CompilerParams(vmem_limit_bytes=16 * MIB),
        cost_estimate=pl.CostEstimate(flops=1 << 20, bytes_accessed=3 * MIB, transcendentals=0),
        name="forward",
    )(following, preceding, from_left, from_right)


def row_sums_of(ref, index=None, start=HALF):
    at = [slice(start + 4 * i, start + 4 * i + 4) for i in (0, 1)]
    high, low = (ref[i, :] if index is None else ref[index, i, :] for i in at)
    return high.astype(F32) + low.astype(F32)


def combine_kernel(side, info_ref, own, left, right, keep_ref, s1, s2, s3):
    place = info_ref[18 + side]
    sums = row_sums_of(own, 0) + (row_sums_of(left, 0) + row_sums_of(right, 0))
    tail = row_sum_rows(sums)

    def summed(index):
        at = slice(0, HALF)
        return own[index, at, :].astype(F32) + (left[index, at, :].astype(F32) + right[index, at, :].astype(F32))

    for d, out_ref in ((1, s1), (2, s2), (3, s3)):
        out_ref[:HALF, :] = summed(lax.rem(place + d, 4)).astype(BF16)
        out_ref[HALF:, :] = tail
    keep_ref[:HALF, :] = summed(place)
    keep_ref[HALF:, :] = jnp.concatenate([sums, jnp.zeros((EXTRA - 4, 128), F32)], axis=0)


def combine(side, info, parts):
    return pl.pallas_call(
        functools.partial(combine_kernel, side),
        in_specs=[pl.BlockSpec(memory_space=pltpu.SMEM)] + [pl.BlockSpec(memory_space=pltpu.VMEM)] * 3,
        out_shape=[jax.ShapeDtypeStruct((HALF + EXTRA, 128), F32)] + [jax.ShapeDtypeStruct((HALF + EXTRA, 128), BF16)] * 3,
        compiler_params=pltpu.CompilerParams(vmem_limit_bytes=16 * MIB),
        cost_estimate=pl.CostEstimate(flops=1 << 20, bytes_accessed=3 * MIB, transcendentals=0),
        name="combine",
    )(info, *parts)


def finish_kernel(noise_ref, *refs):
    out_ref = refs[-1]
    for half in range(2):
        own, *others = refs[4 * half : 4 * half + 4]
        sums = own[HALF : HALF + 4, :]
        for other in others:
            sums += row_sums_of(other)
        for a, inverse in enumerate(to_column(1.0 / sums)):
            here = slice(128 * a, 128 * (a + 1))
            at = slice(HALF * half + 128 * a, HALF * half + 128 * (a + 1))
            summed = own[here, :]
            for other in others:
                summed += other[here, :].astype(F32)
            out_ref[at, :] = summed * inverse - noise_ref[at, :].astype(F32)


def finish(noise, parts):
    return pl.pallas_call(
        finish_kernel,
        out_shape=jax.ShapeDtypeStruct((ROWS, 128), F32),
        compiler_params=pltpu.CompilerParams(vmem_limit_bytes=16 * MIB),
        name="finish",
    )(noise, *parts)


def swap(x, axis):
    return lax.all_to_all(x, axis, 0, 0, tiled=True)


def per_device(noise_latents, data_latents, noise_sizes, data_sizes):
    row, col = lax.axis_index("row"), lax.axis_index("col")
    places = jnp.stack([row * ROWS, col * COLS, col // 4, col % 4]).astype(jnp.int32)
    info = jnp.concatenate([noise_sizes, data_sizes, places])
    data = lax.all_gather(data_latents, "row")
    noise, noise_sq = arrange(info, gather_noise(noise_latents))
    score, lse, data_sq = scores(info, noise, data)
    lse, noise_first = first_columns(swap(lse, "col"), score)
    k, sums, data_first = kernel_matrix(swap(lse, "row"), noise_first, score)
    sums, _ = column_sums(swap(sums, "col"), k)
    sums = row_sums(swap(sums, "row"), k)
    sums, noise_scale = column_sums(swap(sums, "col"), k)
    *p, sums, noise_potential, data_potential = coupling(
        swap(sums, "row"), noise_scale, noise_first, noise_sq, data_first, data_sq, k
    )
    way = (over_x, over_z)
    moved = []
    for side in (0, 1):
        to_right, to_left = messages(side, (2,), info, p[side], sums, data)
        moved.append((way[side](to_right, 1), way[side](to_left, 3)))
        sums, _, _ = lax.optimization_barrier((sums, to_right, to_left))
    made = []
    for side in (0, 1):
        made.append(messages(side, (1, 3), info, p[side], sums, data))
        sums, _ = lax.optimization_barrier((sums, made[side]))
    got = []
    for side in (0, 1):
        following, preceding = forward(*made[side], *moved[side])
        got.append((way[side](following, 1), way[side](preceding, 3)))
        sums, _ = lax.optimization_barrier((sums, following))
    ends = []
    for side in (0, 1):
        own = messages(side, (0,), info, p[side], sums, data)[0]
        sums, _ = lax.optimization_barrier((sums, own))
        keep, *others = combine(side, info, (own, *got[side]))
        ends += [keep] + [way[1 - side](v, d) for d, v in zip((1, 2, 3), others)]
    velocity = finish(noise_latents, ends)
    return velocity, noise_potential.reshape(ROWS), data_potential.reshape(COLS)


def solution(mesh):
    placed = (P("row", "col"), P("col", "row"), P(), P())
    return jax.shard_map(
        per_device,
        mesh=mesh,
        in_specs=placed,
        out_specs=(P("row", "col"), P("row"), P("col")),
        check_vma=False,
    )
```

```python
import functools

import jax
import jax.numpy as jnp
from jax import lax
from jax.experimental import pallas as pl
from jax.experimental.pallas import tpu as pltpu
from jax.sharding import PartitionSpec as P

EPS = 0.05
LOG2E = 1.4426950408889634
LN2 = 0.6931471805599453
MASKED = -1e30
CLUSTERS = 8
F32 = jnp.float32
BF16 = jnp.bfloat16
MIB = 1 << 20

ROWS = 1024
COLS = 2048
WIDTH = 2048
COL_BLOCK = 512
SCORE_ROWS = 512
ROW_BLOCK = 256
HALF = 512
N_ROW = 8
N_COL = 16
KAPPA = LOG2E / (WIDTH * EPS)


def vmem(shape, index_map=None):
    if index_map is None:
        return pl.BlockSpec(shape, lambda *_: (0,) * len(shape))
    return pl.BlockSpec(shape, index_map)


def params(mib):
    return pltpu.CompilerParams(vmem_limit_bytes=mib * MIB, dimension_semantics=("arbitrary",))


def lane_totals(pieces):
    return [piece.T for piece in pieces]


def to_column(rows):
    n = rows.shape[0]
    return [jnp.broadcast_to(rows[a : a + 1, :], (128, 128)).T for a in range(n)]


def to_lanes(rows):
    return jnp.concatenate([rows[a : a + 1, :] for a in range(rows.shape[0])], axis=1)


def from_lanes(row):
    return jnp.concatenate([row[:, 128 * a : 128 * (a + 1)] for a in range(row.shape[1] // 128)], axis=0)


def arrange_kernel(info_ref, *refs):
    out_ref, noise_sq_ref = refs[10:]
    z, x = info_ref[18], info_ref[19]
    sums = []
    for half in range(2):
        own, before, after, second_a, second_b = refs[5 * half : 5 * half + 5]
        at = slice(HALF * half, HALF * (half + 1))
        squares = jnp.zeros((HALF, 128), F32)
        for far, source in ((0, own), (1, before), (3, after), (2, None)):
            for near in range(4):
                if source is not None:
                    piece = source[near]
                else:
                    piece = second_a[near] if near < 2 else second_b[near - 2]
                if half == 0:
                    index = lax.rem(z + 4 - far, 4) * 4 + lax.rem(x + 4 - near, 4)
                else:
                    index = lax.rem(z + 4 - near, 4) * 4 + lax.rem(x + 4 - far, 4)
                out_ref[at, pl.ds(pl.multiple_of(index * 128, 128), 128)] = piece
                squares += piece.astype(F32) * piece.astype(F32)
        for a in range(HALF // 128):
            sums.append(jnp.sum(squares[128 * a : 128 * (a + 1), :].T, axis=0, keepdims=True))
    noise_sq_ref[...] = jnp.concatenate(sums, axis=0)


def arrange(info, pieces):
    return pl.pallas_call(
        arrange_kernel,
        in_specs=[pl.BlockSpec(memory_space=pltpu.SMEM)] + [pl.BlockSpec(memory_space=pltpu.VMEM)] * 10,
        out_shape=[jax.ShapeDtypeStruct((ROWS, WIDTH), BF16), NOISE_SHAPE],
        compiler_params=pltpu.CompilerParams(vmem_limit_bytes=24 * MIB),
        cost_estimate=pl.CostEstimate(flops=4 << 20, bytes_accessed=8 * MIB, transcendentals=0),
        name="arrange",
    )(info, *pieces)


def over_x(v, d):
    return lax.ppermute(v, "col", [(4 * z + x, 4 * z + (x + d) % 4) for z in range(4) for x in range(4)])


def over_z(v, d):
    return lax.ppermute(v, "col", [(4 * z + x, 4 * ((z + d) % 4) + x) for z in range(4) for x in range(4)])


def gather_noise(noise):
    gathered = []
    for half, (first, second) in enumerate(((over_x, over_z), (over_z, over_x))):
        own = noise[HALF * half : HALF * (half + 1)]
        own = jnp.stack([own] + [first(own, d) for d in (1, 2, 3)])
        gathered.append((own, second(own, 1), second(own, 3), second))
    pieces = []
    for own, before, after, second in gathered:
        pieces += [own, before, after, second(before[:2], 1), second(after[2:], 3)]
    return pieces


def score_kernel(info_ref, noise_ref, data_ref, score_ref, lse_ref, data_sq_ref, big, total):
    step = pl.program_id(0)

    @pl.when(step == 0)
    def _():
        big[...] = jnp.full(big.shape, MASKED, F32)
        total[...] = jnp.zeros(total.shape, F32)

    data = jnp.concatenate([data_ref[k] for k in range(N_ROW)], axis=1)
    data_sq = []
    for a in range(COL_BLOCK // 128):
        squares = jnp.zeros((128, 128), F32)
        for k in range(WIDTH // 128):
            piece = data[128 * a : 128 * (a + 1), 128 * k : 128 * (k + 1)].astype(F32)
            squares += piece * piece
        data_sq.append(jnp.sum(squares.T, axis=0, keepdims=True))
        data_sq_ref[0, a : a + 1, :] = data_sq[a]

    j = info_ref[17] + step * COL_BLOCK + lax.broadcasted_iota(jnp.int32, (1, COL_BLOCK), 1)
    low = jnp.zeros((1, COL_BLOCK), jnp.int32)
    high = jnp.zeros((1, COL_BLOCK), jnp.int32)
    noise_at = jnp.int32(0)
    data_at = jnp.int32(0)
    for c in range(CLUSTERS):
        noise_end = noise_at + info_ref[c]
        data_end = data_at + info_ref[8 + c]
        if c == CLUSTERS - 1:
            inside = j >= data_at
        else:
            inside = (j >= data_at) & (j < data_end)
        low = jnp.where(inside, noise_at, low)
        high = jnp.where(inside, noise_end, high)
        noise_at, data_at = noise_end, data_end
    low = low - info_ref[16]
    high = high - info_ref[16]

    half = SCORE_ROWS
    for r in range(ROWS // half):
        inner = lax.dot_general(noise_ref[half * r : half * (r + 1), :], data, (((1,), (1,)), ((), ())), preferred_element_type=F32)
        i = half * r + lax.broadcasted_iota(jnp.int32, (half, COL_BLOCK), 0)
        score = jnp.where((i >= low) & (i < high), inner * (2.0 * KAPPA), MASKED)
        score_ref[half * r : half * (r + 1), :] = score
        parts = [score[:, 128 * t : 128 * (t + 1)] - KAPPA * data_sq[t] for t in range(COL_BLOCK // 128)]
        at = slice(half * r, half * (r + 1))
        old = big[at, :]
        new = functools.reduce(jnp.maximum, parts, old)
        total[at, :] = total[at, :] * jnp.exp2(old - new) + functools.reduce(
            jnp.add, [jnp.exp2(part - new) for part in parts]
        )
        big[at, :] = new

    @pl.when(step == pl.num_programs(0) - 1)
    def _():
        rows = []
        for a in range(ROWS // 128):
            at = slice(128 * a, 128 * (a + 1))
            m = big[at, :].T
            s = total[at, :].T
            largest = jnp.max(m, axis=0, keepdims=True)
            summed = jnp.sum(s * jnp.exp2(m - largest), axis=0, keepdims=True)
            rows.append(largest + jnp.log2(summed))
        lse_ref[...] = jnp.broadcast_to(jnp.concatenate(rows, axis=0)[None], lse_ref.shape)


def scores(info, noise, data):
    return pl.pallas_call(
        score_kernel,
        grid=(COLS // COL_BLOCK,),
        in_specs=[
            pl.BlockSpec(memory_space=pltpu.SMEM),
            vmem((ROWS, WIDTH)),
            vmem((N_ROW, COL_BLOCK, 256), lambda j: (0, j, 0)),
        ],
        out_specs=[
            vmem((ROWS, COL_BLOCK), lambda j: (0, j)),
            vmem((N_COL, 8, 128)),
            vmem((1, COL_BLOCK // 128, 128), lambda j: (j, 0, 0)),
        ],
        out_shape=[
            jax.ShapeDtypeStruct((ROWS, COLS), F32),
            jax.ShapeDtypeStruct((N_COL, 8, 128), F32),
            jax.ShapeDtypeStruct((COLS // COL_BLOCK, COL_BLOCK // 128, 128), F32),
        ],
        scratch_shapes=[pltpu.VMEM((ROWS, 128), F32), pltpu.VMEM((ROWS, 128), F32)],
        compiler_params=params(40),
        cost_estimate=pl.CostEstimate(flops=2 * ROWS * COLS * WIDTH, bytes_accessed=20 * MIB, transcendentals=3 << 20),
        name="scores",
    )(info, noise, data)


def merge_lse(parts_ref):
    parts = parts_ref[...]
    largest = jnp.max(parts, axis=0)
    return -(largest + jnp.log2(jnp.sum(jnp.exp2(parts - largest[None]), axis=0)))


def merge_scale(parts_ref):
    return 1.0 / jnp.sum(parts_ref[...], axis=0)


GROUP = 8


def first_columns_kernel(parts_ref, score_ref, lse_ref, noise_ref, column, big, total):
    step = pl.program_id(0)

    @pl.when(step == 0)
    def _():
        potential = merge_lse(parts_ref)
        noise_ref[...] = potential
        for a, piece in enumerate(to_column(potential)):
            column[128 * a : 128 * (a + 1), :] = piece
        big[...] = jnp.full(big.shape, MASKED, F32)
        total[...] = jnp.zeros(total.shape, F32)

    base = step * ROW_BLOCK
    tiles = COLS // 128

    def largest(g, carry):
        shift = column[pl.ds(pl.multiple_of(base + g * GROUP, GROUP), GROUP), :]
        at = pl.ds(pl.multiple_of(g * GROUP, GROUP), GROUP)
        return tuple(jnp.maximum(carry[t], score_ref[at, 128 * t : 128 * (t + 1)] + shift) for t in range(tiles))

    old = tuple(big[:, 128 * t : 128 * (t + 1)] for t in range(tiles))
    new = lax.fori_loop(0, ROW_BLOCK // GROUP, largest, old, unroll=2)

    def add(g, carry):
        shift = column[pl.ds(pl.multiple_of(base + g * GROUP, GROUP), GROUP), :]
        at = pl.ds(pl.multiple_of(g * GROUP, GROUP), GROUP)
        return tuple(
            carry[t] + jnp.exp2(score_ref[at, 128 * t : 128 * (t + 1)] + (shift - new[t])) for t in range(tiles)
        )

    start = tuple(total[:, 128 * t : 128 * (t + 1)] * jnp.exp2(old[t] - new[t]) for t in range(tiles))
    summed = lax.fori_loop(0, ROW_BLOCK // GROUP, add, start, unroll=2)
    for t in range(tiles):
        big[:, 128 * t : 128 * (t + 1)] = new[t]
        total[:, 128 * t : 128 * (t + 1)] = summed[t]

    @pl.when(step == pl.num_programs(0) - 1)
    def _():
        m = jnp.max(big[...], axis=0, keepdims=True)
        s = jnp.sum(total[...] * jnp.exp2(big[...] - m), axis=0, keepdims=True)
        lse_ref[...] = jnp.broadcast_to(from_lanes(m + jnp.log2(s))[None], lse_ref.shape)


def pass_call(kernel, inputs, in_specs, outs, out_specs, scratch, name, transcendentals=0):
    return pl.pallas_call(
        kernel,
        grid=(ROWS // ROW_BLOCK,),
        in_specs=in_specs,
        out_specs=out_specs,
        out_shape=outs,
        scratch_shapes=scratch,
        compiler_params=params(24),
        cost_estimate=pl.CostEstimate(flops=4 * ROWS * COLS, bytes_accessed=8 * MIB, transcendentals=transcendentals),
        name=name,
    )(*inputs)


FROM_COL = vmem((N_COL, 8, 128))
FROM_ROW = vmem((N_ROW, 16, 128))
NOISE = vmem((8, 128))
DATA = vmem((16, 128))
BLOCK = vmem((ROW_BLOCK, COLS), lambda i: (i, 0))
FROM_COL_SHAPE = jax.ShapeDtypeStruct((N_COL, 8, 128), F32)
FROM_ROW_SHAPE = jax.ShapeDtypeStruct((N_ROW, 16, 128), F32)
NOISE_SHAPE = jax.ShapeDtypeStruct((8, 128), F32)
DATA_SHAPE = jax.ShapeDtypeStruct((16, 128), F32)
BLOCK_SHAPE = jax.ShapeDtypeStruct((ROWS, COLS), F32)


def first_columns(parts, score):
    return pass_call(
        first_columns_kernel,
        (parts, score),
        [FROM_COL, BLOCK],
        [FROM_ROW_SHAPE, NOISE_SHAPE],
        [FROM_ROW, NOISE],
        [pltpu.VMEM((ROWS, 128), F32), pltpu.VMEM((8, COLS), F32), pltpu.VMEM((8, COLS), F32)],
        "first_columns",
        ROWS * COLS,
    )


def write_row_sums(sums, out_ref, rows, step):
    per = ROW_BLOCK // 128
    for a in range(per):
        piece = sums[128 * a : 128 * (a + 1), :].T
        rows[pl.ds(step * per + a, 1), :] = jnp.sum(piece, axis=0, keepdims=True)

    @pl.when(step == pl.num_programs(0) - 1)
    def _():
        out_ref[...] = jnp.broadcast_to(rows[...][None], out_ref.shape)


def kernel_matrix_kernel(parts_ref, noise_ref, score_ref, k_ref, sums_ref, data_ref, column, lanes, sums, rows):
    step = pl.program_id(0)

    @pl.when(step == 0)
    def _():
        potential = merge_lse(parts_ref)
        data_ref[...] = potential
        lanes[...] = jnp.broadcast_to(to_lanes(potential), lanes.shape)
        for a, piece in enumerate(to_column(noise_ref[...])):
            column[128 * a : 128 * (a + 1), :] = piece

    base = step * ROW_BLOCK
    tiles = COLS // 128
    shifts = [lanes[:, 128 * t : 128 * (t + 1)] for t in range(tiles)]

    def body(g, _):
        shift = column[pl.ds(pl.multiple_of(base + g * GROUP, GROUP), GROUP), :]
        at = pl.ds(pl.multiple_of(g * GROUP, GROUP), GROUP)
        summed = jnp.zeros((GROUP, 128), F32)
        for t in range(tiles):
            here = slice(128 * t, 128 * (t + 1))
            value = jnp.exp2(score_ref[at, here] + shift + shifts[t])
            k_ref[at, here] = value
            summed += value
        sums[at, :] = summed
        return 0

    lax.fori_loop(0, ROW_BLOCK // GROUP, body, 0, unroll=2)
    write_row_sums(sums, sums_ref, rows, step)


def kernel_matrix(parts, noise_potential, score):
    return pass_call(
        kernel_matrix_kernel,
        (parts, noise_potential, score),
        [FROM_ROW, NOISE, BLOCK],
        [BLOCK_SHAPE, FROM_COL_SHAPE, DATA_SHAPE],
        [BLOCK, FROM_COL, DATA],
        [
            pltpu.VMEM((ROWS, 128), F32),
            pltpu.VMEM((GROUP, COLS), F32),
            pltpu.VMEM((ROW_BLOCK, 128), F32),
            pltpu.VMEM((8, 128), F32),
        ],
        "kernel_matrix",
        ROWS * COLS,
    )


def column_sums_kernel(parts_ref, k_ref, sums_ref, scale_ref, column, total):
    step = pl.program_id(0)

    @pl.when(step == 0)
    def _():
        scale = merge_scale(parts_ref)
        scale_ref[...] = scale
        for a, piece in enumerate(to_column(scale)):
            column[128 * a : 128 * (a + 1), :] = piece
        total[...] = jnp.zeros(total.shape, F32)

    base = step * ROW_BLOCK
    tiles = COLS // 128

    def add(g, carry):
        scale = column[pl.ds(pl.multiple_of(base + g * GROUP, GROUP), GROUP), :]
        at = pl.ds(pl.multiple_of(g * GROUP, GROUP), GROUP)
        return tuple(carry[t] + k_ref[at, 128 * t : 128 * (t + 1)] * scale for t in range(tiles))

    start = tuple(total[:, 128 * t : 128 * (t + 1)] for t in range(tiles))
    summed = lax.fori_loop(0, ROW_BLOCK // GROUP, add, start, unroll=4)
    for t in range(tiles):
        total[:, 128 * t : 128 * (t + 1)] = summed[t]

    @pl.when(step == pl.num_programs(0) - 1)
    def _():
        s = jnp.sum(total[...], axis=0, keepdims=True)
        sums_ref[...] = jnp.broadcast_to(from_lanes(s)[None], sums_ref.shape)


def column_sums(parts, k):
    return pass_call(
        column_sums_kernel,
        (parts, k),
        [FROM_COL, BLOCK],
        [FROM_ROW_SHAPE, NOISE_SHAPE],
        [FROM_ROW, NOISE],
        [pltpu.VMEM((ROWS, 128), F32), pltpu.VMEM((GROUP, COLS), F32)],
        "column_sums",
    )


def row_sums_kernel(parts_ref, k_ref, sums_ref, lanes, sums, rows):
    step = pl.program_id(0)

    @pl.when(step == 0)
    def _():
        lanes[...] = jnp.broadcast_to(to_lanes(merge_scale(parts_ref)), lanes.shape)

    tiles = COLS // 128
    scales = [lanes[:, 128 * t : 128 * (t + 1)] for t in range(tiles)]

    def body(g, _):
        at = pl.ds(pl.multiple_of(g * GROUP, GROUP), GROUP)
        summed = [k_ref[at, 128 * t : 128 * (t + 1)] * scales[t] for t in range(4)]
        for t in range(4, tiles):
            summed[t % 4] += k_ref[at, 128 * t : 128 * (t + 1)] * scales[t]
        sums[at, :] = (summed[0] + summed[1]) + (summed[2] + summed[3])
        return 0

    lax.fori_loop(0, ROW_BLOCK // GROUP, body, 0, unroll=4)
    write_row_sums(sums, sums_ref, rows, step)


def row_sums(parts, k):
    return pass_call(
        row_sums_kernel,
        (parts, k),
        [FROM_ROW, BLOCK],
        [FROM_COL_SHAPE],
        [FROM_COL],
        [pltpu.VMEM((GROUP, COLS), F32), pltpu.VMEM((ROW_BLOCK, 128), F32), pltpu.VMEM((8, 128), F32)],
        "row_sums",
    )[0]


def coupling_kernel(
    parts_ref, scale_ref, noise_first, noise_sq, data_first, data_sq, k_ref,
    pa_ref, pb_ref, sums_ref, noise_ref, data_ref, column, lanes, sums,
):
    step = pl.program_id(0)

    @pl.when(step == 0)
    def _():
        scale = merge_scale(parts_ref)
        lanes[...] = jnp.broadcast_to(to_lanes(scale), lanes.shape)
        for a, piece in enumerate(to_column(scale_ref[...])):
            column[128 * a : 128 * (a + 1), :] = piece
        noise_ref[...] = (EPS * LN2) * (noise_first[...] + jnp.log2(scale_ref[...])) + noise_sq[...] * (1.0 / WIDTH)
        potential = (EPS * LN2) * (data_first[...] + jnp.log2(scale))
        per = COL_BLOCK // 128
        for k in range(COLS // COL_BLOCK):
            at = slice(per * k, per * (k + 1))
            data_ref[at, :] = potential[at, :] + data_sq[k] * (1.0 / WIDTH)

    base = step * ROW_BLOCK
    tiles = COLS // 128

    def block(p_ref):
        def body(g, _):
            at = pl.ds(pl.multiple_of(g * 16, 16), 16)
            scale = column[pl.ds(pl.multiple_of(base + g * 16, 16), 16), :]
            summed = jnp.zeros((16, 128), F32)
            for t in range(tiles):
                here = slice(128 * t, 128 * (t + 1))
                value = (k_ref[at, here] * (scale * lanes[:, here])).astype(BF16)
                p_ref[at, here] = value
                summed += value.astype(F32)
            sums[at, :] = summed
            return 0

        lax.fori_loop(0, ROW_BLOCK // 16, body, 0, unroll=2)

    @pl.when(step < 2)
    def _():
        block(pa_ref)

    @pl.when(step >= 2)
    def _():
        block(pb_ref)

    per = ROW_BLOCK // 128
    for a in range(per):
        piece = sums[128 * a : 128 * (a + 1), :].T
        sums_ref[pl.ds(step * per + a, 1), :] = jnp.sum(piece, axis=0, keepdims=True)


def coupling(parts, noise_scale, noise_first, noise_sq, data_first, data_sq, k):
    half = jax.ShapeDtypeStruct((HALF, COLS), BF16)
    return pass_call(
        coupling_kernel,
        (parts, noise_scale, noise_first, noise_sq, data_first, data_sq, k),
        [FROM_ROW, NOISE, NOISE, NOISE, DATA, vmem((COLS // COL_BLOCK, COL_BLOCK // 128, 128)), BLOCK],
        [half, half, NOISE_SHAPE, NOISE_SHAPE, DATA_SHAPE],
        [
            vmem((ROW_BLOCK, COLS), lambda i: (jnp.minimum(i, 1), 0)),
            vmem((ROW_BLOCK, COLS), lambda i: (jnp.maximum(i - 2, 0), 0)),
            NOISE,
            NOISE,
            DATA,
        ],
        [
            pltpu.VMEM((ROWS, 128), F32),
            pltpu.VMEM((16, COLS), F32),
            pltpu.VMEM((ROW_BLOCK, 128), F32),
        ],
        "coupling",
    )


EXTRA = 16


def split(value):
    high = value.astype(BF16)
    return high, (value - high.astype(F32)).astype(BF16)


def row_sum_rows(sums):
    high, low = split(sums)
    return jnp.concatenate([high, low, high, low], axis=0)


def target_kernel(ways, info_ref, pa_ref, pb_ref, sums_ref, data_ref, *out_refs):
    z, x = info_ref[18], info_ref[19]
    out_refs = list(out_refs)
    for side in (0, 1):
        tail = row_sum_rows(sums_ref[4 * side : 4 * side + 4, :])
        for way in ways:
            if side == 0:
                block = lax.rem(x + way, 4)
                lanes = pl.ds(pl.multiple_of(lax.rem(block, 2) * 128, 128), 128)
                data = [data_ref[2 * k + block // 2, :, lanes] for k in range(4)]
                values = pa_ref[...]
            else:
                block = lax.rem(z + way, 4)
                data = [data_ref[2 * block + k] for k in range(2)]
                values = pb_ref[...]
            summed = jnp.dot(values, jnp.concatenate(data, axis=1), preferred_element_type=F32).astype(BF16)
            parts = 2 if way == 2 else 1
            rows = HALF // parts
            for part in range(parts):
                out_ref = out_refs.pop(0)
                for b in range(4):
                    out_ref[b, :rows, :] = summed[rows * part : rows * (part + 1), 128 * b : 128 * (b + 1)]
                    out_ref[b, rows:, :] = tail


def messages(ways, info, p, sums, data):
    rows = [HALF // 2] * 2 if ways == (2,) else [HALF] * len(ways)
    made = pl.pallas_call(
        functools.partial(target_kernel, ways),
        in_specs=[pl.BlockSpec(memory_space=pltpu.SMEM)] + [pl.BlockSpec(memory_space=pltpu.VMEM)] * 4,
        out_shape=[jax.ShapeDtypeStruct((4, n + EXTRA, 128), BF16) for n in rows * 2],
        compiler_params=pltpu.CompilerParams(vmem_limit_bytes=28 * MIB),
        cost_estimate=pl.CostEstimate(
            flops=ROWS * COLS * WIDTH // 2 * len(ways), bytes_accessed=8 * MIB, transcendentals=0
        ),
        name="targets",
    )(info, *p, sums, data)
    return made[: len(rows)], made[len(rows) :]


def forward_kernel(next_ref, last_ref, from_left, from_right, out_next, out_last):
    half = HALF // 2
    low, high, rest = slice(0, half), slice(half, HALF), slice(HALF, HALF + EXTRA)
    for b in range(4):
        out_next[b, low, :] = (next_ref[b, low, :].astype(F32) + from_left[b, low, :].astype(F32)).astype(BF16)
        out_next[b, high, :] = next_ref[b, high, :]
        out_last[b, low, :] = last_ref[b, low, :]
        out_last[b, high, :] = (last_ref[b, high, :].astype(F32) + from_right[b, low, :].astype(F32)).astype(BF16)
        out_next[b, rest, :] = row_sum_rows(row_sums_of(next_ref, 0, HALF) + row_sums_of(from_left, 0, half))
        out_last[b, rest, :] = last_ref[b, rest, :]


def forward(following, preceding, from_left, from_right):
    return pl.pallas_call(
        forward_kernel,
        out_shape=[jax.ShapeDtypeStruct((4, HALF + EXTRA, 128), BF16)] * 2,
        compiler_params=pltpu.CompilerParams(vmem_limit_bytes=16 * MIB),
        cost_estimate=pl.CostEstimate(flops=1 << 20, bytes_accessed=3 * MIB, transcendentals=0),
        name="forward",
    )(following, preceding, from_left, from_right)


def row_sums_of(ref, index=None, start=HALF):
    at = [slice(start + 4 * i, start + 4 * i + 4) for i in (0, 1)]
    high, low = (ref[i, :] if index is None else ref[index, i, :] for i in at)
    return high.astype(F32) + low.astype(F32)


def combine_kernel(side, info_ref, own, left, right, keep_ref, s1, s2, s3):
    place = info_ref[18 + side]
    sums = row_sums_of(own, 0) + (row_sums_of(left, 0) + row_sums_of(right, 0))
    tail = row_sum_rows(sums)

    def summed(index):
        at = slice(0, HALF)
        return own[index, at, :].astype(F32) + (left[index, at, :].astype(F32) + right[index, at, :].astype(F32))

    for d, out_ref in ((1, s1), (2, s2), (3, s3)):
        out_ref[:HALF, :] = summed(lax.rem(place + d, 4)).astype(BF16)
        out_ref[HALF:, :] = tail
    keep_ref[:HALF, :] = summed(place)
    keep_ref[HALF:, :] = jnp.concatenate([sums, jnp.zeros((EXTRA - 4, 128), F32)], axis=0)


def combine(side, info, parts):
    return pl.pallas_call(
        functools.partial(combine_kernel, side),
        in_specs=[pl.BlockSpec(memory_space=pltpu.SMEM)] + [pl.BlockSpec(memory_space=pltpu.VMEM)] * 3,
        out_shape=[jax.ShapeDtypeStruct((HALF + EXTRA, 128), F32)] + [jax.ShapeDtypeStruct((HALF + EXTRA, 128), BF16)] * 3,
        compiler_params=pltpu.CompilerParams(vmem_limit_bytes=16 * MIB),
        cost_estimate=pl.CostEstimate(flops=1 << 20, bytes_accessed=3 * MIB, transcendentals=0),
        name="combine",
    )(info, *parts)


def finish_kernel(noise_ref, *refs):
    out_ref = refs[-1]
    for half in range(2):
        own, *others = refs[4 * half : 4 * half + 4]
        sums = own[HALF : HALF + 4, :]
        for other in others:
            sums += row_sums_of(other)
        for a, inverse in enumerate(to_column(1.0 / sums)):
            here = slice(128 * a, 128 * (a + 1))
            at = slice(HALF * half + 128 * a, HALF * half + 128 * (a + 1))
            summed = own[here, :]
            for other in others:
                summed += other[here, :].astype(F32)
            out_ref[at, :] = summed * inverse - noise_ref[at, :].astype(F32)


def finish(noise, parts):
    return pl.pallas_call(
        finish_kernel,
        out_shape=jax.ShapeDtypeStruct((ROWS, 128), F32),
        compiler_params=pltpu.CompilerParams(vmem_limit_bytes=16 * MIB),
        name="finish",
    )(noise, *parts)


def swap(x, axis):
    return lax.all_to_all(x, axis, 0, 0, tiled=True)


def per_device(noise_latents, data_latents, noise_sizes, data_sizes):
    row, col = lax.axis_index("row"), lax.axis_index("col")
    places = jnp.stack([row * ROWS, col * COLS, col // 4, col % 4]).astype(jnp.int32)
    info = jnp.concatenate([noise_sizes, data_sizes, places])
    data = lax.all_gather(data_latents, "row")
    noise, noise_sq = arrange(info, gather_noise(noise_latents))
    score, lse, data_sq = scores(info, noise, data)
    lse, noise_first = first_columns(swap(lse, "col"), score)
    k, sums, data_first = kernel_matrix(swap(lse, "row"), noise_first, score)
    sums, _ = column_sums(swap(sums, "col"), k)
    sums = row_sums(swap(sums, "row"), k)
    sums, noise_scale = column_sums(swap(sums, "col"), k)
    *p, sums, noise_potential, data_potential = coupling(
        swap(sums, "row"), noise_scale, noise_first, noise_sq, data_first, data_sq, k
    )
    way = (over_x, over_z)
    made = messages((2,), info, p, sums, data)
    moved = [(way[side](made[side][0], 1), way[side](made[side][1], 3)) for side in (0, 1)]
    sums, _ = lax.optimization_barrier((sums, made))
    made = messages((1, 3), info, p, sums, data)
    sums, _ = lax.optimization_barrier((sums, made))
    got = []
    for side in (0, 1):
        following, preceding = forward(*made[side], *moved[side])
        got.append((way[side](following, 1), way[side](preceding, 3)))
        sums, _ = lax.optimization_barrier((sums, following))
    own = messages((0,), info, p, sums, data)
    ends = []
    for side in (0, 1):
        keep, *others = combine(side, info, (own[side][0], *got[side]))
        ends += [keep] + [way[1 - side](v, d) for d, v in zip((1, 2, 3), others)]
    velocity = finish(noise_latents, ends)
    return velocity, noise_potential.reshape(ROWS), data_potential.reshape(COLS)


def solution(mesh):
    placed = (P("row", "col"), P("col", "row"), P(), P())
    return jax.shard_map(
        per_device,
        mesh=mesh,
        in_specs=placed,
        out_specs=(P("row", "col"), P("row"), P("col")),
        check_vma=False,
    )
```

```python
import functools

import jax
import jax.numpy as jnp
from jax import lax
from jax.experimental import pallas as pl
from jax.experimental.pallas import tpu as pltpu
from jax.sharding import PartitionSpec as P

EPS = 0.05
LOG2E = 1.4426950408889634
LN2 = 0.6931471805599453
MASKED = -1e30
CLUSTERS = 8
F32 = jnp.float32
BF16 = jnp.bfloat16
MIB = 1 << 20

ROWS = 1024
COLS = 2048
WIDTH = 2048
COL_BLOCK = 512
SCORE_ROWS = 512
ROW_BLOCK = 256
HALF = 512
N_ROW = 8
N_COL = 16
KAPPA = LOG2E / (WIDTH * EPS)


def vmem(shape, index_map=None):
    if index_map is None:
        return pl.BlockSpec(shape, lambda *_: (0,) * len(shape))
    return pl.BlockSpec(shape, index_map)


def params(mib):
    return pltpu.CompilerParams(vmem_limit_bytes=mib * MIB, dimension_semantics=("arbitrary",))


def lane_totals(pieces):
    return [piece.T for piece in pieces]


def to_column(rows):
    n = rows.shape[0]
    return [jnp.broadcast_to(rows[a : a + 1, :], (128, 128)).T for a in range(n)]


def to_lanes(rows):
    return jnp.concatenate([rows[a : a + 1, :] for a in range(rows.shape[0])], axis=1)


def from_lanes(row):
    return jnp.concatenate([row[:, 128 * a : 128 * (a + 1)] for a in range(row.shape[1] // 128)], axis=0)


def arrange_kernel(info_ref, *refs):
    out_ref, noise_sq_ref = refs[10:]
    z, x = info_ref[18], info_ref[19]
    sums = []
    for half in range(2):
        own, before, after, second_a, second_b = refs[5 * half : 5 * half + 5]
        at = slice(HALF * half, HALF * (half + 1))
        squares = jnp.zeros((HALF, 128), F32)
        for far, source in ((0, own), (1, before), (3, after), (2, None)):
            for near in range(4):
                if source is not None:
                    piece = source[near]
                else:
                    piece = second_a[near] if near < 2 else second_b[near - 2]
                if half == 0:
                    index = lax.rem(z + 4 - far, 4) * 4 + lax.rem(x + 4 - near, 4)
                else:
                    index = lax.rem(z + 4 - near, 4) * 4 + lax.rem(x + 4 - far, 4)
                out_ref[at, pl.ds(pl.multiple_of(index * 128, 128), 128)] = piece
                squares += piece.astype(F32) * piece.astype(F32)
        for a in range(HALF // 128):
            sums.append(jnp.sum(squares[128 * a : 128 * (a + 1), :].T, axis=0, keepdims=True))
    noise_sq_ref[...] = jnp.concatenate(sums, axis=0)


def arrange(info, pieces):
    return pl.pallas_call(
        arrange_kernel,
        in_specs=[pl.BlockSpec(memory_space=pltpu.SMEM)] + [pl.BlockSpec(memory_space=pltpu.VMEM)] * 10,
        out_shape=[jax.ShapeDtypeStruct((ROWS, WIDTH), BF16), NOISE_SHAPE],
        compiler_params=pltpu.CompilerParams(vmem_limit_bytes=24 * MIB),
        cost_estimate=pl.CostEstimate(flops=4 << 20, bytes_accessed=8 * MIB, transcendentals=0),
        name="arrange",
    )(info, *pieces)


def over_x(v, d):
    return lax.ppermute(v, "col", [(4 * z + x, 4 * z + (x + d) % 4) for z in range(4) for x in range(4)])


def over_z(v, d):
    return lax.ppermute(v, "col", [(4 * z + x, 4 * ((z + d) % 4) + x) for z in range(4) for x in range(4)])


def gather_noise(noise):
    gathered = []
    for half, (first, second) in enumerate(((over_x, over_z), (over_z, over_x))):
        own = noise[HALF * half : HALF * (half + 1)]
        own = jnp.stack([own] + [first(own, d) for d in (1, 2, 3)])
        gathered.append((own, second(own, 1), second(own, 3), second))
    pieces = []
    for own, before, after, second in gathered:
        pieces += [own, before, after, second(before[:2], 1), second(after[2:], 3)]
    return pieces


def score_kernel(info_ref, noise_ref, data_ref, score_ref, lse_ref, data_sq_ref, big, total):
    step = pl.program_id(0)

    @pl.when(step == 0)
    def _():
        big[...] = jnp.full(big.shape, MASKED, F32)
        total[...] = jnp.zeros(total.shape, F32)

    data = jnp.concatenate([data_ref[k] for k in range(N_ROW)], axis=1)
    data_sq = []
    for a in range(COL_BLOCK // 128):
        squares = jnp.zeros((128, 128), F32)
        for k in range(WIDTH // 128):
            piece = data[128 * a : 128 * (a + 1), 128 * k : 128 * (k + 1)].astype(F32)
            squares += piece * piece
        data_sq.append(jnp.sum(squares.T, axis=0, keepdims=True))
        data_sq_ref[0, a : a + 1, :] = data_sq[a]

    j = info_ref[17] + step * COL_BLOCK + lax.broadcasted_iota(jnp.int32, (1, COL_BLOCK), 1)
    low = jnp.zeros((1, COL_BLOCK), jnp.int32)
    high = jnp.zeros((1, COL_BLOCK), jnp.int32)
    noise_at = jnp.int32(0)
    data_at = jnp.int32(0)
    for c in range(CLUSTERS):
        noise_end = noise_at + info_ref[c]
        data_end = data_at + info_ref[8 + c]
        if c == CLUSTERS - 1:
            inside = j >= data_at
        else:
            inside = (j >= data_at) & (j < data_end)
        low = jnp.where(inside, noise_at, low)
        high = jnp.where(inside, noise_end, high)
        noise_at, data_at = noise_end, data_end
    low = low - info_ref[16]
    high = high - info_ref[16]

    half = SCORE_ROWS
    for r in range(ROWS // half):
        inner = lax.dot_general(noise_ref[half * r : half * (r + 1), :], data, (((1,), (1,)), ((), ())), preferred_element_type=F32)
        i = half * r + lax.broadcasted_iota(jnp.int32, (half, COL_BLOCK), 0)
        score = jnp.where((i >= low) & (i < high), inner * (2.0 * KAPPA), MASKED)
        score_ref[half * r : half * (r + 1), :] = score
        parts = [score[:, 128 * t : 128 * (t + 1)] - KAPPA * data_sq[t] for t in range(COL_BLOCK // 128)]
        at = slice(half * r, half * (r + 1))
        old = big[at, :]
        new = functools.reduce(jnp.maximum, parts, old)
        total[at, :] = total[at, :] * jnp.exp2(old - new) + functools.reduce(
            jnp.add, [jnp.exp2(part - new) for part in parts]
        )
        big[at, :] = new

    @pl.when(step == pl.num_programs(0) - 1)
    def _():
        rows = []
        for a in range(ROWS // 128):
            at = slice(128 * a, 128 * (a + 1))
            m = big[at, :].T
            s = total[at, :].T
            largest = jnp.max(m, axis=0, keepdims=True)
            summed = jnp.sum(s * jnp.exp2(m - largest), axis=0, keepdims=True)
            rows.append(largest + jnp.log2(summed))
        lse_ref[...] = jnp.broadcast_to(jnp.concatenate(rows, axis=0)[None], lse_ref.shape)


def scores(info, noise, data):
    return pl.pallas_call(
        score_kernel,
        grid=(COLS // COL_BLOCK,),
        in_specs=[
            pl.BlockSpec(memory_space=pltpu.SMEM),
            vmem((ROWS, WIDTH)),
            vmem((N_ROW, COL_BLOCK, 256), lambda j: (0, j, 0)),
        ],
        out_specs=[
            vmem((ROWS, COL_BLOCK), lambda j: (0, j)),
            vmem((N_COL, 8, 128)),
            vmem((1, COL_BLOCK // 128, 128), lambda j: (j, 0, 0)),
        ],
        out_shape=[
            jax.ShapeDtypeStruct((ROWS, COLS), F32),
            jax.ShapeDtypeStruct((N_COL, 8, 128), F32),
            jax.ShapeDtypeStruct((COLS // COL_BLOCK, COL_BLOCK // 128, 128), F32),
        ],
        scratch_shapes=[pltpu.VMEM((ROWS, 128), F32), pltpu.VMEM((ROWS, 128), F32)],
        compiler_params=params(40),
        cost_estimate=pl.CostEstimate(flops=2 * ROWS * COLS * WIDTH, bytes_accessed=20 * MIB, transcendentals=3 << 20),
        name="scores",
    )(info, noise, data)


def merge_lse(parts_ref):
    parts = parts_ref[...]
    largest = jnp.max(parts, axis=0)
    return -(largest + jnp.log2(jnp.sum(jnp.exp2(parts - largest[None]), axis=0)))


def merge_scale(parts_ref):
    return 1.0 / jnp.sum(parts_ref[...], axis=0)


GROUP = 8


def first_columns_kernel(parts_ref, score_ref, lse_ref, noise_ref, e_ref, max_ref, column, big, total):
    step = pl.program_id(0)
    blocks = ROWS // ROW_BLOCK
    tiles = COLS // 128
    base = lax.rem(step, blocks) * ROW_BLOCK

    @pl.when(step == 0)
    def _():
        potential = merge_lse(parts_ref)
        noise_ref[...] = potential
        for a, piece in enumerate(to_column(potential)):
            column[128 * a : 128 * (a + 1), :] = piece
        big[...] = jnp.full(big.shape, MASKED, F32)
        total[...] = jnp.zeros(total.shape, F32)

    @pl.when(step < blocks)
    def _():
        def largest(g, carry):
            shift = column[pl.ds(pl.multiple_of(base + g * GROUP, GROUP), GROUP), :]
            at = pl.ds(pl.multiple_of(g * GROUP, GROUP), GROUP)
            return tuple(jnp.maximum(carry[t], score_ref[at, 128 * t : 128 * (t + 1)] + shift) for t in range(tiles))

        start = tuple(big[:, 128 * t : 128 * (t + 1)] for t in range(tiles))
        new = lax.fori_loop(0, ROW_BLOCK // GROUP, largest, start, unroll=2)
        for t in range(tiles):
            big[:, 128 * t : 128 * (t + 1)] = new[t]

    @pl.when(step == blocks)
    def _():
        big[...] = jnp.broadcast_to(jnp.max(big[...], axis=0, keepdims=True), big.shape)

    @pl.when(step >= blocks)
    def _():
        most = [big[:, 128 * t : 128 * (t + 1)] for t in range(tiles)]

        def add(g, carry):
            shift = column[pl.ds(pl.multiple_of(base + g * GROUP, GROUP), GROUP), :]
            at = pl.ds(pl.multiple_of(g * GROUP, GROUP), GROUP)
            out = []
            for t in range(tiles):
                here = slice(128 * t, 128 * (t + 1))
                value = jnp.exp2(score_ref[at, here] + (shift - most[t]))
                e_ref[at, here] = value
                out.append(carry[t] + value)
            return tuple(out)

        start = tuple(total[:, 128 * t : 128 * (t + 1)] for t in range(tiles))
        summed = lax.fori_loop(0, ROW_BLOCK // GROUP, add, start, unroll=2)
        for t in range(tiles):
            total[:, 128 * t : 128 * (t + 1)] = summed[t]

    @pl.when(step == 2 * blocks - 1)
    def _():
        most = big[0:1, :]
        s = jnp.sum(total[...], axis=0, keepdims=True)
        lse_ref[...] = jnp.broadcast_to(from_lanes(most + jnp.log2(s))[None], lse_ref.shape)
        max_ref[...] = from_lanes(most)


def pass_call(kernel, inputs, in_specs, outs, out_specs, scratch, name, transcendentals=0, sweeps=1):
    return pl.pallas_call(
        kernel,
        grid=(sweeps * (ROWS // ROW_BLOCK),),
        in_specs=in_specs,
        out_specs=out_specs,
        out_shape=outs,
        scratch_shapes=scratch,
        compiler_params=params(24),
        cost_estimate=pl.CostEstimate(flops=4 * ROWS * COLS, bytes_accessed=8 * MIB, transcendentals=transcendentals),
        name=name,
    )(*inputs)


FROM_COL = vmem((N_COL, 8, 128))
FROM_ROW = vmem((N_ROW, 16, 128))
NOISE = vmem((8, 128))
DATA = vmem((16, 128))
BLOCK = vmem((ROW_BLOCK, COLS), lambda i: (i, 0))
FROM_COL_SHAPE = jax.ShapeDtypeStruct((N_COL, 8, 128), F32)
FROM_ROW_SHAPE = jax.ShapeDtypeStruct((N_ROW, 16, 128), F32)
NOISE_SHAPE = jax.ShapeDtypeStruct((8, 128), F32)
DATA_SHAPE = jax.ShapeDtypeStruct((16, 128), F32)
BLOCK_SHAPE = jax.ShapeDtypeStruct((ROWS, COLS), F32)


def first_columns(parts, score):
    blocks = ROWS // ROW_BLOCK
    return pass_call(
        first_columns_kernel,
        (parts, score),
        [FROM_COL, vmem((ROW_BLOCK, COLS), lambda i: (lax.rem(i, blocks), 0))],
        [FROM_ROW_SHAPE, NOISE_SHAPE, BLOCK_SHAPE, DATA_SHAPE],
        [FROM_ROW, NOISE, vmem((ROW_BLOCK, COLS), lambda i: (jnp.maximum(i - blocks, 0), 0)), DATA],
        [pltpu.VMEM((ROWS, 128), F32), pltpu.VMEM((8, COLS), F32), pltpu.VMEM((8, COLS), F32)],
        "first_columns",
        ROWS * COLS,
        2,
    )


def write_row_sums(sums, out_ref, rows, step):
    per = ROW_BLOCK // 128
    for a in range(per):
        piece = sums[128 * a : 128 * (a + 1), :].T
        rows[pl.ds(step * per + a, 1), :] = jnp.sum(piece, axis=0, keepdims=True)

    @pl.when(step == pl.num_programs(0) - 1)
    def _():
        out_ref[...] = jnp.broadcast_to(rows[...][None], out_ref.shape)


def column_sums_kernel(parts_ref, factor_ref, k_ref, sums_ref, scale_ref, column, total):
    step = pl.program_id(0)

    @pl.when(step == 0)
    def _():
        scale = merge_scale(parts_ref)
        scale_ref[...] = scale
        for a, piece in enumerate(to_column(scale)):
            column[128 * a : 128 * (a + 1), :] = piece
        total[...] = jnp.zeros(total.shape, F32)

    base = step * ROW_BLOCK
    tiles = COLS // 128

    def add(g, carry):
        scale = column[pl.ds(pl.multiple_of(base + g * GROUP, GROUP), GROUP), :]
        at = pl.ds(pl.multiple_of(g * GROUP, GROUP), GROUP)
        return tuple(carry[t] + k_ref[at, 128 * t : 128 * (t + 1)] * scale for t in range(tiles))

    start = tuple(total[:, 128 * t : 128 * (t + 1)] for t in range(tiles))
    summed = lax.fori_loop(0, ROW_BLOCK // GROUP, add, start, unroll=4)
    for t in range(tiles):
        total[:, 128 * t : 128 * (t + 1)] = summed[t]

    @pl.when(step == pl.num_programs(0) - 1)
    def _():
        s = jnp.sum(total[...], axis=0, keepdims=True)
        sums_ref[...] = jnp.broadcast_to((from_lanes(s) * factor_ref[...])[None], sums_ref.shape)


def column_sums(parts, factor, k):
    return pass_call(
        column_sums_kernel,
        (parts, factor, k),
        [FROM_COL, DATA, BLOCK],
        [FROM_ROW_SHAPE, NOISE_SHAPE],
        [FROM_ROW, NOISE],
        [pltpu.VMEM((ROWS, 128), F32), pltpu.VMEM((GROUP, COLS), F32)],
        "column_sums",
    )


def row_sums_kernel(first, parts_ref, factor_ref, k_ref, sums_ref, *refs):
    lanes, sums, rows = refs[-3:]
    step = pl.program_id(0)

    @pl.when(step == 0)
    def _():
        if first:
            data_ref, out_ref = refs[:2]
            potential = merge_lse(parts_ref)
            data_ref[...] = potential
            scale = jnp.exp2(factor_ref[...] + potential)
            out_ref[...] = scale
        else:
            scale = factor_ref[...] * merge_scale(parts_ref)
        lanes[...] = jnp.broadcast_to(to_lanes(scale), lanes.shape)

    tiles = COLS // 128
    scales = [lanes[:, 128 * t : 128 * (t + 1)] for t in range(tiles)]

    def body(g, _):
        at = pl.ds(pl.multiple_of(g * GROUP, GROUP), GROUP)
        summed = [k_ref[at, 128 * t : 128 * (t + 1)] * scales[t] for t in range(4)]
        for t in range(4, tiles):
            summed[t % 4] += k_ref[at, 128 * t : 128 * (t + 1)] * scales[t]
        sums[at, :] = (summed[0] + summed[1]) + (summed[2] + summed[3])
        return 0

    lax.fori_loop(0, ROW_BLOCK // GROUP, body, 0, unroll=4)
    write_row_sums(sums, sums_ref, rows, step)


def row_sums(first, parts, factor, k):
    more = 2 if first else 0
    return pass_call(
        functools.partial(row_sums_kernel, first),
        (parts, factor, k),
        [FROM_ROW, DATA, BLOCK],
        [FROM_COL_SHAPE] + [DATA_SHAPE] * more,
        [FROM_COL] + [DATA] * more,
        [pltpu.VMEM((GROUP, COLS), F32), pltpu.VMEM((ROW_BLOCK, 128), F32), pltpu.VMEM((8, 128), F32)],
        "row_sums",
    )


def coupling_kernel(
    parts_ref, scale_ref, noise_first, noise_sq, data_first, data_sq, factor_ref, k_ref,
    pa_ref, pb_ref, sums_ref, noise_ref, data_ref, column, lanes, sums,
):
    step = pl.program_id(0)

    @pl.when(step == 0)
    def _():
        scale = merge_scale(parts_ref)
        lanes[...] = jnp.broadcast_to(to_lanes(factor_ref[...] * scale), lanes.shape)
        for a, piece in enumerate(to_column(scale_ref[...])):
            column[128 * a : 128 * (a + 1), :] = piece
        noise_ref[...] = (EPS * LN2) * (noise_first[...] + jnp.log2(scale_ref[...])) + noise_sq[...] * (1.0 / WIDTH)
        potential = (EPS * LN2) * (data_first[...] + jnp.log2(scale))
        per = COL_BLOCK // 128
        for k in range(COLS // COL_BLOCK):
            at = slice(per * k, per * (k + 1))
            data_ref[at, :] = potential[at, :] + data_sq[k] * (1.0 / WIDTH)

    base = step * ROW_BLOCK
    tiles = COLS // 128

    def block(p_ref):
        def body(g, _):
            at = pl.ds(pl.multiple_of(g * 16, 16), 16)
            scale = column[pl.ds(pl.multiple_of(base + g * 16, 16), 16), :]
            summed = jnp.zeros((16, 128), F32)
            for t in range(tiles):
                here = slice(128 * t, 128 * (t + 1))
                value = (k_ref[at, here] * (scale * lanes[:, here])).astype(BF16)
                p_ref[at, here] = value
                summed += value.astype(F32)
            sums[at, :] = summed
            return 0

        lax.fori_loop(0, ROW_BLOCK // 16, body, 0, unroll=2)

    @pl.when(step < 2)
    def _():
        block(pa_ref)

    @pl.when(step >= 2)
    def _():
        block(pb_ref)

    per = ROW_BLOCK // 128
    for a in range(per):
        piece = sums[128 * a : 128 * (a + 1), :].T
        sums_ref[pl.ds(step * per + a, 1), :] = jnp.sum(piece, axis=0, keepdims=True)


def coupling(parts, noise_scale, noise_first, noise_sq, data_first, data_sq, factor, k):
    half = jax.ShapeDtypeStruct((HALF, COLS), BF16)
    return pass_call(
        coupling_kernel,
        (parts, noise_scale, noise_first, noise_sq, data_first, data_sq, factor, k),
        [FROM_ROW, NOISE, NOISE, NOISE, DATA, vmem((COLS // COL_BLOCK, COL_BLOCK // 128, 128)), DATA, BLOCK],
        [half, half, NOISE_SHAPE, NOISE_SHAPE, DATA_SHAPE],
        [
            vmem((ROW_BLOCK, COLS), lambda i: (jnp.minimum(i, 1), 0)),
            vmem((ROW_BLOCK, COLS), lambda i: (jnp.maximum(i - 2, 0), 0)),
            NOISE,
            NOISE,
            DATA,
        ],
        [
            pltpu.VMEM((ROWS, 128), F32),
            pltpu.VMEM((16, COLS), F32),
            pltpu.VMEM((ROW_BLOCK, 128), F32),
        ],
        "coupling",
    )


EXTRA = 16


def split(value):
    high = value.astype(BF16)
    return high, (value - high.astype(F32)).astype(BF16)


def row_sum_rows(sums):
    high, low = split(sums)
    return jnp.concatenate([high, low, high, low], axis=0)


def target_kernel(ways, info_ref, pa_ref, pb_ref, sums_ref, data_ref, *out_refs):
    z, x = info_ref[18], info_ref[19]
    out_refs = list(out_refs)
    for side in (0, 1):
        tail = row_sum_rows(sums_ref[4 * side : 4 * side + 4, :])
        for way in ways:
            if side == 0:
                block = lax.rem(x + way, 4)
                lanes = pl.ds(pl.multiple_of(lax.rem(block, 2) * 128, 128), 128)
                data = [data_ref[2 * k + block // 2, :, lanes] for k in range(4)]
                values = pa_ref[...]
            else:
                block = lax.rem(z + way, 4)
                data = [data_ref[2 * block + k] for k in range(2)]
                values = pb_ref[...]
            summed = jnp.dot(values, jnp.concatenate(data, axis=1), preferred_element_type=F32).astype(BF16)
            parts = 2 if way == 2 else 1
            rows = HALF // parts
            for part in range(parts):
                out_ref = out_refs.pop(0)
                for b in range(4):
                    out_ref[b, :rows, :] = summed[rows * part : rows * (part + 1), 128 * b : 128 * (b + 1)]
                    out_ref[b, rows:, :] = tail


def messages(ways, info, p, sums, data):
    rows = [HALF // 2] * 2 if ways == (2,) else [HALF] * len(ways)
    made = pl.pallas_call(
        functools.partial(target_kernel, ways),
        in_specs=[pl.BlockSpec(memory_space=pltpu.SMEM)] + [pl.BlockSpec(memory_space=pltpu.VMEM)] * 4,
        out_shape=[jax.ShapeDtypeStruct((4, n + EXTRA, 128), BF16) for n in rows * 2],
        compiler_params=pltpu.CompilerParams(vmem_limit_bytes=28 * MIB),
        cost_estimate=pl.CostEstimate(
            flops=ROWS * COLS * WIDTH // 2 * len(ways), bytes_accessed=8 * MIB, transcendentals=0
        ),
        name="targets",
    )(info, *p, sums, data)
    return made[: len(rows)], made[len(rows) :]


def forward_kernel(next_ref, last_ref, from_left, from_right, out_next, out_last):
    half = HALF // 2
    low, high, rest = slice(0, half), slice(half, HALF), slice(HALF, HALF + EXTRA)
    for b in range(4):
        out_next[b, low, :] = (next_ref[b, low, :].astype(F32) + from_left[b, low, :].astype(F32)).astype(BF16)
        out_next[b, high, :] = next_ref[b, high, :]
        out_last[b, low, :] = last_ref[b, low, :]
        out_last[b, high, :] = (last_ref[b, high, :].astype(F32) + from_right[b, low, :].astype(F32)).astype(BF16)
        out_next[b, rest, :] = row_sum_rows(row_sums_of(next_ref, 0, HALF) + row_sums_of(from_left, 0, half))
        out_last[b, rest, :] = last_ref[b, rest, :]


def forward(following, preceding, from_left, from_right):
    return pl.pallas_call(
        forward_kernel,
        out_shape=[jax.ShapeDtypeStruct((4, HALF + EXTRA, 128), BF16)] * 2,
        compiler_params=pltpu.CompilerParams(vmem_limit_bytes=16 * MIB),
        cost_estimate=pl.CostEstimate(flops=1 << 20, bytes_accessed=3 * MIB, transcendentals=0),
        name="forward",
    )(following, preceding, from_left, from_right)


def row_sums_of(ref, index=None, start=HALF):
    at = [slice(start + 4 * i, start + 4 * i + 4) for i in (0, 1)]
    high, low = (ref[i, :] if index is None else ref[index, i, :] for i in at)
    return high.astype(F32) + low.astype(F32)


def combine_kernel(side, info_ref, own, left, right, keep_ref, s1, s2, s3):
    place = info_ref[18 + side]
    sums = row_sums_of(own, 0) + (row_sums_of(left, 0) + row_sums_of(right, 0))
    tail = row_sum_rows(sums)

    def summed(index):
        at = slice(0, HALF)
        return own[index, at, :].astype(F32) + (left[index, at, :].astype(F32) + right[index, at, :].astype(F32))

    for d, out_ref in ((1, s1), (2, s2), (3, s3)):
        out_ref[:HALF, :] = summed(lax.rem(place + d, 4)).astype(BF16)
        out_ref[HALF:, :] = tail
    keep_ref[:HALF, :] = summed(place)
    keep_ref[HALF:, :] = jnp.concatenate([sums, jnp.zeros((EXTRA - 4, 128), F32)], axis=0)


def combine(side, info, parts):
    return pl.pallas_call(
        functools.partial(combine_kernel, side),
        in_specs=[pl.BlockSpec(memory_space=pltpu.SMEM)] + [pl.BlockSpec(memory_space=pltpu.VMEM)] * 3,
        out_shape=[jax.ShapeDtypeStruct((HALF + EXTRA, 128), F32)] + [jax.ShapeDtypeStruct((HALF + EXTRA, 128), BF16)] * 3,
        compiler_params=pltpu.CompilerParams(vmem_limit_bytes=16 * MIB),
        cost_estimate=pl.CostEstimate(flops=1 << 20, bytes_accessed=3 * MIB, transcendentals=0),
        name="combine",
    )(info, *parts)


def finish_kernel(noise_ref, *refs):
    out_ref = refs[-1]
    for half in range(2):
        own, *others = refs[4 * half : 4 * half + 4]
        sums = own[HALF : HALF + 4, :]
        for other in others:
            sums += row_sums_of(other)
        for a, inverse in enumerate(to_column(1.0 / sums)):
            here = slice(128 * a, 128 * (a + 1))
            at = slice(HALF * half + 128 * a, HALF * half + 128 * (a + 1))
            summed = own[here, :]
            for other in others:
                summed += other[here, :].astype(F32)
            out_ref[at, :] = summed * inverse - noise_ref[at, :].astype(F32)


def finish(noise, parts):
    return pl.pallas_call(
        finish_kernel,
        out_shape=jax.ShapeDtypeStruct((ROWS, 128), F32),
        compiler_params=pltpu.CompilerParams(vmem_limit_bytes=16 * MIB),
        name="finish",
    )(noise, *parts)


def swap(x, axis):
    return lax.all_to_all(x, axis, 0, 0, tiled=True)


def per_device(noise_latents, data_latents, noise_sizes, data_sizes):
    row, col = lax.axis_index("row"), lax.axis_index("col")
    places = jnp.stack([row * ROWS, col * COLS, col // 4, col % 4]).astype(jnp.int32)
    info = jnp.concatenate([noise_sizes, data_sizes, places])
    data = lax.all_gather(data_latents, "row")
    noise, noise_sq = arrange(info, gather_noise(noise_latents))
    score, lse, data_sq = scores(info, noise, data)
    lse, noise_first, e, most = first_columns(swap(lse, "col"), score)
    sums, data_first, factor = row_sums(True, swap(lse, "row"), most, e)
    sums, _ = column_sums(swap(sums, "col"), factor, e)
    sums = row_sums(False, swap(sums, "row"), factor, e)[0]
    sums, noise_scale = column_sums(swap(sums, "col"), factor, e)
    *p, sums, noise_potential, data_potential = coupling(
        swap(sums, "row"), noise_scale, noise_first, noise_sq, data_first, data_sq, factor, e
    )
    way = (over_x, over_z)
    made = messages((2,), info, p, sums, data)
    moved = [(way[side](made[side][0], 1), way[side](made[side][1], 3)) for side in (0, 1)]
    sums, _ = lax.optimization_barrier((sums, made))
    made = messages((1, 3), info, p, sums, data)
    sums, _ = lax.optimization_barrier((sums, made))
    got = []
    for side in (0, 1):
        following, preceding = forward(*made[side], *moved[side])
        got.append((way[side](following, 1), way[side](preceding, 3)))
        sums, _ = lax.optimization_barrier((sums, following))
    own = messages((0,), info, p, sums, data)
    ends = []
    for side in (0, 1):
        keep, *others = combine(side, info, (own[side][0], *got[side]))
        ends += [keep] + [way[1 - side](v, d) for d, v in zip((1, 2, 3), others)]
    velocity = finish(noise_latents, ends)
    return velocity, noise_potential.reshape(ROWS), data_potential.reshape(COLS)


def solution(mesh):
    placed = (P("row", "col"), P("col", "row"), P(), P())
    return jax.shard_map(
        per_device,
        mesh=mesh,
        in_specs=placed,
        out_specs=(P("row", "col"), P("row"), P("col")),
        check_vma=False,
    )
```

```python
import functools

import jax
import jax.numpy as jnp
from jax import lax
from jax.experimental import pallas as pl
from jax.experimental.pallas import tpu as pltpu
from jax.sharding import PartitionSpec as P

EPS = 0.05
LOG2E = 1.4426950408889634
LN2 = 0.6931471805599453
MASKED = -1e30
CLUSTERS = 8
F32 = jnp.float32
BF16 = jnp.bfloat16
MIB = 1 << 20

ROWS = 1024
COLS = 2048
WIDTH = 2048
COL_BLOCK = 512
SCORE_ROWS = 1024
ROW_BLOCK = 256
HALF = 512
N_ROW = 8
N_COL = 16
KAPPA = LOG2E / (WIDTH * EPS)


def vmem(shape, index_map=None):
    if index_map is None:
        return pl.BlockSpec(shape, lambda *_: (0,) * len(shape))
    return pl.BlockSpec(shape, index_map)


def params(mib):
    return pltpu.CompilerParams(vmem_limit_bytes=mib * MIB, dimension_semantics=("arbitrary",))


def lane_totals(pieces):
    return [piece.T for piece in pieces]


def to_column(rows):
    n = rows.shape[0]
    return [jnp.broadcast_to(rows[a : a + 1, :], (128, 128)).T for a in range(n)]


def to_lanes(rows):
    return jnp.concatenate([rows[a : a + 1, :] for a in range(rows.shape[0])], axis=1)


def from_lanes(row):
    return jnp.concatenate([row[:, 128 * a : 128 * (a + 1)] for a in range(row.shape[1] // 128)], axis=0)


def arrange_kernel(info_ref, *refs):
    out_ref, noise_sq_ref = refs[10:]
    z, x = info_ref[18], info_ref[19]
    sums = []
    for half in range(2):
        own, before, after, second_a, second_b = refs[5 * half : 5 * half + 5]
        at = slice(HALF * half, HALF * (half + 1))
        squares = jnp.zeros((HALF, 128), F32)
        for far, source in ((0, own), (1, before), (3, after), (2, None)):
            for near in range(4):
                if source is not None:
                    piece = source[near]
                else:
                    piece = second_a[near] if near < 2 else second_b[near - 2]
                if half == 0:
                    index = lax.rem(z + 4 - far, 4) * 4 + lax.rem(x + 4 - near, 4)
                else:
                    index = lax.rem(z + 4 - near, 4) * 4 + lax.rem(x + 4 - far, 4)
                out_ref[at, pl.ds(pl.multiple_of(index * 128, 128), 128)] = piece
                squares += piece.astype(F32) * piece.astype(F32)
        for a in range(HALF // 128):
            sums.append(jnp.sum(squares[128 * a : 128 * (a + 1), :].T, axis=0, keepdims=True))
    noise_sq_ref[...] = jnp.concatenate(sums, axis=0)


def arrange(info, pieces):
    return pl.pallas_call(
        arrange_kernel,
        in_specs=[pl.BlockSpec(memory_space=pltpu.SMEM)] + [pl.BlockSpec(memory_space=pltpu.VMEM)] * 10,
        out_shape=[jax.ShapeDtypeStruct((ROWS, WIDTH), BF16), NOISE_SHAPE],
        compiler_params=pltpu.CompilerParams(vmem_limit_bytes=24 * MIB),
        cost_estimate=pl.CostEstimate(flops=4 << 20, bytes_accessed=8 * MIB, transcendentals=0),
        name="arrange",
    )(info, *pieces)


def over_x(v, d):
    return lax.ppermute(v, "col", [(4 * z + x, 4 * z + (x + d) % 4) for z in range(4) for x in range(4)])


def over_z(v, d):
    return lax.ppermute(v, "col", [(4 * z + x, 4 * ((z + d) % 4) + x) for z in range(4) for x in range(4)])


def gather_noise(noise):
    gathered = []
    for half, (first, second) in enumerate(((over_x, over_z), (over_z, over_x))):
        own = noise[HALF * half : HALF * (half + 1)]
        own = jnp.stack([own] + [first(own, d) for d in (1, 2, 3)])
        gathered.append((own, second(own, 1), second(own, 3), second))
    pieces = []
    for own, before, after, second in gathered:
        pieces += [own, before, after, second(before[:2], 1), second(after[2:], 3)]
    return pieces


def score_kernel(info_ref, noise_ref, data_ref, score_ref, lse_ref, data_sq_ref, big, total):
    step = pl.program_id(0)

    @pl.when(step == 0)
    def _():
        big[...] = jnp.full(big.shape, MASKED, F32)
        total[...] = jnp.zeros(total.shape, F32)

    data = jnp.concatenate([data_ref[k] for k in range(N_ROW)], axis=1)
    data_sq = []
    for a in range(COL_BLOCK // 128):
        squares = jnp.zeros((128, 128), F32)
        for k in range(WIDTH // 128):
            piece = data[128 * a : 128 * (a + 1), 128 * k : 128 * (k + 1)].astype(F32)
            squares += piece * piece
        data_sq.append(jnp.sum(squares.T, axis=0, keepdims=True))
        data_sq_ref[0, a : a + 1, :] = data_sq[a]

    j = info_ref[17] + step * COL_BLOCK + lax.broadcasted_iota(jnp.int32, (1, COL_BLOCK), 1)
    low = jnp.zeros((1, COL_BLOCK), jnp.int32)
    high = jnp.zeros((1, COL_BLOCK), jnp.int32)
    noise_at = jnp.int32(0)
    data_at = jnp.int32(0)
    for c in range(CLUSTERS):
        noise_end = noise_at + info_ref[c]
        data_end = data_at + info_ref[8 + c]
        if c == CLUSTERS - 1:
            inside = j >= data_at
        else:
            inside = (j >= data_at) & (j < data_end)
        low = jnp.where(inside, noise_at, low)
        high = jnp.where(inside, noise_end, high)
        noise_at, data_at = noise_end, data_end
    low = low - info_ref[16]
    span = (high - info_ref[16] - low).astype(jnp.uint32)

    half = SCORE_ROWS
    for r in range(ROWS // half):
        inner = lax.dot_general(noise_ref[half * r : half * (r + 1), :], data, (((1,), (1,)), ((), ())), preferred_element_type=F32)
        i = half * r + lax.broadcasted_iota(jnp.int32, (half, COL_BLOCK), 0)
        score = jnp.where((i - low).astype(jnp.uint32) < span, inner * (2.0 * KAPPA), MASKED)
        score_ref[half * r : half * (r + 1), :] = score
        parts = [score[:, 128 * t : 128 * (t + 1)] - KAPPA * data_sq[t] for t in range(COL_BLOCK // 128)]
        at = slice(half * r, half * (r + 1))
        old = big[at, :]
        new = functools.reduce(jnp.maximum, parts, old)
        total[at, :] = total[at, :] * jnp.exp2(old - new) + functools.reduce(
            jnp.add, [jnp.exp2(part - new) for part in parts]
        )
        big[at, :] = new

    @pl.when(step == pl.num_programs(0) - 1)
    def _():
        rows = []
        for a in range(ROWS // 128):
            at = slice(128 * a, 128 * (a + 1))
            m = big[at, :].T
            s = total[at, :].T
            largest = jnp.max(m, axis=0, keepdims=True)
            summed = jnp.sum(s * jnp.exp2(m - largest), axis=0, keepdims=True)
            rows.append(largest + jnp.log2(summed))
        lse_ref[...] = jnp.broadcast_to(jnp.concatenate(rows, axis=0)[None], lse_ref.shape)


def scores(info, noise, data):
    return pl.pallas_call(
        score_kernel,
        grid=(COLS // COL_BLOCK,),
        in_specs=[
            pl.BlockSpec(memory_space=pltpu.SMEM),
            vmem((ROWS, WIDTH)),
            vmem((N_ROW, COL_BLOCK, 256), lambda j: (0, j, 0)),
        ],
        out_specs=[
            vmem((ROWS, COL_BLOCK), lambda j: (0, j)),
            vmem((N_COL, 8, 128)),
            vmem((1, COL_BLOCK // 128, 128), lambda j: (j, 0, 0)),
        ],
        out_shape=[
            jax.ShapeDtypeStruct((ROWS, COLS), F32),
            jax.ShapeDtypeStruct((N_COL, 8, 128), F32),
            jax.ShapeDtypeStruct((COLS // COL_BLOCK, COL_BLOCK // 128, 128), F32),
        ],
        scratch_shapes=[pltpu.VMEM((ROWS, 128), F32), pltpu.VMEM((ROWS, 128), F32)],
        compiler_params=params(40),
        cost_estimate=pl.CostEstimate(flops=2 * ROWS * COLS * WIDTH, bytes_accessed=20 * MIB, transcendentals=3 << 20),
        name="scores",
    )(info, noise, data)


def merge_lse(parts_ref):
    parts = parts_ref[...]
    largest = jnp.max(parts, axis=0)
    return -(largest + jnp.log2(jnp.sum(jnp.exp2(parts - largest[None]), axis=0)))


def merge_scale(parts_ref):
    return 1.0 / jnp.sum(parts_ref[...], axis=0)


GROUP = 8


def first_columns_kernel(parts_ref, score_ref, lse_ref, noise_ref, e_ref, max_ref, column, big, total):
    step = pl.program_id(0)
    blocks = ROWS // ROW_BLOCK
    tiles = COLS // 128
    base = lax.rem(step, blocks) * ROW_BLOCK

    @pl.when(step == 0)
    def _():
        potential = merge_lse(parts_ref)
        noise_ref[...] = potential
        for a, piece in enumerate(to_column(potential)):
            column[128 * a : 128 * (a + 1), :] = piece
        big[...] = jnp.full(big.shape, MASKED, F32)
        total[...] = jnp.zeros(total.shape, F32)

    @pl.when(step < blocks)
    def _():
        def largest(g, carry):
            shift = column[pl.ds(pl.multiple_of(base + g * GROUP, GROUP), GROUP), :]
            at = pl.ds(pl.multiple_of(g * GROUP, GROUP), GROUP)
            return tuple(jnp.maximum(carry[t], score_ref[at, 128 * t : 128 * (t + 1)] + shift) for t in range(tiles))

        start = tuple(big[:, 128 * t : 128 * (t + 1)] for t in range(tiles))
        new = lax.fori_loop(0, ROW_BLOCK // GROUP, largest, start, unroll=4)
        for t in range(tiles):
            big[:, 128 * t : 128 * (t + 1)] = new[t]

    @pl.when(step == blocks)
    def _():
        big[...] = jnp.broadcast_to(jnp.max(big[...], axis=0, keepdims=True), big.shape)

    @pl.when(step >= blocks)
    def _():
        most = [big[:, 128 * t : 128 * (t + 1)] for t in range(tiles)]

        def add(g, carry):
            shift = column[pl.ds(pl.multiple_of(base + g * GROUP, GROUP), GROUP), :]
            at = pl.ds(pl.multiple_of(g * GROUP, GROUP), GROUP)
            out = []
            for t in range(tiles):
                here = slice(128 * t, 128 * (t + 1))
                value = jnp.exp2(score_ref[at, here] + (shift - most[t]))
                e_ref[at, here] = value
                out.append(carry[t] + value)
            return tuple(out)

        start = tuple(total[:, 128 * t : 128 * (t + 1)] for t in range(tiles))
        summed = lax.fori_loop(0, ROW_BLOCK // GROUP, add, start, unroll=4)
        for t in range(tiles):
            total[:, 128 * t : 128 * (t + 1)] = summed[t]

    @pl.when(step == 2 * blocks - 1)
    def _():
        most = big[0:1, :]
        s = jnp.sum(total[...], axis=0, keepdims=True)
        lse_ref[...] = jnp.broadcast_to(from_lanes(most + jnp.log2(s))[None], lse_ref.shape)
        max_ref[...] = from_lanes(most)


def pass_call(kernel, inputs, in_specs, outs, out_specs, scratch, name, transcendentals=0, sweeps=1):
    return pl.pallas_call(
        kernel,
        grid=(sweeps * (ROWS // ROW_BLOCK),),
        in_specs=in_specs,
        out_specs=out_specs,
        out_shape=outs,
        scratch_shapes=scratch,
        compiler_params=params(24),
        cost_estimate=pl.CostEstimate(flops=4 * ROWS * COLS, bytes_accessed=8 * MIB, transcendentals=transcendentals),
        name=name,
    )(*inputs)


FROM_COL = vmem((N_COL, 8, 128))
FROM_ROW = vmem((N_ROW, 16, 128))
NOISE = vmem((8, 128))
DATA = vmem((16, 128))
BLOCK = vmem((ROW_BLOCK, COLS), lambda i: (i, 0))
FROM_COL_SHAPE = jax.ShapeDtypeStruct((N_COL, 8, 128), F32)
FROM_ROW_SHAPE = jax.ShapeDtypeStruct((N_ROW, 16, 128), F32)
NOISE_SHAPE = jax.ShapeDtypeStruct((8, 128), F32)
DATA_SHAPE = jax.ShapeDtypeStruct((16, 128), F32)
BLOCK_SHAPE = jax.ShapeDtypeStruct((ROWS, COLS), F32)


def first_columns(parts, score):
    blocks = ROWS // ROW_BLOCK
    return pass_call(
        first_columns_kernel,
        (parts, score),
        [FROM_COL, vmem((ROW_BLOCK, COLS), lambda i: (lax.rem(i, blocks), 0))],
        [FROM_ROW_SHAPE, NOISE_SHAPE, BLOCK_SHAPE, DATA_SHAPE],
        [FROM_ROW, NOISE, vmem((ROW_BLOCK, COLS), lambda i: (jnp.maximum(i - blocks, 0), 0)), DATA],
        [pltpu.VMEM((ROWS, 128), F32), pltpu.VMEM((8, COLS), F32), pltpu.VMEM((8, COLS), F32)],
        "first_columns",
        ROWS * COLS,
        2,
    )


def write_row_sums(sums, out_ref, rows, step):
    per = ROW_BLOCK // 128
    for a in range(per):
        piece = sums[128 * a : 128 * (a + 1), :].T
        rows[pl.ds(step * per + a, 1), :] = jnp.sum(piece, axis=0, keepdims=True)

    @pl.when(step == pl.num_programs(0) - 1)
    def _():
        out_ref[...] = jnp.broadcast_to(rows[...][None], out_ref.shape)


def column_sums_kernel(parts_ref, factor_ref, k_ref, sums_ref, scale_ref, column, total):
    step = pl.program_id(0)

    @pl.when(step == 0)
    def _():
        scale = merge_scale(parts_ref)
        scale_ref[...] = scale
        for a, piece in enumerate(to_column(scale)):
            column[128 * a : 128 * (a + 1), :] = piece
        total[...] = jnp.zeros(total.shape, F32)

    base = step * ROW_BLOCK
    tiles = COLS // 128

    def add(g, carry):
        scale = column[pl.ds(pl.multiple_of(base + g * GROUP, GROUP), GROUP), :]
        at = pl.ds(pl.multiple_of(g * GROUP, GROUP), GROUP)
        return tuple(carry[t] + k_ref[at, 128 * t : 128 * (t + 1)] * scale for t in range(tiles))

    start = tuple(total[:, 128 * t : 128 * (t + 1)] for t in range(tiles))
    summed = lax.fori_loop(0, ROW_BLOCK // GROUP, add, start, unroll=4)
    for t in range(tiles):
        total[:, 128 * t : 128 * (t + 1)] = summed[t]

    @pl.when(step == pl.num_programs(0) - 1)
    def _():
        s = jnp.sum(total[...], axis=0, keepdims=True)
        sums_ref[...] = jnp.broadcast_to((from_lanes(s) * factor_ref[...])[None], sums_ref.shape)


def column_sums(parts, factor, k):
    return pass_call(
        column_sums_kernel,
        (parts, factor, k),
        [FROM_COL, DATA, BLOCK],
        [FROM_ROW_SHAPE, NOISE_SHAPE],
        [FROM_ROW, NOISE],
        [pltpu.VMEM((ROWS, 128), F32), pltpu.VMEM((GROUP, COLS), F32)],
        "column_sums",
    )


def row_sums_kernel(first, parts_ref, factor_ref, k_ref, sums_ref, *refs):
    lanes, sums, rows = refs[-3:]
    step = pl.program_id(0)

    @pl.when(step == 0)
    def _():
        if first:
            data_ref, out_ref = refs[:2]
            potential = merge_lse(parts_ref)
            data_ref[...] = potential
            scale = jnp.exp2(factor_ref[...] + potential)
            out_ref[...] = scale
        else:
            scale = factor_ref[...] * merge_scale(parts_ref)
        lanes[...] = jnp.broadcast_to(to_lanes(scale), lanes.shape)

    tiles = COLS // 128
    scales = [lanes[:, 128 * t : 128 * (t + 1)] for t in range(tiles)]

    def body(g, _):
        at = pl.ds(pl.multiple_of(g * GROUP, GROUP), GROUP)
        summed = [k_ref[at, 128 * t : 128 * (t + 1)] * scales[t] for t in range(4)]
        for t in range(4, tiles):
            summed[t % 4] += k_ref[at, 128 * t : 128 * (t + 1)] * scales[t]
        sums[at, :] = (summed[0] + summed[1]) + (summed[2] + summed[3])
        return 0

    lax.fori_loop(0, ROW_BLOCK // GROUP, body, 0, unroll=4)
    write_row_sums(sums, sums_ref, rows, step)


def row_sums(first, parts, factor, k):
    more = 2 if first else 0
    return pass_call(
        functools.partial(row_sums_kernel, first),
        (parts, factor, k),
        [FROM_ROW, DATA, BLOCK],
        [FROM_COL_SHAPE] + [DATA_SHAPE] * more,
        [FROM_COL] + [DATA] * more,
        [pltpu.VMEM((GROUP, COLS), F32), pltpu.VMEM((ROW_BLOCK, 128), F32), pltpu.VMEM((8, 128), F32)],
        "row_sums",
    )


def coupling_kernel(
    parts_ref, scale_ref, noise_first, noise_sq, data_first, data_sq, factor_ref, k_ref,
    pa_ref, pb_ref, sums_ref, noise_ref, data_ref, column, lanes, sums,
):
    step = pl.program_id(0)

    @pl.when(step == 0)
    def _():
        scale = merge_scale(parts_ref)
        lanes[...] = jnp.broadcast_to(to_lanes(factor_ref[...] * scale), lanes.shape)
        for a, piece in enumerate(to_column(scale_ref[...])):
            column[128 * a : 128 * (a + 1), :] = piece
        noise_ref[...] = (EPS * LN2) * (noise_first[...] + jnp.log2(scale_ref[...])) + noise_sq[...] * (1.0 / WIDTH)
        potential = (EPS * LN2) * (data_first[...] + jnp.log2(scale))
        per = COL_BLOCK // 128
        for k in range(COLS // COL_BLOCK):
            at = slice(per * k, per * (k + 1))
            data_ref[at, :] = potential[at, :] + data_sq[k] * (1.0 / WIDTH)

    base = step * ROW_BLOCK
    tiles = COLS // 128

    def block(p_ref):
        def body(g, _):
            at = pl.ds(pl.multiple_of(g * 16, 16), 16)
            scale = column[pl.ds(pl.multiple_of(base + g * 16, 16), 16), :]
            summed = jnp.zeros((16, 128), F32)
            for t in range(tiles):
                here = slice(128 * t, 128 * (t + 1))
                value = (k_ref[at, here] * (scale * lanes[:, here])).astype(BF16)
                p_ref[at, here] = value
                summed += value.astype(F32)
            sums[at, :] = summed
            return 0

        lax.fori_loop(0, ROW_BLOCK // 16, body, 0, unroll=4)

    @pl.when(step < 2)
    def _():
        block(pa_ref)

    @pl.when(step >= 2)
    def _():
        block(pb_ref)

    per = ROW_BLOCK // 128
    for a in range(per):
        piece = sums[128 * a : 128 * (a + 1), :].T
        sums_ref[pl.ds(step * per + a, 1), :] = jnp.sum(piece, axis=0, keepdims=True)


def coupling(parts, noise_scale, noise_first, noise_sq, data_first, data_sq, factor, k):
    half = jax.ShapeDtypeStruct((HALF, COLS), BF16)
    return pass_call(
        coupling_kernel,
        (parts, noise_scale, noise_first, noise_sq, data_first, data_sq, factor, k),
        [FROM_ROW, NOISE, NOISE, NOISE, DATA, vmem((COLS // COL_BLOCK, COL_BLOCK // 128, 128)), DATA, BLOCK],
        [half, half, NOISE_SHAPE, NOISE_SHAPE, DATA_SHAPE],
        [
            vmem((ROW_BLOCK, COLS), lambda i: (jnp.minimum(i, 1), 0)),
            vmem((ROW_BLOCK, COLS), lambda i: (jnp.maximum(i - 2, 0), 0)),
            NOISE,
            NOISE,
            DATA,
        ],
        [
            pltpu.VMEM((ROWS, 128), F32),
            pltpu.VMEM((16, COLS), F32),
            pltpu.VMEM((ROW_BLOCK, 128), F32),
        ],
        "coupling",
    )


EXTRA = 16


def split(value):
    high = value.astype(BF16)
    return high, (value - high.astype(F32)).astype(BF16)


def row_sum_rows(sums):
    high, low = split(sums)
    return jnp.concatenate([high, low, high, low], axis=0)


def target_kernel(ways, info_ref, pa_ref, pb_ref, sums_ref, data_ref, *out_refs):
    z, x = info_ref[18], info_ref[19]
    out_refs = list(out_refs)
    for side in (0, 1):
        tail = row_sum_rows(sums_ref[4 * side : 4 * side + 4, :])
        for way in ways:
            if side == 0:
                block = lax.rem(x + way, 4)
                lanes = pl.ds(pl.multiple_of(lax.rem(block, 2) * 128, 128), 128)
                data = [data_ref[2 * k + block // 2, :, lanes] for k in range(4)]
                values = pa_ref[...]
            else:
                block = lax.rem(z + way, 4)
                data = [data_ref[2 * block + k] for k in range(2)]
                values = pb_ref[...]
            summed = jnp.dot(values, jnp.concatenate(data, axis=1), preferred_element_type=F32).astype(BF16)
            parts = 2 if way == 2 else 1
            rows = HALF // parts
            for part in range(parts):
                out_ref = out_refs.pop(0)
                for b in range(4):
                    out_ref[b, :rows, :] = summed[rows * part : rows * (part + 1), 128 * b : 128 * (b + 1)]
                    out_ref[b, rows:, :] = tail


def messages(ways, info, p, sums, data):
    rows = [HALF // 2] * 2 if ways == (2,) else [HALF] * len(ways)
    made = pl.pallas_call(
        functools.partial(target_kernel, ways),
        in_specs=[pl.BlockSpec(memory_space=pltpu.SMEM)] + [pl.BlockSpec(memory_space=pltpu.VMEM)] * 4,
        out_shape=[jax.ShapeDtypeStruct((4, n + EXTRA, 128), BF16) for n in rows * 2],
        compiler_params=pltpu.CompilerParams(vmem_limit_bytes=28 * MIB),
        cost_estimate=pl.CostEstimate(
            flops=ROWS * COLS * WIDTH // 2 * len(ways), bytes_accessed=8 * MIB, transcendentals=0
        ),
        name="targets",
    )(info, *p, sums, data)
    return made[: len(rows)], made[len(rows) :]


def forward_kernel(next_ref, last_ref, from_left, from_right, out_next, out_last):
    half = HALF // 2
    low, high, rest = slice(0, half), slice(half, HALF), slice(HALF, HALF + EXTRA)
    for b in range(4):
        out_next[b, low, :] = (next_ref[b, low, :].astype(F32) + from_left[b, low, :].astype(F32)).astype(BF16)
        out_next[b, high, :] = next_ref[b, high, :]
        out_last[b, low, :] = last_ref[b, low, :]
        out_last[b, high, :] = (last_ref[b, high, :].astype(F32) + from_right[b, low, :].astype(F32)).astype(BF16)
        out_next[b, rest, :] = row_sum_rows(row_sums_of(next_ref, 0, HALF) + row_sums_of(from_left, 0, half))
        out_last[b, rest, :] = last_ref[b, rest, :]


def forward(following, preceding, from_left, from_right):
    return pl.pallas_call(
        forward_kernel,
        out_shape=[jax.ShapeDtypeStruct((4, HALF + EXTRA, 128), BF16)] * 2,
        compiler_params=pltpu.CompilerParams(vmem_limit_bytes=16 * MIB),
        cost_estimate=pl.CostEstimate(flops=1 << 20, bytes_accessed=3 * MIB, transcendentals=0),
        name="forward",
    )(following, preceding, from_left, from_right)


def row_sums_of(ref, index=None, start=HALF):
    at = [slice(start + 4 * i, start + 4 * i + 4) for i in (0, 1)]
    high, low = (ref[i, :] if index is None else ref[index, i, :] for i in at)
    return high.astype(F32) + low.astype(F32)


def combine_kernel(side, info_ref, own, left, right, keep_ref, s1, s2, s3):
    place = info_ref[18 + side]
    sums = row_sums_of(own, 0) + (row_sums_of(left, 0) + row_sums_of(right, 0))
    tail = row_sum_rows(sums)

    def summed(index):
        at = slice(0, HALF)
        return own[index, at, :].astype(F32) + (left[index, at, :].astype(F32) + right[index, at, :].astype(F32))

    for d, out_ref in ((1, s1), (2, s2), (3, s3)):
        out_ref[:HALF, :] = summed(lax.rem(place + d, 4)).astype(BF16)
        out_ref[HALF:, :] = tail
    keep_ref[:HALF, :] = summed(place)
    keep_ref[HALF:, :] = jnp.concatenate([sums, jnp.zeros((EXTRA - 4, 128), F32)], axis=0)


def combine(side, info, parts):
    return pl.pallas_call(
        functools.partial(combine_kernel, side),
        in_specs=[pl.BlockSpec(memory_space=pltpu.SMEM)] + [pl.BlockSpec(memory_space=pltpu.VMEM)] * 3,
        out_shape=[jax.ShapeDtypeStruct((HALF + EXTRA, 128), F32)] + [jax.ShapeDtypeStruct((HALF + EXTRA, 128), BF16)] * 3,
        compiler_params=pltpu.CompilerParams(vmem_limit_bytes=16 * MIB),
        cost_estimate=pl.CostEstimate(flops=1 << 20, bytes_accessed=3 * MIB, transcendentals=0),
        name="combine",
    )(info, *parts)


def finish_kernel(noise_ref, *refs):
    out_ref = refs[-1]
    for half in range(2):
        own, *others = refs[4 * half : 4 * half + 4]
        sums = own[HALF : HALF + 4, :]
        for other in others:
            sums += row_sums_of(other)
        for a, inverse in enumerate(to_column(1.0 / sums)):
            here = slice(128 * a, 128 * (a + 1))
            at = slice(HALF * half + 128 * a, HALF * half + 128 * (a + 1))
            summed = own[here, :]
            for other in others:
                summed += other[here, :].astype(F32)
            out_ref[at, :] = summed * inverse - noise_ref[at, :].astype(F32)


def finish(noise, parts):
    return pl.pallas_call(
        finish_kernel,
        out_shape=jax.ShapeDtypeStruct((ROWS, 128), F32),
        compiler_params=pltpu.CompilerParams(vmem_limit_bytes=16 * MIB),
        name="finish",
    )(noise, *parts)


def swap(x, axis):
    return lax.all_to_all(x, axis, 0, 0, tiled=True)


def per_device(noise_latents, data_latents, noise_sizes, data_sizes):
    row, col = lax.axis_index("row"), lax.axis_index("col")
    places = jnp.stack([row * ROWS, col * COLS, col // 4, col % 4]).astype(jnp.int32)
    info = jnp.concatenate([noise_sizes, data_sizes, places])
    data = lax.all_gather(data_latents, "row")
    noise, noise_sq = arrange(info, gather_noise(noise_latents))
    score, lse, data_sq = scores(info, noise, data)
    lse, noise_first, e, most = first_columns(swap(lse, "col"), score)
    sums, data_first, factor = row_sums(True, swap(lse, "row"), most, e)
    sums, _ = column_sums(swap(sums, "col"), factor, e)
    sums = row_sums(False, swap(sums, "row"), factor, e)[0]
    sums, noise_scale = column_sums(swap(sums, "col"), factor, e)
    *p, sums, noise_potential, data_potential = coupling(
        swap(sums, "row"), noise_scale, noise_first, noise_sq, data_first, data_sq, factor, e
    )
    way = (over_x, over_z)
    made = messages((2,), info, p, sums, data)
    moved = [(way[side](made[side][0], 1), way[side](made[side][1], 3)) for side in (0, 1)]
    sums, _ = lax.optimization_barrier((sums, made))
    made = messages((1, 3), info, p, sums, data)
    sums, _ = lax.optimization_barrier((sums, made))
    got = []
    for side in (0, 1):
        following, preceding = forward(*made[side], *moved[side])
        got.append((way[side](following, 1), way[side](preceding, 3)))
        sums, _ = lax.optimization_barrier((sums, following))
    own = messages((0,), info, p, sums, data)
    ends = []
    for side in (0, 1):
        keep, *others = combine(side, info, (own[side][0], *got[side]))
        ends += [keep] + [way[1 - side](v, d) for d, v in zip((1, 2, 3), others)]
    velocity = finish(noise_latents, ends)
    return velocity, noise_potential.reshape(ROWS), data_potential.reshape(COLS)


def solution(mesh):
    placed = (P("row", "col"), P("col", "row"), P(), P())
    return jax.shard_map(
        per_device,
        mesh=mesh,
        in_specs=placed,
        out_specs=(P("row", "col"), P("row"), P("col")),
        check_vma=False,
    )
```

```python
import functools

import jax
import jax.numpy as jnp
from jax import lax
from jax.experimental import pallas as pl
from jax.experimental.pallas import tpu as pltpu
from jax.sharding import PartitionSpec as P

EPS = 0.05
LOG2E = 1.4426950408889634
LN2 = 0.6931471805599453
MASKED = -1e30
CLUSTERS = 8
F32 = jnp.float32
BF16 = jnp.bfloat16
MIB = 1 << 20

ROWS = 1024
COLS = 2048
WIDTH = 2048
COL_BLOCK = 512
SCORE_ROWS = 1024
ROW_BLOCK = 256
HALF = 512
N_ROW = 8
N_COL = 16
KAPPA = LOG2E / (WIDTH * EPS)


def vmem(shape, index_map=None):
    if index_map is None:
        return pl.BlockSpec(shape, lambda *_: (0,) * len(shape))
    return pl.BlockSpec(shape, index_map)


def params(mib):
    return pltpu.CompilerParams(vmem_limit_bytes=mib * MIB, dimension_semantics=("arbitrary",))


def lane_totals(pieces):
    return [piece.T for piece in pieces]


def to_column(rows):
    n = rows.shape[0]
    return [jnp.broadcast_to(rows[a : a + 1, :], (128, 128)).T for a in range(n)]


def to_lanes(rows):
    return jnp.concatenate([rows[a : a + 1, :] for a in range(rows.shape[0])], axis=1)


def from_lanes(row):
    return jnp.concatenate([row[:, 128 * a : 128 * (a + 1)] for a in range(row.shape[1] // 128)], axis=0)


def arrange_kernel(info_ref, *refs):
    out_ref, noise_sq_ref = refs[10:]
    z, x = info_ref[18], info_ref[19]
    sums = []
    for half in range(2):
        own, before, after, second_a, second_b = refs[5 * half : 5 * half + 5]
        at = slice(HALF * half, HALF * (half + 1))
        squares = jnp.zeros((HALF, 128), F32)
        for far, source in ((0, own), (1, before), (3, after), (2, None)):
            for near in range(4):
                if source is not None:
                    piece = source[near]
                else:
                    piece = second_a[near] if near < 2 else second_b[near - 2]
                if half == 0:
                    index = lax.rem(z + 4 - far, 4) * 4 + lax.rem(x + 4 - near, 4)
                else:
                    index = lax.rem(z + 4 - near, 4) * 4 + lax.rem(x + 4 - far, 4)
                out_ref[at, pl.ds(pl.multiple_of(index * 128, 128), 128)] = piece
                squares += piece.astype(F32) * piece.astype(F32)
        for a in range(HALF // 128):
            sums.append(jnp.sum(squares[128 * a : 128 * (a + 1), :].T, axis=0, keepdims=True))
    noise_sq_ref[...] = jnp.concatenate(sums, axis=0)


def arrange(info, pieces):
    return pl.pallas_call(
        arrange_kernel,
        in_specs=[pl.BlockSpec(memory_space=pltpu.SMEM)] + [pl.BlockSpec(memory_space=pltpu.VMEM)] * 10,
        out_shape=[jax.ShapeDtypeStruct((ROWS, WIDTH), BF16), NOISE_SHAPE],
        compiler_params=pltpu.CompilerParams(vmem_limit_bytes=24 * MIB),
        cost_estimate=pl.CostEstimate(flops=4 << 20, bytes_accessed=8 * MIB, transcendentals=0),
        name="arrange",
    )(info, *pieces)


def over_x(v, d):
    return lax.ppermute(v, "col", [(4 * z + x, 4 * z + (x + d) % 4) for z in range(4) for x in range(4)])


def over_z(v, d):
    return lax.ppermute(v, "col", [(4 * z + x, 4 * ((z + d) % 4) + x) for z in range(4) for x in range(4)])


def gather_noise(noise):
    gathered = []
    for half, (first, second) in enumerate(((over_x, over_z), (over_z, over_x))):
        own = noise[HALF * half : HALF * (half + 1)]
        own = jnp.stack([own] + [first(own, d) for d in (1, 2, 3)])
        gathered.append((own, second(own, 1), second(own, 3), second))
    pieces = []
    for own, before, after, second in gathered:
        pieces += [own, before, after, second(before[:2], 1), second(after[2:], 3)]
    return pieces


def score_kernel(info_ref, noise_ref, data_ref, score_ref, lse_ref, data_sq_ref, big, total):
    step = pl.program_id(0)

    @pl.when(step == 0)
    def _():
        big[...] = jnp.full(big.shape, MASKED, F32)
        total[...] = jnp.zeros(total.shape, F32)

    data = jnp.concatenate([data_ref[k] for k in range(N_ROW)], axis=1)
    data_sq = []
    for a in range(COL_BLOCK // 128):
        squares = jnp.zeros((128, 128), F32)
        for k in range(WIDTH // 128):
            piece = data[128 * a : 128 * (a + 1), 128 * k : 128 * (k + 1)].astype(F32)
            squares += piece * piece
        data_sq.append(jnp.sum(squares.T, axis=0, keepdims=True))
        data_sq_ref[0, a : a + 1, :] = data_sq[a]

    j = info_ref[17] + step * COL_BLOCK + lax.broadcasted_iota(jnp.int32, (1, COL_BLOCK), 1)
    low = jnp.zeros((1, COL_BLOCK), jnp.int32)
    high = jnp.zeros((1, COL_BLOCK), jnp.int32)
    noise_at = jnp.int32(0)
    data_at = jnp.int32(0)
    for c in range(CLUSTERS):
        noise_end = noise_at + info_ref[c]
        data_end = data_at + info_ref[8 + c]
        if c == CLUSTERS - 1:
            inside = j >= data_at
        else:
            inside = (j >= data_at) & (j < data_end)
        low = jnp.where(inside, noise_at, low)
        high = jnp.where(inside, noise_end, high)
        noise_at, data_at = noise_end, data_end
    low = low - info_ref[16]
    span = (high - info_ref[16] - low).astype(jnp.uint32)

    half = SCORE_ROWS
    for r in range(ROWS // half):
        inner = lax.dot_general(noise_ref[half * r : half * (r + 1), :], data, (((1,), (1,)), ((), ())), preferred_element_type=F32)
        i = half * r + lax.broadcasted_iota(jnp.int32, (half, COL_BLOCK), 0)
        score = jnp.where((i - low).astype(jnp.uint32) < span, inner * (2.0 * KAPPA), MASKED)
        score_ref[half * r : half * (r + 1), :] = score
        parts = [score[:, 128 * t : 128 * (t + 1)] - KAPPA * data_sq[t] for t in range(COL_BLOCK // 128)]
        at = slice(half * r, half * (r + 1))
        old = big[at, :]
        new = functools.reduce(jnp.maximum, parts, old)
        total[at, :] = total[at, :] * jnp.exp2(old - new) + functools.reduce(
            jnp.add, [jnp.exp2(part - new) for part in parts]
        )
        big[at, :] = new

    @pl.when(step == pl.num_programs(0) - 1)
    def _():
        rows = []
        for a in range(ROWS // 128):
            at = slice(128 * a, 128 * (a + 1))
            m = big[at, :].T
            s = total[at, :].T
            largest = jnp.max(m, axis=0, keepdims=True)
            summed = jnp.sum(s * jnp.exp2(m - largest), axis=0, keepdims=True)
            rows.append(largest + jnp.log2(summed))
        lse_ref[...] = jnp.broadcast_to(jnp.concatenate(rows, axis=0)[None], lse_ref.shape)


def scores(info, noise, data):
    return pl.pallas_call(
        score_kernel,
        grid=(COLS // COL_BLOCK,),
        in_specs=[
            pl.BlockSpec(memory_space=pltpu.SMEM),
            pl.BlockSpec(memory_space=pltpu.VMEM),
            vmem((N_ROW, COL_BLOCK, 256), lambda j: (0, j, 0)),
        ],
        out_specs=[
            vmem((ROWS, COL_BLOCK), lambda j: (0, j)),
            vmem((N_COL, 8, 128)),
            vmem((1, COL_BLOCK // 128, 128), lambda j: (j, 0, 0)),
        ],
        out_shape=[
            jax.ShapeDtypeStruct((ROWS, COLS), F32),
            jax.ShapeDtypeStruct((N_COL, 8, 128), F32),
            jax.ShapeDtypeStruct((COLS // COL_BLOCK, COL_BLOCK // 128, 128), F32),
        ],
        scratch_shapes=[pltpu.VMEM((ROWS, 128), F32), pltpu.VMEM((ROWS, 128), F32)],
        compiler_params=params(40),
        cost_estimate=pl.CostEstimate(flops=2 * ROWS * COLS * WIDTH, bytes_accessed=20 * MIB, transcendentals=3 << 20),
        name="scores",
    )(info, noise, data)


def merge_lse(parts_ref):
    parts = parts_ref[...]
    largest = jnp.max(parts, axis=0)
    return -(largest + jnp.log2(jnp.sum(jnp.exp2(parts - largest[None]), axis=0)))


def merge_scale(parts_ref):
    return 1.0 / jnp.sum(parts_ref[...], axis=0)


GROUP = 8


def first_columns_kernel(parts_ref, score_ref, lse_ref, noise_ref, e_ref, max_ref, column, big, total):
    step = pl.program_id(0)
    blocks = ROWS // ROW_BLOCK
    tiles = COLS // 128
    base = lax.rem(step, blocks) * ROW_BLOCK

    @pl.when(step == 0)
    def _():
        potential = merge_lse(parts_ref)
        noise_ref[...] = potential
        for a, piece in enumerate(to_column(potential)):
            column[128 * a : 128 * (a + 1), :] = piece
        big[...] = jnp.full(big.shape, MASKED, F32)
        total[...] = jnp.zeros(total.shape, F32)

    @pl.when(step < blocks)
    def _():
        def largest(g, carry):
            shift = column[pl.ds(pl.multiple_of(base + g * GROUP, GROUP), GROUP), :]
            at = pl.ds(pl.multiple_of(g * GROUP, GROUP), GROUP)
            return tuple(jnp.maximum(carry[t], score_ref[at, 128 * t : 128 * (t + 1)] + shift) for t in range(tiles))

        start = tuple(big[:, 128 * t : 128 * (t + 1)] for t in range(tiles))
        new = lax.fori_loop(0, ROW_BLOCK // GROUP, largest, start, unroll=4)
        for t in range(tiles):
            big[:, 128 * t : 128 * (t + 1)] = new[t]

    @pl.when(step == blocks)
    def _():
        big[...] = jnp.broadcast_to(jnp.max(big[...], axis=0, keepdims=True), big.shape)

    @pl.when(step >= blocks)
    def _():
        most = [big[:, 128 * t : 128 * (t + 1)] for t in range(tiles)]

        def add(g, carry):
            shift = column[pl.ds(pl.multiple_of(base + g * GROUP, GROUP), GROUP), :]
            at = pl.ds(pl.multiple_of(g * GROUP, GROUP), GROUP)
            out = []
            for t in range(tiles):
                here = slice(128 * t, 128 * (t + 1))
                value = jnp.exp2(score_ref[at, here] + (shift - most[t]))
                e_ref[at, here] = value
                out.append(carry[t] + value)
            return tuple(out)

        start = tuple(total[:, 128 * t : 128 * (t + 1)] for t in range(tiles))
        summed = lax.fori_loop(0, ROW_BLOCK // GROUP, add, start, unroll=4)
        for t in range(tiles):
            total[:, 128 * t : 128 * (t + 1)] = summed[t]

    @pl.when(step == 2 * blocks - 1)
    def _():
        most = big[0:1, :]
        s = jnp.sum(total[...], axis=0, keepdims=True)
        lse_ref[...] = jnp.broadcast_to(from_lanes(most + jnp.log2(s))[None], lse_ref.shape)
        max_ref[...] = from_lanes(most)


def pass_call(kernel, inputs, in_specs, outs, out_specs, scratch, name, transcendentals=0, sweeps=1):
    return pl.pallas_call(
        kernel,
        grid=(sweeps * (ROWS // ROW_BLOCK),),
        in_specs=in_specs,
        out_specs=out_specs,
        out_shape=outs,
        scratch_shapes=scratch,
        compiler_params=params(24),
        cost_estimate=pl.CostEstimate(flops=4 * ROWS * COLS, bytes_accessed=8 * MIB, transcendentals=transcendentals),
        name=name,
    )(*inputs)


FROM_COL = vmem((N_COL, 8, 128))
FROM_ROW = vmem((N_ROW, 16, 128))
NOISE = vmem((8, 128))
DATA = vmem((16, 128))
BLOCK = vmem((ROW_BLOCK, COLS), lambda i: (i, 0))
FROM_COL_SHAPE = jax.ShapeDtypeStruct((N_COL, 8, 128), F32)
FROM_ROW_SHAPE = jax.ShapeDtypeStruct((N_ROW, 16, 128), F32)
NOISE_SHAPE = jax.ShapeDtypeStruct((8, 128), F32)
DATA_SHAPE = jax.ShapeDtypeStruct((16, 128), F32)
BLOCK_SHAPE = jax.ShapeDtypeStruct((ROWS, COLS), F32)


def first_columns(parts, score):
    blocks = ROWS // ROW_BLOCK
    return pass_call(
        first_columns_kernel,
        (parts, score),
        [FROM_COL, vmem((ROW_BLOCK, COLS), lambda i: (lax.rem(i, blocks), 0))],
        [FROM_ROW_SHAPE, NOISE_SHAPE, BLOCK_SHAPE, DATA_SHAPE],
        [FROM_ROW, NOISE, vmem((ROW_BLOCK, COLS), lambda i: (jnp.maximum(i - blocks, 0), 0)), DATA],
        [pltpu.VMEM((ROWS, 128), F32), pltpu.VMEM((8, COLS), F32), pltpu.VMEM((8, COLS), F32)],
        "first_columns",
        ROWS * COLS,
        2,
    )


def write_row_sums(sums, out_ref, rows, step):
    per = ROW_BLOCK // 128
    for a in range(per):
        piece = sums[128 * a : 128 * (a + 1), :].T
        rows[pl.ds(step * per + a, 1), :] = jnp.sum(piece, axis=0, keepdims=True)

    @pl.when(step == pl.num_programs(0) - 1)
    def _():
        out_ref[...] = jnp.broadcast_to(rows[...][None], out_ref.shape)


def column_sums_kernel(parts_ref, factor_ref, k_ref, sums_ref, scale_ref, column, total):
    step = pl.program_id(0)

    @pl.when(step == 0)
    def _():
        scale = merge_scale(parts_ref)
        scale_ref[...] = scale
        for a, piece in enumerate(to_column(scale)):
            column[128 * a : 128 * (a + 1), :] = piece
        total[...] = jnp.zeros(total.shape, F32)

    base = step * ROW_BLOCK
    tiles = COLS // 128

    def add(g, carry):
        scale = column[pl.ds(pl.multiple_of(base + g * GROUP, GROUP), GROUP), :]
        at = pl.ds(pl.multiple_of(g * GROUP, GROUP), GROUP)
        return tuple(carry[t] + k_ref[at, 128 * t : 128 * (t + 1)] * scale for t in range(tiles))

    start = tuple(total[:, 128 * t : 128 * (t + 1)] for t in range(tiles))
    summed = lax.fori_loop(0, ROW_BLOCK // GROUP, add, start, unroll=4)
    for t in range(tiles):
        total[:, 128 * t : 128 * (t + 1)] = summed[t]

    @pl.when(step == pl.num_programs(0) - 1)
    def _():
        s = jnp.sum(total[...], axis=0, keepdims=True)
        sums_ref[...] = jnp.broadcast_to((from_lanes(s) * factor_ref[...])[None], sums_ref.shape)


def column_sums(parts, factor, k):
    return pass_call(
        column_sums_kernel,
        (parts, factor, k),
        [FROM_COL, DATA, BLOCK],
        [FROM_ROW_SHAPE, NOISE_SHAPE],
        [FROM_ROW, NOISE],
        [pltpu.VMEM((ROWS, 128), F32), pltpu.VMEM((GROUP, COLS), F32)],
        "column_sums",
    )


def row_sums_kernel(first, parts_ref, factor_ref, k_ref, sums_ref, *refs):
    lanes, sums, rows = refs[-3:]
    step = pl.program_id(0)

    @pl.when(step == 0)
    def _():
        if first:
            data_ref, out_ref = refs[:2]
            potential = merge_lse(parts_ref)
            data_ref[...] = potential
            scale = jnp.exp2(factor_ref[...] + potential)
            out_ref[...] = scale
        else:
            scale = factor_ref[...] * merge_scale(parts_ref)
        lanes[...] = jnp.broadcast_to(to_lanes(scale), lanes.shape)

    tiles = COLS // 128
    scales = [lanes[:, 128 * t : 128 * (t + 1)] for t in range(tiles)]

    def body(g, _):
        at = pl.ds(pl.multiple_of(g * GROUP, GROUP), GROUP)
        summed = [k_ref[at, 128 * t : 128 * (t + 1)] * scales[t] for t in range(4)]
        for t in range(4, tiles):
            summed[t % 4] += k_ref[at, 128 * t : 128 * (t + 1)] * scales[t]
        sums[at, :] = (summed[0] + summed[1]) + (summed[2] + summed[3])
        return 0

    lax.fori_loop(0, ROW_BLOCK // GROUP, body, 0, unroll=4)
    write_row_sums(sums, sums_ref, rows, step)


def row_sums(first, parts, factor, k):
    more = 2 if first else 0
    return pass_call(
        functools.partial(row_sums_kernel, first),
        (parts, factor, k),
        [FROM_ROW, DATA, BLOCK],
        [FROM_COL_SHAPE] + [DATA_SHAPE] * more,
        [FROM_COL] + [DATA] * more,
        [pltpu.VMEM((GROUP, COLS), F32), pltpu.VMEM((ROW_BLOCK, 128), F32), pltpu.VMEM((8, 128), F32)],
        "row_sums",
    )


def coupling_kernel(
    parts_ref, scale_ref, noise_first, noise_sq, data_first, data_sq, factor_ref, k_ref,
    pa_ref, pb_ref, sums_ref, noise_ref, data_ref, column, lanes, sums,
):
    step = pl.program_id(0)

    @pl.when(step == 0)
    def _():
        scale = merge_scale(parts_ref)
        lanes[...] = jnp.broadcast_to(to_lanes(factor_ref[...] * scale), lanes.shape)
        for a, piece in enumerate(to_column(scale_ref[...])):
            column[128 * a : 128 * (a + 1), :] = piece
        noise_ref[...] = (EPS * LN2) * (noise_first[...] + jnp.log2(scale_ref[...])) + noise_sq[...] * (1.0 / WIDTH)
        potential = (EPS * LN2) * (data_first[...] + jnp.log2(scale))
        per = COL_BLOCK // 128
        for k in range(COLS // COL_BLOCK):
            at = slice(per * k, per * (k + 1))
            data_ref[at, :] = potential[at, :] + data_sq[k] * (1.0 / WIDTH)

    base = step * ROW_BLOCK
    tiles = COLS // 128

    def block(p_ref):
        def body(g, _):
            at = pl.ds(pl.multiple_of(g * 16, 16), 16)
            scale = column[pl.ds(pl.multiple_of(base + g * 16, 16), 16), :]
            summed = jnp.zeros((16, 128), F32)
            for t in range(tiles):
                here = slice(128 * t, 128 * (t + 1))
                value = (k_ref[at, here] * (scale * lanes[:, here])).astype(BF16)
                p_ref[at, here] = value
                summed += value.astype(F32)
            sums[at, :] = summed
            return 0

        lax.fori_loop(0, ROW_BLOCK // 16, body, 0, unroll=4)

    @pl.when(step < 2)
    def _():
        block(pa_ref)

    @pl.when(step >= 2)
    def _():
        block(pb_ref)

    per = ROW_BLOCK // 128
    for a in range(per):
        piece = sums[128 * a : 128 * (a + 1), :].T
        sums_ref[pl.ds(step * per + a, 1), :] = jnp.sum(piece, axis=0, keepdims=True)


def coupling(parts, noise_scale, noise_first, noise_sq, data_first, data_sq, factor, k):
    half = jax.ShapeDtypeStruct((HALF, COLS), BF16)
    return pass_call(
        coupling_kernel,
        (parts, noise_scale, noise_first, noise_sq, data_first, data_sq, factor, k),
        [FROM_ROW, NOISE, NOISE, NOISE, DATA, vmem((COLS // COL_BLOCK, COL_BLOCK // 128, 128)), DATA, BLOCK],
        [half, half, NOISE_SHAPE, NOISE_SHAPE, DATA_SHAPE],
        [
            vmem((ROW_BLOCK, COLS), lambda i: (jnp.minimum(i, 1), 0)),
            vmem((ROW_BLOCK, COLS), lambda i: (jnp.maximum(i - 2, 0), 0)),
            NOISE,
            NOISE,
            DATA,
        ],
        [
            pltpu.VMEM((ROWS, 128), F32),
            pltpu.VMEM((16, COLS), F32),
            pltpu.VMEM((ROW_BLOCK, 128), F32),
        ],
        "coupling",
    )


EXTRA = 16


def split(value):
    high = value.astype(BF16)
    return high, (value - high.astype(F32)).astype(BF16)


def row_sum_rows(sums):
    high, low = split(sums)
    return jnp.concatenate([high, low, high, low], axis=0)


def target_kernel(ways, info_ref, pa_ref, pb_ref, sums_ref, data_ref, *out_refs):
    z, x = info_ref[18], info_ref[19]
    out_refs = list(out_refs)
    for side in (0, 1):
        tail = row_sum_rows(sums_ref[4 * side : 4 * side + 4, :])
        for way in ways:
            if side == 0:
                block = lax.rem(x + way, 4)
                lanes = pl.ds(pl.multiple_of(lax.rem(block, 2) * 128, 128), 128)
                data = [data_ref[2 * k + block // 2, :, lanes] for k in range(4)]
                values = pa_ref[...]
            else:
                block = lax.rem(z + way, 4)
                data = [data_ref[2 * block + k] for k in range(2)]
                values = pb_ref[...]
            summed = jnp.dot(values, jnp.concatenate(data, axis=1), preferred_element_type=F32).astype(BF16)
            parts = 2 if way == 2 else 1
            rows = HALF // parts
            for part in range(parts):
                out_ref = out_refs.pop(0)
                for b in range(4):
                    out_ref[b, :rows, :] = summed[rows * part : rows * (part + 1), 128 * b : 128 * (b + 1)]
                    out_ref[b, rows:, :] = tail


def messages(ways, info, p, sums, data):
    rows = [HALF // 2] * 2 if ways == (2,) else [HALF] * len(ways)
    made = pl.pallas_call(
        functools.partial(target_kernel, ways),
        in_specs=[pl.BlockSpec(memory_space=pltpu.SMEM)] + [pl.BlockSpec(memory_space=pltpu.VMEM)] * 4,
        out_shape=[jax.ShapeDtypeStruct((4, n + EXTRA, 128), BF16) for n in rows * 2],
        compiler_params=pltpu.CompilerParams(vmem_limit_bytes=28 * MIB),
        cost_estimate=pl.CostEstimate(
            flops=ROWS * COLS * WIDTH // 2 * len(ways), bytes_accessed=8 * MIB, transcendentals=0
        ),
        name="targets",
    )(info, *p, sums, data)
    return made[: len(rows)], made[len(rows) :]


def forward_kernel(next_ref, last_ref, from_left, from_right, out_next, out_last):
    half = HALF // 2
    low, high, rest = slice(0, half), slice(half, HALF), slice(HALF, HALF + EXTRA)
    for b in range(4):
        out_next[b, low, :] = (next_ref[b, low, :].astype(F32) + from_left[b, low, :].astype(F32)).astype(BF16)
        out_next[b, high, :] = next_ref[b, high, :]
        out_last[b, low, :] = last_ref[b, low, :]
        out_last[b, high, :] = (last_ref[b, high, :].astype(F32) + from_right[b, low, :].astype(F32)).astype(BF16)
        out_next[b, rest, :] = row_sum_rows(row_sums_of(next_ref, 0, HALF) + row_sums_of(from_left, 0, half))
        out_last[b, rest, :] = last_ref[b, rest, :]


def forward(following, preceding, from_left, from_right):
    return pl.pallas_call(
        forward_kernel,
        out_shape=[jax.ShapeDtypeStruct((4, HALF + EXTRA, 128), BF16)] * 2,
        compiler_params=pltpu.CompilerParams(vmem_limit_bytes=16 * MIB),
        cost_estimate=pl.CostEstimate(flops=1 << 20, bytes_accessed=3 * MIB, transcendentals=0),
        name="forward",
    )(following, preceding, from_left, from_right)


def row_sums_of(ref, index=None, start=HALF):
    at = [slice(start + 4 * i, start + 4 * i + 4) for i in (0, 1)]
    high, low = (ref[i, :] if index is None else ref[index, i, :] for i in at)
    return high.astype(F32) + low.astype(F32)


def combine_kernel(side, info_ref, own, left, right, keep_ref, s1, s2, s3):
    place = info_ref[18 + side]
    sums = row_sums_of(own, 0) + (row_sums_of(left, 0) + row_sums_of(right, 0))
    tail = row_sum_rows(sums)

    def summed(index):
        at = slice(0, HALF)
        return own[index, at, :].astype(F32) + (left[index, at, :].astype(F32) + right[index, at, :].astype(F32))

    for d, out_ref in ((1, s1), (2, s2), (3, s3)):
        out_ref[:HALF, :] = summed(lax.rem(place + d, 4)).astype(BF16)
        out_ref[HALF:, :] = tail
    keep_ref[:HALF, :] = summed(place)
    keep_ref[HALF:, :] = jnp.concatenate([sums, jnp.zeros((EXTRA - 4, 128), F32)], axis=0)


def combine(side, info, parts):
    return pl.pallas_call(
        functools.partial(combine_kernel, side),
        in_specs=[pl.BlockSpec(memory_space=pltpu.SMEM)] + [pl.BlockSpec(memory_space=pltpu.VMEM)] * 3,
        out_shape=[jax.ShapeDtypeStruct((HALF + EXTRA, 128), F32)] + [jax.ShapeDtypeStruct((HALF + EXTRA, 128), BF16)] * 3,
        compiler_params=pltpu.CompilerParams(vmem_limit_bytes=16 * MIB),
        cost_estimate=pl.CostEstimate(flops=1 << 20, bytes_accessed=3 * MIB, transcendentals=0),
        name="combine",
    )(info, *parts)


def finish_kernel(noise_ref, *refs):
    out_ref = refs[-1]
    for half in range(2):
        own, *others = refs[4 * half : 4 * half + 4]
        sums = own[HALF : HALF + 4, :]
        for other in others:
            sums += row_sums_of(other)
        for a, inverse in enumerate(to_column(1.0 / sums)):
            here = slice(128 * a, 128 * (a + 1))
            at = slice(HALF * half + 128 * a, HALF * half + 128 * (a + 1))
            summed = own[here, :]
            for other in others:
                summed += other[here, :].astype(F32)
            out_ref[at, :] = summed * inverse - noise_ref[at, :].astype(F32)


def finish(noise, parts):
    return pl.pallas_call(
        finish_kernel,
        out_shape=jax.ShapeDtypeStruct((ROWS, 128), F32),
        compiler_params=pltpu.CompilerParams(vmem_limit_bytes=16 * MIB),
        name="finish",
    )(noise, *parts)


def swap(x, axis):
    return lax.all_to_all(x, axis, 0, 0, tiled=True)


def per_device(noise_latents, data_latents, noise_sizes, data_sizes):
    row, col = lax.axis_index("row"), lax.axis_index("col")
    places = jnp.stack([row * ROWS, col * COLS, col // 4, col % 4]).astype(jnp.int32)
    info = jnp.concatenate([noise_sizes, data_sizes, places])
    data = lax.all_gather(data_latents, "row")
    noise, noise_sq = arrange(info, gather_noise(noise_latents))
    score, lse, data_sq = scores(info, noise, data)
    lse, noise_first, e, most = first_columns(swap(lse, "col"), score)
    sums, data_first, factor = row_sums(True, swap(lse, "row"), most, e)
    sums, _ = column_sums(swap(sums, "col"), factor, e)
    sums = row_sums(False, swap(sums, "row"), factor, e)[0]
    sums, noise_scale = column_sums(swap(sums, "col"), factor, e)
    *p, sums, noise_potential, data_potential = coupling(
        swap(sums, "row"), noise_scale, noise_first, noise_sq, data_first, data_sq, factor, e
    )
    way = (over_x, over_z)
    made = messages((2,), info, p, sums, data)
    moved = [(way[side](made[side][0], 1), way[side](made[side][1], 3)) for side in (0, 1)]
    sums, _ = lax.optimization_barrier((sums, made))
    made = messages((1, 3), info, p, sums, data)
    sums, _ = lax.optimization_barrier((sums, made))
    got = []
    for side in (0, 1):
        following, preceding = forward(*made[side], *moved[side])
        got.append((way[side](following, 1), way[side](preceding, 3)))
        sums, _ = lax.optimization_barrier((sums, following))
    own = messages((0,), info, p, sums, data)
    ends = []
    for side in (0, 1):
        keep, *others = combine(side, info, (own[side][0], *got[side]))
        ends += [keep] + [way[1 - side](v, d) for d, v in zip((1, 2, 3), others)]
    velocity = finish(noise_latents, ends)
    return velocity, noise_potential.reshape(ROWS), data_potential.reshape(COLS)


def solution(mesh):
    placed = (P("row", "col"), P("col", "row"), P(), P())
    return jax.shard_map(
        per_device,
        mesh=mesh,
        in_specs=placed,
        out_specs=(P("row", "col"), P("row"), P("col")),
        check_vma=False,
    )
```
